32 devices in a mesh: ta: 4 (over x, core), xyz: 8 (over z, y).
Axes of the slice: x: 2, y: 2, z: 4, core: 2. Of those that a mesh axis runs over, the one named last changes fastest.
Arguments:
- nulls: bfloat16 [16, 32, 32, 16, 128], P('ta', 'xyz'), may hold values from -1.1953125 to 1.1953125
- time_links: bfloat16 [8, 32, 32, 64, 128], P('ta', 'xyz'), may hold values from -0.5 to 0.5
- space_links: bfloat16 [16, 16, 32, 64, 128], P('ta', 'xyz'), may hold values from -0.5 to 0.5
- owner_lists: int32 [8, 64], replicated, may hold values from -1 to 255, as said below
Outputs:
- coarse_links: float32 [4, 512, 1024], P('ta', 'xyz')
The draws below stay inside these ranges and needn't reach their ends.
Inputs may be any that keep to these rules, and one draw needn't show every extreme that they name: `owner_lists`: row d lists, in increasing order, the aggregates that shard d owns, followed by -1 in the remaining slots; each of the 256 aggregate ids appears exactly once. Exactly half of the shards own 64 aggregates each and the others none. The 32 aggregates with ids q * 32 to q * 32 + 31 belong to exactly 4 owners, 8 to each.
All inputs are finite; a program needn't handle non-finite values.
Results may differ from the reference program's by a relative error of at most 0.0029.
Values may be sent and summed in bfloat16 or wider, within the bound.
No kernel may reach another device: no remote copies, remote signals or barrier semaphores. Data moves between devices by JAX's collectives and lax.ppermute only.
A program may use at most 64 MiB of HBM per device.

```python
import jax
import jax.numpy as jnp
from jax import lax

FINE = 64
NV = 16
AT = 2
AX = 2
AS = 8
A_DEV = 32
LT = 16
LX = 32
YZ = 32
SEND_MOST = 8
CAP = 64
N_TA = 4
N_XYZ = 8


def draw_owner_lists(key, part):
    heavy_key = jax.random.fold_in(key, 11)
    order_key = jax.random.fold_in(key, 12)
    half_count = N_XYZ // 2
    heavy = jax.random.permutation(heavy_key, N_XYZ)[:half_count]
    shard_keys = jax.random.split(order_key, N_XYZ)
    orders = jax.vmap(lambda shard_key: jax.random.permutation(shard_key, A_DEV))(shard_keys)
    places = jnp.argsort(orders, axis=1)
    groups_of = places // SEND_MOST
    shard_ids = jnp.arange(N_XYZ)[:, None]
    owners = heavy[(shard_ids + groups_of) % half_count].reshape(-1)
    agg_ids = (shard_ids * A_DEV + jnp.arange(A_DEV)[None, :]).reshape(-1)
    beyond = N_XYZ * A_DEV
    keyed = jnp.where(owners[None, :] == jnp.arange(N_XYZ)[:, None], agg_ids[None, :], beyond)
    ordered = jnp.sort(keyed, axis=1)[:, :CAP]
    return jnp.where(ordered == beyond, -1, ordered).astype(jnp.int32)


def level_of(key, extent, shards, smallest, top_value):
    def one(dim, parts):
        steps = jax.random.uniform(jax.random.fold_in(jax.random.fold_in(key, 6), dim), (parts,), jnp.float32, smallest / len(shards), top_value / len(shards))
        return jnp.repeat(jnp.exp(steps), extent[dim] // parts).reshape((-1,) + (1,) * (len(extent) - dim - 1))

    gain = one(*shards[0])
    for cut in shards[1:]:
        gain = gain * one(*cut)
    return gain


def centred(own_key, shape, deviation, bound, shards=(), kind=jnp.bfloat16):
    result = jax.random.normal(own_key, shape, jnp.float32) * deviation
    if len(shards) > 0:
        result = level_of(own_key, shape, shards, -0.22, 0.18) * result
    return jnp.clip(result, min=-bound, max=bound).astype(kind)


def setup_inputs(seed: int = 0) -> dict:
    keys = jax.random.split(jax.random.key(seed), 5)
    nulls = centred(keys[0], (LT, LX, YZ, NV, 2 * FINE), 0.2, 1.1953125, ((0, 4), (1, 8)))
    time_links = centred(keys[1], (LT // 2, LX, YZ, FINE, 2 * FINE), (2 * FINE) ** -0.5, 0.5, ((0, 4), (1, 8)))
    space_links = centred(keys[2], (LT, LX // 2, YZ, FINE, 2 * FINE), (2 * FINE) ** -0.5, 0.5, ((0, 4), (1, 8)))
    owner_lists = draw_owner_lists(jax.random.fold_in(keys[4], 71), 0)
    return dict(nulls=nulls, time_links=time_links, space_links=space_links, owner_lists=owner_lists)


def forward_image(link_mats, upper_nulls):
    half_width = link_mats.shape[-2]
    upper_real = upper_nulls[..., :half_width]
    upper_imag = upper_nulls[..., half_width:]
    paired = jnp.stack([jnp.concatenate([upper_real, -upper_imag], axis=-1), jnp.concatenate([upper_imag, upper_real], axis=-1)], axis=-3)
    image_pair = jnp.einsum("...ik,...pnk->...pni", link_mats.astype(jnp.float32), paired.astype(jnp.float32), precision=lax.Precision.HIGHEST)
    joined = jnp.concatenate([image_pair[..., 0, :, :], image_pair[..., 1, :, :]], axis=-1)
    return joined.astype(jnp.bfloat16)


def conjugate_pair(lower_nulls):
    half_width = lower_nulls.shape[-1] // 2
    turned = jnp.concatenate([-lower_nulls[..., half_width:], lower_nulls[..., :half_width]], axis=-1)
    return jnp.stack([lower_nulls, turned], axis=-3)


def reference(nulls, time_links, space_links, owner_lists):
    time_sites = nulls.shape[0]
    half_time = time_sites // 2
    time_lower = nulls[1::2]
    time_upper = jnp.roll(nulls, -1, axis=0)[1::2]
    space_lower = nulls[:, 1::2]
    space_upper = jnp.roll(nulls, -1, axis=1)[:, 1::2]

    def regroup(array):
        return array.reshape((half_time, 2) + array.shape[1:])

    def one_step(step_items):
        time_mats, low_time, up_time, space_mats, low_space, up_space = step_items
        x_sites = time_mats.shape[0]
        w_sites = time_mats.shape[1]
        vectors = low_time.shape[-2]
        doubled = low_time.shape[-1]
        image_time = forward_image(time_mats, up_time).astype(jnp.float32).reshape(x_sites // 2, 2, w_sites // 4, 4, vectors, doubled)
        pair_time = conjugate_pair(low_time).astype(jnp.float32).reshape(x_sites // 2, 2, w_sites // 4, 4, 2, vectors, doubled)
        block_time = jnp.einsum("xcaypnk,xcaymk->xapnm", pair_time, image_time, precision=lax.Precision.HIGHEST)
        image_space = forward_image(space_mats, up_space).astype(jnp.float32).reshape(2, x_sites // 2, w_sites // 4, 4, vectors, doubled)
        pair_space = conjugate_pair(low_space).astype(jnp.float32).reshape(2, x_sites // 2, w_sites // 4, 4, 2, vectors, doubled)
        block_space = jnp.einsum("cxaypnk,cxaymk->xapnm", pair_space, image_space, precision=lax.Precision.HIGHEST)
        block_width = 2 * vectors * vectors
        return jnp.concatenate([block_time.reshape(x_sites // 2, w_sites // 4, block_width), block_space.reshape(x_sites // 2, w_sites // 4, block_width)], axis=-1)

    all_rows = lax.map(one_step, (time_links, time_lower, time_upper, regroup(space_links), regroup(space_lower), regroup(space_upper)))
    row_len = all_rows.shape[-1]
    grouped = all_rows.reshape(N_TA, AT, N_XYZ, AX, AS, row_len).transpose(0, 2, 1, 3, 4, 5).reshape(N_TA, N_XYZ * AT * AX * AS, row_len)
    flat_lists = owner_lists.reshape(-1).astype(jnp.int32)
    live_slot = (flat_lists >= 0).astype(jnp.float32)
    picked = jnp.take(grouped, jnp.maximum(flat_lists, 0), axis=1)
    return picked * live_slot[None, :, None]
```

```python
import jax
import jax.numpy as jnp
from jax import lax
from jax.experimental import pallas as pl
from jax.experimental.pallas import tpu as pltpu
from jax.sharding import PartitionSpec as P

ROW_DIMS = (((1,), (1,)), ((), ()))
MAT_DIMS = (((1,), (0,)), ((), ()))
SIDE = 4
MOST = 8


def shifted(array, axis, by):
    count = lax.axis_size(axis)
    return lax.ppermute(array, axis, [(i, (i + by) % count) for i in range(count)])


def dot(left, right, dims):
    return lax.dot_general(left, right, dims, preferred_element_type=jnp.float32)


def swapped(array):
    return pltpu.roll(array, array.shape[-1] // 2, axis=array.ndim - 1)


def lower_half(shape):
    return lax.broadcasted_iota(jnp.int32, shape, len(shape) - 1) < shape[-1] // 2


def signs(shape, dtype):
    return jnp.where(lower_half(shape), 1.0, -1.0).astype(dtype)


def image_item(links, lower, upper, slot, left_ref, right_ref):
    sites, vectors, width = lower.shape
    half = width // 2
    low = lower_half((vectors, width))
    sign = signs((vectors, width), jnp.bfloat16)
    for pair in range(sites // 2):
        agg, part = divmod(pair, SIDE // 2)
        at = 2 * pair
        up_a, up_b = upper[at], upper[at + 1]
        rows = jnp.concatenate([up_a * sign, swapped(up_a), up_b * sign, swapped(up_b)], axis=0)
        mats = links[pl.ds(at, 2)].reshape(2 * half, width)
        images = dot(rows, mats, ROW_DIMS)
        real = jnp.where(low, images[:vectors], images[2 * vectors : 3 * vectors])
        imag = jnp.where(low, images[vectors : 2 * vectors], images[3 * vectors :])
        cols = pl.ds((slot * 2 + part) * 2 * width, 2 * width)
        right_ref[pl.ds(agg * vectors, vectors), cols] = jnp.concatenate([real, imag], axis=1).astype(jnp.bfloat16)
        lo_a, lo_b = lower[at], lower[at + 1]
        lo_real = jnp.where(low, lo_a, swapped(lo_b))
        lo_imag = jnp.where(low, swapped(lo_a), lo_b)
        left_ref[pl.ds(agg * 2 * vectors, 2 * vectors), cols] = jnp.concatenate(
            [
                jnp.concatenate([lo_real, lo_imag], axis=1),
                jnp.concatenate([-lo_imag, lo_real], axis=1),
            ],
            axis=0,
        )


def adjoint_item(links, lower, slot, left_ref):
    sites, vectors, width = lower.shape
    half = width // 2
    low = lower_half((vectors, width))
    sign = signs((vectors, width), jnp.float32)
    for pair in range(sites // 2):
        agg, part = divmod(pair, SIDE // 2)
        at = 2 * pair
        lo_a, lo_b = lower[at], lower[at + 1]
        zero = jnp.zeros_like(lo_a)
        rows = jnp.concatenate(
            [
                jnp.where(low, lo_a, zero),
                jnp.where(low, swapped(lo_a), zero),
                jnp.where(low, zero, swapped(lo_b)),
                jnp.where(low, zero, lo_b),
            ],
            axis=0,
        )
        mats = links[pl.ds(at, 2)].reshape(2 * half, width)
        prod = dot(rows, mats, MAT_DIMS)
        adj_a = sign * prod[:vectors] + swapped(prod[vectors : 2 * vectors])
        adj_b = sign * prod[2 * vectors : 3 * vectors] + swapped(prod[3 * vectors :])
        turn_a = -sign * swapped(adj_a)
        turn_b = -sign * swapped(adj_b)
        cols = pl.ds((slot * 2 + part) * 2 * width, 2 * width)
        left_ref[pl.ds(agg * 2 * vectors, 2 * vectors), cols] = jnp.concatenate(
            [
                jnp.concatenate([adj_a, adj_b], axis=1),
                jnp.concatenate([turn_a, turn_b], axis=1),
            ],
            axis=0,
        ).astype(jnp.bfloat16)


def group_rows(left, right, vectors):
    full = dot(left, right, ROW_DIMS)
    aggs = full.shape[1] // vectors
    lanes = lax.broadcasted_iota(jnp.int32, (2 * vectors, full.shape[1]), 1) // vectors
    own = jnp.zeros((2 * vectors, full.shape[1]), jnp.float32)
    for agg in range(aggs):
        own = jnp.where(lanes == agg, full[agg * 2 * vectors : (agg + 1) * 2 * vectors], own)
    pieces = []
    lane_group = lax.broadcasted_iota(jnp.int32, (aggs, full.shape[1]), 1) // vectors
    sub = lax.broadcasted_iota(jnp.int32, (aggs, full.shape[1]), 0)
    total = full.shape[1]
    for piece in range(2 * vectors // aggs):
        value = own[piece * aggs : (piece + 1) * aggs]
        step = 1
        while step < aggs:
            sub_bit = (sub // step) % 2
            lane_bit = (lane_group // step) % 2
            up = pltpu.roll(pltpu.roll(value, aggs - step, axis=0), step * vectors, axis=1)
            down = pltpu.roll(pltpu.roll(value, step, axis=0), total - step * vectors, axis=1)
            value = jnp.where(sub_bit == lane_bit, value, jnp.where(sub_bit == 0, up, down))
            step *= 2
        pieces.append(value)
    return jnp.concatenate(pieces, axis=1)


def inner_kernel(place, lists, nulls, time_links, space_links, time_rows, space_rows, adjoint, picks, links, left, right, sems):
    time_count, space_count, sites, vectors, width = nulls.shape
    copies = []

    def fetch(source):
        slot = len(copies)
        copy = pltpu.make_async_copy(source, links.at[slot], sems.at[slot])
        copy.start()
        copies.append(copy)

    for x in range(4):
        fetch(time_links.at[0, x])
    for t in range(4):
        fetch(space_links.at[t, 0])
    for t in range(4):
        fetch(space_links.at[t, 1])
    me = place[0]
    shards, cap = lists.shape
    count = picks.shape[2]
    lane = lax.broadcasted_iota(jnp.int32, (MOST, cap), 1)
    want = lax.broadcasted_iota(jnp.int32, (MOST, cap), 0)
    column = lax.broadcasted_iota(jnp.int32, (MOST, count), 1)
    quarter = count // 4
    turned = (column // quarter % 2) * 2 * quarter + (column // (2 * quarter)) * quarter + column % quarter
    for shard in range(shards):
        mine = jnp.broadcast_to(lists[pl.ds(shard, 1), :], (MOST, cap))
        before = jnp.where((mine >= 0) & (mine < me * count), 1, 0)
        start = jnp.sum(before.astype(jnp.float32), axis=1, keepdims=True).astype(jnp.int32)
        inside = (mine >= me * count) & (mine < (me + 1) * count)
        match = inside & (lane - start == want)
        chosen = jnp.sum(jnp.where(match, mine - me * count + 1, 0).astype(jnp.float32), axis=1, keepdims=True)
        chosen = chosen.astype(jnp.int32) - 1
        picks[0, pl.ds(shard * MOST, MOST), :] = jnp.where(column == chosen, 1.0, 0.0)
        picks[1, pl.ds(shard * MOST, MOST), :] = jnp.where(turned == chosen, 1.0, 0.0)
    for a_x in range(2):
        for c in range(2):
            x = 2 * a_x + c
            copies[x].wait()
            image_item(links.at[x], nulls.at[1, x], nulls.at[2, x], c, left, right)
        time_rows[pl.ds(a_x * 8, 8), :] = group_rows(left[...], right[...], vectors)
    for a_t in range(2):
        for c in range(2):
            t = 2 * a_t + c
            copies[4 + t].wait()
            image_item(links.at[4 + t], nulls.at[t, 1], nulls.at[t, 2], c, left, right)
        space_rows[pl.ds(a_t * 8, 8), :] = group_rows(left[...], right[...], vectors)
    for t in range(4):
        copies[8 + t].wait()
        adjoint_item(links.at[8 + t], nulls.at[t, 3], t % 2, adjoint.at[t // 2])


def time_edge_kernel(nulls, edge, time_links, time_rows, links, left, right, sems):
    vectors = nulls.shape[-2]
    copies = []
    for x in range(4):
        copy = pltpu.make_async_copy(time_links.at[1, x], links.at[x], sems.at[x])
        copy.start()
        copies.append(copy)
    for a_x in range(2):
        for c in range(2):
            x = 2 * a_x + c
            copies[x].wait()
            image_item(links.at[x], nulls.at[0, x], edge.at[0, x], c, left, right)
        time_rows[pl.ds(a_x * 8, 8), :] = group_rows(left[...], right[...], vectors)


def final_kernel(edge, adjoint, picks, time_low, time_high, space_low, packed):
    sites, vectors, width = edge.shape[2:]
    aggs = sites // SIDE
    found = []
    for a_t in range(2):
        parts = []
        for c in range(2):
            for site in range(SIDE):
                rows = [edge[2 * a_t + c, 0, agg * SIDE + site] for agg in range(aggs)]
                parts.append(jnp.concatenate(rows, axis=0))
        found.append(group_rows(adjoint[a_t], jnp.concatenate(parts, axis=1), vectors))
    time_rows = jnp.concatenate([time_low[...], time_high[...]], axis=0).astype(jnp.bfloat16)
    space_rows = jnp.concatenate([space_low[...]] + found, axis=0).astype(jnp.bfloat16)
    wide = time_rows.shape[1]
    packed[:, pl.ds(0, wide)] = dot(picks[0].astype(jnp.bfloat16), time_rows, MAT_DIMS).astype(jnp.bfloat16)
    packed[:, pl.ds(wide, wide)] = dot(picks[1].astype(jnp.bfloat16), space_rows, MAT_DIMS).astype(jnp.bfloat16)


def on_device(nulls, time_links, space_links, owner_lists):
    time_count, space_count, sites, vectors, width = nulls.shape
    shards, cap = owner_lists.shape
    aggs = sites // SIDE
    local_count = (time_count // 2) * (space_count // 2) * aggs
    wide = 2 * vectors * vectors
    edge_space = shifted(nulls[:, 0:1], "xyz", -1)
    edge_time = shifted(nulls[0:1], "ta", -1)
    place = lax.axis_index("xyz").astype(jnp.int32).reshape(1)
    vmem = pl.BlockSpec(memory_space=pltpu.VMEM)
    smem = pl.BlockSpec(memory_space=pltpu.SMEM)
    anywhere = pl.BlockSpec(memory_space=pl.ANY)
    half = width // 2
    grouped = [
        pltpu.VMEM((2 * vectors * aggs, 8 * width), jnp.bfloat16),
        pltpu.VMEM((vectors * aggs, 8 * width), jnp.bfloat16),
    ]
    params = pltpu.CompilerParams(vmem_limit_bytes=40 * 1024 * 1024)
    time_low, space_low, adjoint, picks = pl.pallas_call(
        inner_kernel,
        in_specs=[smem, vmem, vmem, anywhere, anywhere],
        out_specs=[vmem] * 4,
        out_shape=[
            jax.ShapeDtypeStruct((2 * aggs, wide), jnp.float32),
            jax.ShapeDtypeStruct((2 * aggs, wide), jnp.float32),
            jax.ShapeDtypeStruct((2, 2 * vectors * aggs, 8 * width), jnp.bfloat16),
            jax.ShapeDtypeStruct((2, shards * MOST, local_count), jnp.float32),
        ],
        scratch_shapes=[pltpu.VMEM((12, sites, half, width), jnp.bfloat16)] + grouped + [pltpu.SemaphoreType.DMA((12,))],
        compiler_params=params,
        cost_estimate=pl.CostEstimate(flops=400 * 10**6, bytes_accessed=10 * 2**20, transcendentals=0),
        name="inner",
    )(place, owner_lists, nulls, time_links, space_links)
    time_high = pl.pallas_call(
        time_edge_kernel,
        in_specs=[vmem, vmem, anywhere],
        out_specs=vmem,
        out_shape=jax.ShapeDtypeStruct((2 * aggs, wide), jnp.float32),
        scratch_shapes=[pltpu.VMEM((4, sites, half, width), jnp.bfloat16)] + grouped + [pltpu.SemaphoreType.DMA((4,))],
        compiler_params=params,
        cost_estimate=pl.CostEstimate(flops=130 * 10**6, bytes_accessed=3 * 2**20, transcendentals=0),
        name="time_edge",
    )(nulls[3:4], edge_time, time_links)
    packed = pl.pallas_call(
        final_kernel,
        in_specs=[vmem] * 6,
        out_specs=vmem,
        out_shape=jax.ShapeDtypeStruct((shards * MOST, 2 * wide), jnp.bfloat16),
        compiler_params=params,
        cost_estimate=pl.CostEstimate(flops=130 * 10**6, bytes_accessed=2 * 2**20, transcendentals=0),
        name="final",
    )(edge_space, adjoint, picks, time_low, time_high, space_low)
    arrived = lax.all_to_all(packed, "xyz", 0, 0, tiled=True)
    if shards * MOST == cap:
        result = arrived.astype(jnp.float32)
    else:
        my_list = lax.dynamic_index_in_dim(owner_lists, lax.axis_index("xyz"), 0, keepdims=False)
        source = jnp.maximum(my_list, 0) // local_count
        order = jnp.arange(cap, dtype=jnp.int32)
        same = (source[:, None] == source[None, :]) & (order[None, :] < order[:, None])
        offset = jnp.sum(same.astype(jnp.int32), axis=1)
        picked = arrived[source * MOST + offset].astype(jnp.float32)
        result = jnp.where((my_list >= 0)[:, None], picked, 0.0)
    return result[None]


def solution(mesh):
    return jax.shard_map(
        on_device,
        mesh=mesh,
        in_specs=(
            P("ta", "xyz", None, None, None),
            P("ta", "xyz", None, None, None),
            P("ta", "xyz", None, None, None),
            P(),
        ),
        out_specs=P("ta", "xyz", None),
        check_vma=False,
    )
```

```python
import jax
import jax.numpy as jnp
from jax import lax
from jax.experimental import pallas as pl
from jax.experimental.pallas import tpu as pltpu
from jax.sharding import PartitionSpec as P

ROW_DIMS = (((1,), (1,)), ((), ()))
MAT_DIMS = (((1,), (0,)), ((), ()))
SIDE = 4
MOST = 8


def shifted(array, axis, by):
    count = lax.axis_size(axis)
    return lax.ppermute(array, axis, [(i, (i + by) % count) for i in range(count)])


def dot(left, right, dims):
    return lax.dot_general(left, right, dims, preferred_element_type=jnp.float32)


def swapped(array):
    return pltpu.roll(array, array.shape[-1] // 2, axis=array.ndim - 1)


def lower_half(shape):
    return lax.broadcasted_iota(jnp.int32, shape, len(shape) - 1) < shape[-1] // 2


def signs(shape, dtype):
    return jnp.where(lower_half(shape), 1.0, -1.0).astype(dtype)


def image_item(links, lower, upper, slot, left_ref, right_ref):
    sites, vectors, width = lower.shape
    half = width // 2
    aggs = sites // SIDE
    sign = signs((vectors, width), jnp.bfloat16)
    zero = jnp.zeros((vectors, width), jnp.bfloat16)
    owner = lax.broadcasted_iota(jnp.int32, (half, 2 * aggs * vectors), 1) // (2 * vectors) % (aggs // 2)
    for part in range(SIDE):
        at = (slot * SIDE + part) * width
        mats = []
        plain, crossed = [], []
        for agg in range(aggs):
            site = agg * SIDE + part
            up = upper[site]
            pair = (up * sign, swapped(up))
            for rows, value in zip((plain, crossed), pair):
                rows.append(jnp.concatenate([value, zero] if agg % 2 == 0 else [zero, value], axis=1))
            if agg % 2 == 0:
                mats.append(jnp.concatenate([links[site], links[site + SIDE]], axis=1))
            low = lower[site]
            left_ref[pl.ds(agg * 2 * vectors, 2 * vectors), pl.ds(at, width)] = jnp.concatenate(
                [low, -sign * swapped(low)], axis=0
            )
        images = dot(jnp.concatenate(mats, axis=0), jnp.concatenate(plain + crossed, axis=0), ROW_DIMS)
        own = images[:half]
        for pair in range(1, aggs // 2):
            own = jnp.where(owner == pair, images[pair * half : (pair + 1) * half], own)
        own = own.astype(jnp.bfloat16)
        right_ref[pl.ds(at, half), :] = own[:, : aggs * vectors]
        right_ref[pl.ds(at + half, half), :] = own[:, aggs * vectors :]


def adjoint_item(links, lower, slot, left_ref):
    sites, vectors, width = lower.shape
    half = width // 2
    low = lower_half((vectors, width))
    sign = signs((vectors, width), jnp.float32)
    zero = jnp.zeros((vectors, width), jnp.bfloat16)
    for agg in range(sites // SIDE):
        rows = []
        mats = []
        for pair in range(SIDE // 2):
            at = agg * SIDE + 2 * pair
            lo_a, lo_b = lower[at], lower[at + 1]
            rows += [
                jnp.where(low, lo_a, zero),
                jnp.where(low, swapped(lo_a), zero),
                jnp.where(low, zero, swapped(lo_b)),
                jnp.where(low, zero, lo_b),
            ]
            mats.append(jnp.concatenate([links[at], links[at + 1]], axis=0))
        prod = dot(jnp.concatenate(rows, axis=0), jnp.concatenate(mats, axis=1), MAT_DIMS)
        for part in range(SIDE):
            top = part * 2 * vectors
            mine = prod[top : top + 2 * vectors, part // 2 * width : (part // 2 + 1) * width]
            adj = sign * mine[:vectors] + swapped(mine[vectors:])
            both = jnp.concatenate([adj, -sign * swapped(adj)], axis=0).astype(jnp.bfloat16)
            left_ref[pl.ds(agg * 2 * vectors, 2 * vectors), pl.ds((slot * SIDE + part) * width, width)] = both


def group_rows(left, right, dims, vectors):
    full = dot(left, right, dims)
    aggs = full.shape[1] // vectors
    lanes = lax.broadcasted_iota(jnp.int32, (2 * vectors, full.shape[1]), 1) // vectors
    own = jnp.zeros((2 * vectors, full.shape[1]), jnp.float32)
    for agg in range(aggs):
        own = jnp.where(lanes == agg, full[agg * 2 * vectors : (agg + 1) * 2 * vectors], own)
    pieces = []
    lane_group = lax.broadcasted_iota(jnp.int32, (aggs, full.shape[1]), 1) // vectors
    sub = lax.broadcasted_iota(jnp.int32, (aggs, full.shape[1]), 0)
    total = full.shape[1]
    for piece in range(2 * vectors // aggs):
        value = own[piece * aggs : (piece + 1) * aggs]
        step = 1
        while step < aggs:
            sub_bit = (sub // step) % 2
            lane_bit = (lane_group // step) % 2
            up = pltpu.roll(pltpu.roll(value, aggs - step, axis=0), step * vectors, axis=1)
            down = pltpu.roll(pltpu.roll(value, step, axis=0), total - step * vectors, axis=1)
            value = jnp.where(sub_bit == lane_bit, value, jnp.where(sub_bit == 0, up, down))
            step *= 2
        pieces.append(value)
    return jnp.concatenate(pieces, axis=1)


def edges_kernel(nulls, space_edge, time_edge, sems):
    copies = [pltpu.make_async_copy(nulls.at[:, pl.ds(0, 1)], space_edge, sems.at[0])]
    copies.append(pltpu.make_async_copy(nulls.at[pl.ds(0, 1)], time_edge, sems.at[1]))
    for copy in copies:
        copy.start()
    for copy in copies:
        copy.wait()


def inner_kernel(place, lists, nulls, time_links, space_links, time_rows, space_rows, adjoint, picks, links, vecs, left, right, sems):
    time_count, space_count, sites, vectors, width = nulls.shape
    copies = []
    base = pltpu.make_async_copy(nulls, vecs, sems.at[12])
    base.start()

    def fetch(source):
        slot = len(copies)
        copy = pltpu.make_async_copy(source, links.at[slot], sems.at[slot])
        copy.start()
        copies.append(copy)

    for x in range(4):
        fetch(time_links.at[0, x])
    for t in range(4):
        fetch(space_links.at[t, 0])
    for t in range(4):
        fetch(space_links.at[t, 1])
    me = place[0]
    shards, cap = lists.shape
    count = picks.shape[2]
    lane = lax.broadcasted_iota(jnp.int32, (MOST, cap), 1)
    want = lax.broadcasted_iota(jnp.int32, (MOST, cap), 0)
    column = lax.broadcasted_iota(jnp.int32, (MOST, count), 1)
    quarter = count // 4
    turned = (column // quarter % 2) * 2 * quarter + (column // (2 * quarter)) * quarter + column % quarter
    for shard in range(shards):
        mine = jnp.broadcast_to(lists[pl.ds(shard, 1), :], (MOST, cap))
        before = jnp.where((mine >= 0) & (mine < me * count), 1, 0)
        start = jnp.sum(before.astype(jnp.float32), axis=1, keepdims=True).astype(jnp.int32)
        inside = (mine >= me * count) & (mine < (me + 1) * count)
        match = inside & (lane - start == want)
        chosen = jnp.sum(jnp.where(match, mine - me * count + 1, 0).astype(jnp.float32), axis=1, keepdims=True)
        chosen = chosen.astype(jnp.int32) - 1
        picks[0, pl.ds(shard * MOST, MOST), :] = jnp.where(column == chosen, 1.0, 0.0)
        picks[1, pl.ds(shard * MOST, MOST), :] = jnp.where(turned == chosen, 1.0, 0.0)
    base.wait()
    for a_x in range(2):
        copies[2 * a_x].wait()
        copies[2 * a_x + 1].wait()
        for c in range(2):
            x = 2 * a_x + c
            image_item(links.at[x], vecs.at[1, x], vecs.at[2, x], c, left, right)
        time_rows[pl.ds(a_x * 8, 8), :] = group_rows(left[...], right[...], MAT_DIMS, vectors)
    for a_t in range(2):
        copies[4 + 2 * a_t].wait()
        copies[5 + 2 * a_t].wait()
        for c in range(2):
            t = 2 * a_t + c
            image_item(links.at[4 + t], vecs.at[t, 1], vecs.at[t, 2], c, left, right)
        space_rows[pl.ds(a_t * 8, 8), :] = group_rows(left[...], right[...], MAT_DIMS, vectors)
    for t in range(4):
        copies[8 + t].wait()
    for t in range(4):
        adjoint_item(links.at[8 + t], vecs.at[t, 3], t % 2, adjoint.at[t // 2])


def time_edge_kernel(nulls, edge, time_links, time_rows, links, left, right, sems):
    vectors = nulls.shape[-2]
    copies = []
    for x in range(4):
        copy = pltpu.make_async_copy(time_links.at[1, x], links.at[x], sems.at[x])
        copy.start()
        copies.append(copy)
    for a_x in range(2):
        copies[2 * a_x].wait()
        copies[2 * a_x + 1].wait()
        for c in range(2):
            x = 2 * a_x + c
            image_item(links.at[x], nulls.at[0, x], edge.at[0, x], c, left, right)
        time_rows[pl.ds(a_x * 8, 8), :] = group_rows(left[...], right[...], MAT_DIMS, vectors)


def final_kernel(edge, adjoint, picks, time_low, time_high, space_low, packed):
    sites, vectors, width = edge.shape[2:]
    aggs = sites // SIDE
    found = []
    for a_t in range(2):
        parts = []
        for c in range(2):
            for site in range(SIDE):
                rows = [edge[2 * a_t + c, 0, agg * SIDE + site] for agg in range(aggs)]
                parts.append(jnp.concatenate(rows, axis=0))
        found.append(group_rows(adjoint[a_t], jnp.concatenate(parts, axis=1), ROW_DIMS, vectors))
    time_rows = jnp.concatenate([time_low[...], time_high[...]], axis=0).astype(jnp.bfloat16)
    space_rows = jnp.concatenate([space_low[...]] + found, axis=0).astype(jnp.bfloat16)
    wide = time_rows.shape[1]
    packed[:, pl.ds(0, wide)] = dot(picks[0].astype(jnp.bfloat16), time_rows, MAT_DIMS).astype(jnp.bfloat16)
    packed[:, pl.ds(wide, wide)] = dot(picks[1].astype(jnp.bfloat16), space_rows, MAT_DIMS).astype(jnp.bfloat16)


def on_device(nulls, time_links, space_links, owner_lists):
    time_count, space_count, sites, vectors, width = nulls.shape
    shards, cap = owner_lists.shape
    aggs = sites // SIDE
    local_count = (time_count // 2) * (space_count // 2) * aggs
    wide = 2 * vectors * vectors
    place = lax.axis_index("xyz").astype(jnp.int32).reshape(1)
    vmem = pl.BlockSpec(memory_space=pltpu.VMEM)
    smem = pl.BlockSpec(memory_space=pltpu.SMEM)
    anywhere = pl.BlockSpec(memory_space=pl.ANY)
    outside = pl.BlockSpec(memory_space=pltpu.HBM)
    half = width // 2
    roomy = pltpu.CompilerParams(vmem_limit_bytes=58 * 1024 * 1024)
    modest = pltpu.CompilerParams(vmem_limit_bytes=24 * 1024 * 1024)
    grouped = [
        pltpu.VMEM((2 * vectors * aggs, 8 * width), jnp.bfloat16),
        pltpu.VMEM((8 * width, vectors * aggs), jnp.bfloat16),
    ]
    space_edge, time_edge = pl.pallas_call(
        edges_kernel,
        in_specs=[outside],
        out_specs=[anywhere] * 2,
        out_shape=[
            jax.ShapeDtypeStruct((time_count, 1, sites, vectors, width), nulls.dtype),
            jax.ShapeDtypeStruct((1, space_count, sites, vectors, width), nulls.dtype),
        ],
        scratch_shapes=[pltpu.SemaphoreType.DMA((2,))],
        compiler_params=pltpu.CompilerParams(vmem_limit_bytes=62 * 1024 * 1024),
        cost_estimate=pl.CostEstimate(flops=0, bytes_accessed=2**21, transcendentals=0),
        name="edges",
    )(nulls)
    edge_space = shifted(space_edge, "xyz", -1)
    edge_time = shifted(time_edge, "ta", -1)
    time_low, space_low, adjoint, picks = pl.pallas_call(
        inner_kernel,
        in_specs=[smem, vmem, outside, outside, outside],
        out_specs=[vmem] * 4,
        out_shape=[
            jax.ShapeDtypeStruct((2 * aggs, wide), jnp.float32),
            jax.ShapeDtypeStruct((2 * aggs, wide), jnp.float32),
            jax.ShapeDtypeStruct((2, 2 * vectors * aggs, 8 * width), jnp.bfloat16),
            jax.ShapeDtypeStruct((2, shards * MOST, local_count), jnp.float32),
        ],
        scratch_shapes=[
            pltpu.VMEM((12, sites, half, width), jnp.bfloat16),
            pltpu.VMEM(nulls.shape, nulls.dtype),
        ]
        + grouped
        + [pltpu.SemaphoreType.DMA((13,))],
        compiler_params=roomy,
        cost_estimate=pl.CostEstimate(flops=400 * 10**6, bytes_accessed=10 * 2**20, transcendentals=0),
        name="inner",
    )(place, owner_lists, nulls, time_links, space_links)
    time_high = pl.pallas_call(
        time_edge_kernel,
        in_specs=[vmem, vmem, outside],
        out_specs=vmem,
        out_shape=jax.ShapeDtypeStruct((2 * aggs, wide), jnp.float32),
        scratch_shapes=[pltpu.VMEM((4, sites, half, width), jnp.bfloat16)] + grouped + [pltpu.SemaphoreType.DMA((4,))],
        compiler_params=modest,
        cost_estimate=pl.CostEstimate(flops=130 * 10**6, bytes_accessed=3 * 2**20, transcendentals=0),
        name="time_edge",
    )(nulls[3:4], edge_time, time_links)
    packed = pl.pallas_call(
        final_kernel,
        in_specs=[vmem] * 6,
        out_specs=vmem,
        out_shape=jax.ShapeDtypeStruct((shards * MOST, 2 * wide), jnp.bfloat16),
        compiler_params=modest,
        cost_estimate=pl.CostEstimate(flops=130 * 10**6, bytes_accessed=2 * 2**20, transcendentals=0),
        name="final",
    )(edge_space, adjoint, picks, time_low, time_high, space_low)
    arrived = lax.all_to_all(packed, "xyz", 0, 0, tiled=True)
    if shards * MOST == cap:
        result = arrived.astype(jnp.float32)
    else:
        my_list = lax.dynamic_index_in_dim(owner_lists, lax.axis_index("xyz"), 0, keepdims=False)
        source = jnp.maximum(my_list, 0) // local_count
        order = jnp.arange(cap, dtype=jnp.int32)
        same = (source[:, None] == source[None, :]) & (order[None, :] < order[:, None])
        offset = jnp.sum(same.astype(jnp.int32), axis=1)
        picked = arrived[source * MOST + offset].astype(jnp.float32)
        result = jnp.where((my_list >= 0)[:, None], picked, 0.0)
    return result[None]


def solution(mesh):
    return jax.shard_map(
        on_device,
        mesh=mesh,
        in_specs=(
            P("ta", "xyz", None, None, None),
            P("ta", "xyz", None, None, None),
            P("ta", "xyz", None, None, None),
            P(),
        ),
        out_specs=P("ta", "xyz", None),
        check_vma=False,
    )
```

```python
import jax
import jax.numpy as jnp
from jax import lax
from jax.experimental import pallas as pl
from jax.experimental.pallas import tpu as pltpu
from jax.sharding import PartitionSpec as P

ROW_DIMS = (((1,), (1,)), ((), ()))
MAT_DIMS = (((1,), (0,)), ((), ()))
SIDE = 4
MOST = 8


def shifted(array, axis, by):
    count = lax.axis_size(axis)
    return lax.ppermute(array, axis, [(i, (i + by) % count) for i in range(count)])


def dot(left, right, dims):
    return lax.dot_general(left, right, dims, preferred_element_type=jnp.float32)


def swapped(array):
    return pltpu.roll(array, array.shape[-1] // 2, axis=array.ndim - 1)


def lower_half(shape):
    return lax.broadcasted_iota(jnp.int32, shape, len(shape) - 1) < shape[-1] // 2


def signs(shape, dtype):
    return jnp.where(lower_half(shape), 1.0, -1.0).astype(dtype)


def image_item(links, lower, upper, slot, left_ref, right_ref):
    sites, vectors, width = lower.shape
    half = width // 2
    aggs = sites // SIDE
    sign = signs((vectors, width), jnp.bfloat16)
    zero = jnp.zeros((vectors, width), jnp.bfloat16)
    owner = lax.broadcasted_iota(jnp.int32, (half, 2 * aggs * vectors), 1) // (2 * vectors) % (aggs // 2)
    for part in range(SIDE):
        at = (slot * SIDE + part) * width
        mats = []
        plain, crossed = [], []
        for agg in range(aggs):
            site = agg * SIDE + part
            up = upper[site]
            pair = (up * sign, swapped(up))
            for rows, value in zip((plain, crossed), pair):
                rows.append(jnp.concatenate([value, zero] if agg % 2 == 0 else [zero, value], axis=1))
            if agg % 2 == 0:
                mats.append(jnp.concatenate([links[site], links[site + SIDE]], axis=1))
            low = lower[site]
            left_ref[pl.ds(agg * 2 * vectors, 2 * vectors), pl.ds(at, width)] = jnp.concatenate(
                [low, -sign * swapped(low)], axis=0
            )
        images = dot(jnp.concatenate(mats, axis=0), jnp.concatenate(plain + crossed, axis=0), ROW_DIMS)
        own = images[:half]
        for pair in range(1, aggs // 2):
            own = jnp.where(owner == pair, images[pair * half : (pair + 1) * half], own)
        own = own.astype(jnp.bfloat16)
        right_ref[pl.ds(at, half), :] = own[:, : aggs * vectors]
        right_ref[pl.ds(at + half, half), :] = own[:, aggs * vectors :]


def adjoint_item(links, lower, slot, left_ref):
    sites, vectors, width = lower.shape
    half = width // 2
    low = lower_half((vectors, width))
    sign = signs((vectors, width), jnp.float32)
    zero = jnp.zeros((vectors, width), jnp.bfloat16)
    for agg in range(sites // SIDE):
        rows = []
        mats = []
        for pair in range(SIDE // 2):
            at = agg * SIDE + 2 * pair
            lo_a, lo_b = lower[at], lower[at + 1]
            rows += [
                jnp.where(low, lo_a, zero),
                jnp.where(low, swapped(lo_a), zero),
                jnp.where(low, zero, swapped(lo_b)),
                jnp.where(low, zero, lo_b),
            ]
            mats.append(jnp.concatenate([links[at], links[at + 1]], axis=0))
        prod = dot(jnp.concatenate(rows, axis=0), jnp.concatenate(mats, axis=1), MAT_DIMS)
        for part in range(SIDE):
            top = part * 2 * vectors
            mine = prod[top : top + 2 * vectors, part // 2 * width : (part // 2 + 1) * width]
            adj = sign * mine[:vectors] + swapped(mine[vectors:])
            both = jnp.concatenate([adj, -sign * swapped(adj)], axis=0).astype(jnp.bfloat16)
            left_ref[pl.ds(agg * 2 * vectors, 2 * vectors), pl.ds((slot * SIDE + part) * width, width)] = both


def group_rows(left, right, dims, vectors):
    full = dot(left, right, dims)
    aggs = full.shape[1] // vectors
    lanes = lax.broadcasted_iota(jnp.int32, (2 * vectors, full.shape[1]), 1) // vectors
    own = jnp.zeros((2 * vectors, full.shape[1]), jnp.float32)
    for agg in range(aggs):
        own = jnp.where(lanes == agg, full[agg * 2 * vectors : (agg + 1) * 2 * vectors], own)
    pieces = []
    lane_group = lax.broadcasted_iota(jnp.int32, (aggs, full.shape[1]), 1) // vectors
    sub = lax.broadcasted_iota(jnp.int32, (aggs, full.shape[1]), 0)
    total = full.shape[1]
    for piece in range(2 * vectors // aggs):
        value = own[piece * aggs : (piece + 1) * aggs]
        step = 1
        while step < aggs:
            sub_bit = (sub // step) % 2
            lane_bit = (lane_group // step) % 2
            up = pltpu.roll(pltpu.roll(value, aggs - step, axis=0), step * vectors, axis=1)
            down = pltpu.roll(pltpu.roll(value, step, axis=0), total - step * vectors, axis=1)
            value = jnp.where(sub_bit == lane_bit, value, jnp.where(sub_bit == 0, up, down))
            step *= 2
        pieces.append(value)
    return jnp.concatenate(pieces, axis=1)


def slice_kernel(nulls, space_edge, time_edge, sems):
    copies = [
        pltpu.make_async_copy(nulls.at[:, pl.ds(0, 1)], space_edge, sems.at[0]),
        pltpu.make_async_copy(nulls.at[pl.ds(0, 1)], time_edge, sems.at[1]),
    ]
    for copy in copies:
        copy.start()
    for copy in copies:
        copy.wait()


def inner_kernel(place, lists, nulls, time_links, space_links, time_rows, space_rows, adjoint, picks, links, vecs, left, right, sems):
    time_count, space_count, sites, vectors, width = nulls.shape
    copies = []
    base = pltpu.make_async_copy(nulls, vecs, sems.at[12])
    base.start()

    def fetch(source):
        slot = len(copies)
        copy = pltpu.make_async_copy(source, links.at[slot], sems.at[slot])
        copy.start()
        copies.append(copy)

    for x in range(4):
        fetch(time_links.at[0, x])
    for t in range(4):
        fetch(space_links.at[t, 0])
    for t in range(4):
        fetch(space_links.at[t, 1])
    me = place[0]
    shards, cap = lists.shape
    count = picks.shape[2]
    lane = lax.broadcasted_iota(jnp.int32, (MOST, cap), 1)
    want = lax.broadcasted_iota(jnp.int32, (MOST, cap), 0)
    column = lax.broadcasted_iota(jnp.int32, (MOST, count), 1)
    quarter = count // 4
    turned = (column // quarter % 2) * 2 * quarter + (column // (2 * quarter)) * quarter + column % quarter
    for shard in range(shards):
        mine = jnp.broadcast_to(lists[pl.ds(shard, 1), :], (MOST, cap))
        before = jnp.where((mine >= 0) & (mine < me * count), 1, 0)
        start = jnp.sum(before.astype(jnp.float32), axis=1, keepdims=True).astype(jnp.int32)
        inside = (mine >= me * count) & (mine < (me + 1) * count)
        match = inside & (lane - start == want)
        chosen = jnp.sum(jnp.where(match, mine - me * count + 1, 0).astype(jnp.float32), axis=1, keepdims=True)
        chosen = chosen.astype(jnp.int32) - 1
        picks[0, pl.ds(shard * MOST, MOST), :] = jnp.where(column == chosen, 1.0, 0.0)
        picks[1, pl.ds(shard * MOST, MOST), :] = jnp.where(turned == chosen, 1.0, 0.0)
    base.wait()
    for a_x in range(2):
        copies[2 * a_x].wait()
        copies[2 * a_x + 1].wait()
        for c in range(2):
            x = 2 * a_x + c
            image_item(links.at[x], vecs.at[1, x], vecs.at[2, x], c, left, right)
        time_rows[pl.ds(a_x * 8, 8), :] = group_rows(left[...], right[...], MAT_DIMS, vectors)
    for a_t in range(2):
        copies[4 + 2 * a_t].wait()
        copies[5 + 2 * a_t].wait()
        for c in range(2):
            t = 2 * a_t + c
            image_item(links.at[4 + t], vecs.at[t, 1], vecs.at[t, 2], c, left, right)
        space_rows[pl.ds(a_t * 8, 8), :] = group_rows(left[...], right[...], MAT_DIMS, vectors)
    for t in range(4):
        copies[8 + t].wait()
    for t in range(4):
        adjoint_item(links.at[8 + t], vecs.at[t, 3], t % 2, adjoint.at[t // 2])


def time_edge_kernel(nulls, edge, time_links, time_rows, links, vecs, left, right, sems):
    vectors = nulls.shape[-2]
    copies = []
    base = pltpu.make_async_copy(nulls.at[3], vecs, sems.at[4])
    base.start()
    for x in range(4):
        copy = pltpu.make_async_copy(time_links.at[1, x], links.at[x], sems.at[x])
        copy.start()
        copies.append(copy)
    base.wait()
    for a_x in range(2):
        copies[2 * a_x].wait()
        copies[2 * a_x + 1].wait()
        for c in range(2):
            x = 2 * a_x + c
            image_item(links.at[x], vecs.at[x], edge.at[0, x], c, left, right)
        time_rows[pl.ds(a_x * 8, 8), :] = group_rows(left[...], right[...], MAT_DIMS, vectors)


def final_kernel(edge, adjoint, picks, time_low, time_high, space_low, packed):
    sites, vectors, width = edge.shape[2:]
    aggs = sites // SIDE
    found = []
    for a_t in range(2):
        parts = []
        for c in range(2):
            for site in range(SIDE):
                rows = [edge[2 * a_t + c, 0, agg * SIDE + site] for agg in range(aggs)]
                parts.append(jnp.concatenate(rows, axis=0))
        found.append(group_rows(adjoint[a_t], jnp.concatenate(parts, axis=1), ROW_DIMS, vectors))
    time_rows = jnp.concatenate([time_low[...], time_high[...]], axis=0).astype(jnp.bfloat16)
    space_rows = jnp.concatenate([space_low[...]] + found, axis=0).astype(jnp.bfloat16)
    wide = time_rows.shape[1]
    packed[:, pl.ds(0, wide)] = dot(picks[0].astype(jnp.bfloat16), time_rows, MAT_DIMS).astype(jnp.bfloat16)
    packed[:, pl.ds(wide, wide)] = dot(picks[1].astype(jnp.bfloat16), space_rows, MAT_DIMS).astype(jnp.bfloat16)


def on_device(nulls, time_links, space_links, owner_lists):
    time_count, space_count, sites, vectors, width = nulls.shape
    shards, cap = owner_lists.shape
    aggs = sites // SIDE
    local_count = (time_count // 2) * (space_count // 2) * aggs
    wide = 2 * vectors * vectors
    place = lax.axis_index("xyz").astype(jnp.int32).reshape(1)
    vmem = pl.BlockSpec(memory_space=pltpu.VMEM)
    smem = pl.BlockSpec(memory_space=pltpu.SMEM)
    anywhere = pl.BlockSpec(memory_space=pl.ANY)
    outside = pl.BlockSpec(memory_space=pltpu.HBM)
    half = width // 2
    roomy = pltpu.CompilerParams(vmem_limit_bytes=58 * 1024 * 1024)
    modest = pltpu.CompilerParams(vmem_limit_bytes=24 * 1024 * 1024)
    grouped = [
        pltpu.VMEM((2 * vectors * aggs, 8 * width), jnp.bfloat16),
        pltpu.VMEM((8 * width, vectors * aggs), jnp.bfloat16),
    ]
    first = pltpu.CompilerParams(vmem_limit_bytes=60 * 1024 * 1024)
    space_edge, time_edge = pl.pallas_call(
        slice_kernel,
        in_specs=[outside],
        out_specs=[vmem] * 2,
        out_shape=[
            jax.ShapeDtypeStruct((time_count, 1, sites, vectors, width), nulls.dtype),
            jax.ShapeDtypeStruct((1, space_count, sites, vectors, width), nulls.dtype),
        ],
        scratch_shapes=[pltpu.SemaphoreType.DMA((2,))],
        compiler_params=first,
        cost_estimate=pl.CostEstimate(flops=1000, bytes_accessed=1000, transcendentals=0),
        name="slices",
    )(nulls)
    edge_time = shifted(time_edge, "ta", -1)
    edge_space = shifted(space_edge, "xyz", -1)
    time_low, space_low, adjoint, picks = pl.pallas_call(
        inner_kernel,
        in_specs=[smem, vmem, outside, outside, outside],
        out_specs=[vmem] * 4,
        out_shape=[
            jax.ShapeDtypeStruct((2 * aggs, wide), jnp.float32),
            jax.ShapeDtypeStruct((2 * aggs, wide), jnp.float32),
            jax.ShapeDtypeStruct((2, 2 * vectors * aggs, 8 * width), jnp.bfloat16),
            jax.ShapeDtypeStruct((2, shards * MOST, local_count), jnp.float32),
        ],
        scratch_shapes=[
            pltpu.VMEM((12, sites, half, width), jnp.bfloat16),
            pltpu.VMEM(nulls.shape, nulls.dtype),
        ]
        + grouped
        + [pltpu.SemaphoreType.DMA((13,))],
        compiler_params=roomy,
        cost_estimate=pl.CostEstimate(flops=1000, bytes_accessed=1000, transcendentals=0),
        name="inner",
    )(place, owner_lists, nulls, time_links, space_links)
    time_high = pl.pallas_call(
        time_edge_kernel,
        in_specs=[outside, vmem, outside],
        out_specs=vmem,
        out_shape=jax.ShapeDtypeStruct((2 * aggs, wide), jnp.float32),
        scratch_shapes=[
            pltpu.VMEM((4, sites, half, width), jnp.bfloat16),
            pltpu.VMEM(nulls.shape[1:], nulls.dtype),
        ]
        + grouped
        + [pltpu.SemaphoreType.DMA((5,))],
        compiler_params=modest,
        cost_estimate=pl.CostEstimate(flops=1000, bytes_accessed=1000, transcendentals=0),
        name="time_edge",
    )(nulls, edge_time, time_links)
    packed = pl.pallas_call(
        final_kernel,
        in_specs=[vmem] * 6,
        out_specs=vmem,
        out_shape=jax.ShapeDtypeStruct((shards * MOST, 2 * wide), jnp.bfloat16),
        compiler_params=modest,
        cost_estimate=pl.CostEstimate(flops=1000, bytes_accessed=1000, transcendentals=0),
        name="final",
    )(edge_space, adjoint, picks, time_low, time_high, space_low)
    arrived = lax.all_to_all(packed, "xyz", 0, 0, tiled=True)
    if shards * MOST == cap:
        result = arrived.astype(jnp.float32)
    else:
        my_list = lax.dynamic_index_in_dim(owner_lists, lax.axis_index("xyz"), 0, keepdims=False)
        source = jnp.maximum(my_list, 0) // local_count
        order = jnp.arange(cap, dtype=jnp.int32)
        same = (source[:, None] == source[None, :]) & (order[None, :] < order[:, None])
        offset = jnp.sum(same.astype(jnp.int32), axis=1)
        picked = arrived[source * MOST + offset].astype(jnp.float32)
        result = jnp.where((my_list >= 0)[:, None], picked, 0.0)
    return result[None]


def solution(mesh):
    return jax.shard_map(
        on_device,
        mesh=mesh,
        in_specs=(
            P("ta", "xyz", None, None, None),
            P("ta", "xyz", None, None, None),
            P("ta", "xyz", None, None, None),
            P(),
        ),
        out_specs=P("ta", "xyz", None),
        check_vma=False,
    )
```

```python
import jax
import jax.numpy as jnp
from jax import lax
from jax.experimental import pallas as pl
from jax.experimental.pallas import tpu as pltpu
from jax.sharding import PartitionSpec as P

ROW_DIMS = (((1,), (1,)), ((), ()))
MAT_DIMS = (((1,), (0,)), ((), ()))
SIDE = 4
MOST = 8


def shifted(array, axis, by):
    count = lax.axis_size(axis)
    return lax.ppermute(array, axis, [(i, (i + by) % count) for i in range(count)])


def dot(left, right, dims):
    return lax.dot_general(left, right, dims, preferred_element_type=jnp.float32)


def swapped(array):
    return pltpu.roll(array, array.shape[-1] // 2, axis=array.ndim - 1)


def lower_half(shape):
    return lax.broadcasted_iota(jnp.int32, shape, len(shape) - 1) < shape[-1] // 2


def signs(shape, dtype):
    return jnp.where(lower_half(shape), 1.0, -1.0).astype(dtype)


def image_item(links, lower, upper, slot, left_ref, right_ref):
    sites, vectors, width = lower.shape
    half = width // 2
    aggs = sites // SIDE
    sign = signs((vectors, width), jnp.bfloat16)
    zero = jnp.zeros((vectors, width), jnp.bfloat16)
    owner = lax.broadcasted_iota(jnp.int32, (half, 2 * aggs * vectors), 1) // (2 * vectors) % (aggs // 2)
    for part in range(SIDE):
        at = (slot * SIDE + part) * width
        mats = []
        plain, crossed = [], []
        for agg in range(aggs):
            site = agg * SIDE + part
            up = upper[site]
            pair = (up * sign, swapped(up))
            for rows, value in zip((plain, crossed), pair):
                rows.append(jnp.concatenate([value, zero] if agg % 2 == 0 else [zero, value], axis=1))
            if agg % 2 == 0:
                mats.append(jnp.concatenate([links[site], links[site + SIDE]], axis=1))
            low = lower[site]
            left_ref[pl.ds(agg * 2 * vectors, 2 * vectors), pl.ds(at, width)] = jnp.concatenate(
                [low, -sign * swapped(low)], axis=0
            )
        images = dot(jnp.concatenate(mats, axis=0), jnp.concatenate(plain + crossed, axis=0), ROW_DIMS)
        own = images[:half]
        for pair in range(1, aggs // 2):
            own = jnp.where(owner == pair, images[pair * half : (pair + 1) * half], own)
        own = own.astype(jnp.bfloat16)
        right_ref[pl.ds(at, half), :] = own[:, : aggs * vectors]
        right_ref[pl.ds(at + half, half), :] = own[:, aggs * vectors :]


def adjoint_item(links, lower, slot, left_ref):
    sites, vectors, width = lower.shape
    half = width // 2
    low = lower_half((vectors, width))
    sign = signs((vectors, width), jnp.float32)
    zero = jnp.zeros((vectors, width), jnp.bfloat16)
    for agg in range(sites // SIDE):
        rows = []
        mats = []
        for pair in range(SIDE // 2):
            at = agg * SIDE + 2 * pair
            lo_a, lo_b = lower[at], lower[at + 1]
            rows += [
                jnp.where(low, lo_a, zero),
                jnp.where(low, swapped(lo_a), zero),
                jnp.where(low, zero, swapped(lo_b)),
                jnp.where(low, zero, lo_b),
            ]
            mats.append(jnp.concatenate([links[at], links[at + 1]], axis=0))
        prod = dot(jnp.concatenate(rows, axis=0), jnp.concatenate(mats, axis=1), MAT_DIMS)
        for part in range(SIDE):
            top = part * 2 * vectors
            mine = prod[top : top + 2 * vectors, part // 2 * width : (part // 2 + 1) * width]
            adj = sign * mine[:vectors] + swapped(mine[vectors:])
            both = jnp.concatenate([adj, -sign * swapped(adj)], axis=0).astype(jnp.bfloat16)
            left_ref[pl.ds(agg * 2 * vectors, 2 * vectors), pl.ds((slot * SIDE + part) * width, width)] = both


def group_rows(left, right, dims, vectors):
    full = dot(left, right, dims)
    aggs = full.shape[1] // vectors
    lanes = lax.broadcasted_iota(jnp.int32, (2 * vectors, full.shape[1]), 1) // vectors
    own = jnp.zeros((2 * vectors, full.shape[1]), jnp.float32)
    for agg in range(aggs):
        own = jnp.where(lanes == agg, full[agg * 2 * vectors : (agg + 1) * 2 * vectors], own)
    pieces = []
    lane_group = lax.broadcasted_iota(jnp.int32, (aggs, full.shape[1]), 1) // vectors
    sub = lax.broadcasted_iota(jnp.int32, (aggs, full.shape[1]), 0)
    total = full.shape[1]
    for piece in range(2 * vectors // aggs):
        value = own[piece * aggs : (piece + 1) * aggs]
        step = 1
        while step < aggs:
            sub_bit = (sub // step) % 2
            lane_bit = (lane_group // step) % 2
            up = pltpu.roll(pltpu.roll(value, aggs - step, axis=0), step * vectors, axis=1)
            down = pltpu.roll(pltpu.roll(value, step, axis=0), total - step * vectors, axis=1)
            value = jnp.where(sub_bit == lane_bit, value, jnp.where(sub_bit == 0, up, down))
            step *= 2
        pieces.append(value)
    return jnp.concatenate(pieces, axis=1)


def slice_kernel(nulls, space_edge, time_edge, sems):
    copies = [
        pltpu.make_async_copy(nulls.at[:, pl.ds(0, 1)], space_edge, sems.at[0]),
        pltpu.make_async_copy(nulls.at[pl.ds(0, 1)], time_edge, sems.at[1]),
    ]
    for copy in copies:
        copy.start()
    for copy in copies:
        copy.wait()


def inner_kernel(place, lists, nulls, time_links, space_links, time_rows, space_rows, adjoint, picks, links, vecs, left, right, sems):
    time_count, space_count, sites, vectors, width = nulls.shape
    copies = []
    base = pltpu.make_async_copy(nulls, vecs, sems.at[12])
    base.start()

    def fetch(source):
        slot = len(copies)
        copy = pltpu.make_async_copy(source, links.at[slot], sems.at[slot])
        copy.start()
        copies.append(copy)

    for x in range(4):
        fetch(time_links.at[0, x])
    for t in range(4):
        fetch(space_links.at[t, 0])
    for t in range(4):
        fetch(space_links.at[t, 1])
    me = place[0]
    shards, cap = lists.shape
    count = picks.shape[2]
    lane = lax.broadcasted_iota(jnp.int32, (MOST, cap), 1)
    want = lax.broadcasted_iota(jnp.int32, (MOST, cap), 0)
    column = lax.broadcasted_iota(jnp.int32, (MOST, count), 1)
    quarter = count // 4
    turned = (column // quarter % 2) * 2 * quarter + (column // (2 * quarter)) * quarter + column % quarter
    for shard in range(shards):
        mine = jnp.broadcast_to(lists[pl.ds(shard, 1), :], (MOST, cap))
        before = jnp.where((mine >= 0) & (mine < me * count), 1, 0)
        start = jnp.sum(before.astype(jnp.float32), axis=1, keepdims=True).astype(jnp.int32)
        inside = (mine >= me * count) & (mine < (me + 1) * count)
        match = inside & (lane - start == want)
        chosen = jnp.sum(jnp.where(match, mine - me * count + 1, 0).astype(jnp.float32), axis=1, keepdims=True)
        chosen = chosen.astype(jnp.int32) - 1
        picks[0, pl.ds(shard * MOST, MOST), :] = jnp.where(column == chosen, 1.0, 0.0)
        picks[1, pl.ds(shard * MOST, MOST), :] = jnp.where(turned == chosen, 1.0, 0.0)
    base.wait()
    for a_x in range(2):
        copies[2 * a_x].wait()
        copies[2 * a_x + 1].wait()
        for c in range(2):
            x = 2 * a_x + c
            image_item(links.at[x], vecs.at[1, x], vecs.at[2, x], c, left, right)
        time_rows[pl.ds(a_x * 8, 8), :] = group_rows(left[...], right[...], MAT_DIMS, vectors)
    for a_t in range(2):
        copies[4 + 2 * a_t].wait()
        copies[5 + 2 * a_t].wait()
        for c in range(2):
            t = 2 * a_t + c
            image_item(links.at[4 + t], vecs.at[t, 1], vecs.at[t, 2], c, left, right)
        space_rows[pl.ds(a_t * 8, 8), :] = group_rows(left[...], right[...], MAT_DIMS, vectors)
    for t in range(4):
        copies[8 + t].wait()
    for t in range(4):
        adjoint_item(links.at[8 + t], vecs.at[t, 3], t % 2, adjoint.at[t // 2])


def time_edge_kernel(nulls, edge, time_links, time_rows, links, vecs, left, right, sems):
    vectors = nulls.shape[-2]
    copies = []
    base = pltpu.make_async_copy(nulls.at[3], vecs, sems.at[4])
    base.start()
    for x in range(4):
        copy = pltpu.make_async_copy(time_links.at[1, x], links.at[x], sems.at[x])
        copy.start()
        copies.append(copy)
    base.wait()
    for a_x in range(2):
        copies[2 * a_x].wait()
        copies[2 * a_x + 1].wait()
        for c in range(2):
            x = 2 * a_x + c
            image_item(links.at[x], vecs.at[x], edge.at[0, x], c, left, right)
        time_rows[pl.ds(a_x * 8, 8), :] = group_rows(left[...], right[...], MAT_DIMS, vectors)


def final_kernel(edge, adjoint, picks, time_low, time_high, space_low, packed):
    sites, vectors, width = edge.shape[2:]
    aggs = sites // SIDE
    found = []
    for a_t in range(2):
        parts = []
        for c in range(2):
            for site in range(SIDE):
                rows = [edge[2 * a_t + c, 0, agg * SIDE + site] for agg in range(aggs)]
                parts.append(jnp.concatenate(rows, axis=0))
        found.append(group_rows(adjoint[a_t], jnp.concatenate(parts, axis=1), ROW_DIMS, vectors))
    time_rows = jnp.concatenate([time_low[...], time_high[...]], axis=0).astype(jnp.bfloat16)
    space_rows = jnp.concatenate([space_low[...]] + found, axis=0).astype(jnp.bfloat16)
    wide = time_rows.shape[1]
    packed[:, pl.ds(0, wide)] = dot(picks[0].astype(jnp.bfloat16), time_rows, MAT_DIMS).astype(jnp.bfloat16)
    packed[:, pl.ds(wide, wide)] = dot(picks[1].astype(jnp.bfloat16), space_rows, MAT_DIMS).astype(jnp.bfloat16)


def on_device(nulls, time_links, space_links, owner_lists):
    time_count, space_count, sites, vectors, width = nulls.shape
    shards, cap = owner_lists.shape
    aggs = sites // SIDE
    local_count = (time_count // 2) * (space_count // 2) * aggs
    wide = 2 * vectors * vectors
    place = lax.axis_index("xyz").astype(jnp.int32).reshape(1)
    vmem = pl.BlockSpec(memory_space=pltpu.VMEM)
    smem = pl.BlockSpec(memory_space=pltpu.SMEM)
    anywhere = pl.BlockSpec(memory_space=pl.ANY)
    outside = pl.BlockSpec(memory_space=pltpu.HBM)
    half = width // 2
    roomy = pltpu.CompilerParams(vmem_limit_bytes=54 * 1024 * 1024)
    middle = pltpu.CompilerParams(vmem_limit_bytes=52 * 1024 * 1024)
    modest = pltpu.CompilerParams(vmem_limit_bytes=24 * 1024 * 1024)
    grouped = [
        pltpu.VMEM((2 * vectors * aggs, 8 * width), jnp.bfloat16),
        pltpu.VMEM((8 * width, vectors * aggs), jnp.bfloat16),
    ]
    first = pltpu.CompilerParams(vmem_limit_bytes=52 * 1024 * 1024)
    space_edge, time_edge = pl.pallas_call(
        slice_kernel,
        in_specs=[outside],
        out_specs=[vmem] * 2,
        out_shape=[
            jax.ShapeDtypeStruct((time_count, 1, sites, vectors, width), nulls.dtype),
            jax.ShapeDtypeStruct((1, space_count, sites, vectors, width), nulls.dtype),
        ],
        scratch_shapes=[pltpu.SemaphoreType.DMA((2,))],
        compiler_params=first,
        cost_estimate=pl.CostEstimate(flops=1000, bytes_accessed=1000, transcendentals=0),
        name="slices",
    )(nulls)
    edge_time = shifted(time_edge, "ta", -1)
    edge_space = shifted(space_edge, "xyz", -1)
    time_low, space_low, adjoint, picks = pl.pallas_call(
        inner_kernel,
        in_specs=[smem, vmem, outside, outside, outside],
        out_specs=[vmem] * 4,
        out_shape=[
            jax.ShapeDtypeStruct((2 * aggs, wide), jnp.float32),
            jax.ShapeDtypeStruct((2 * aggs, wide), jnp.float32),
            jax.ShapeDtypeStruct((2, 2 * vectors * aggs, 8 * width), jnp.bfloat16),
            jax.ShapeDtypeStruct((2, shards * MOST, local_count), jnp.float32),
        ],
        scratch_shapes=[
            pltpu.VMEM((12, sites, half, width), jnp.bfloat16),
            pltpu.VMEM(nulls.shape, nulls.dtype),
        ]
        + grouped
        + [pltpu.SemaphoreType.DMA((13,))],
        compiler_params=roomy,
        cost_estimate=pl.CostEstimate(flops=1000, bytes_accessed=1000, transcendentals=0),
        name="inner",
    )(place, owner_lists, nulls, time_links, space_links)
    time_high = pl.pallas_call(
        time_edge_kernel,
        in_specs=[outside, vmem, outside],
        out_specs=vmem,
        out_shape=jax.ShapeDtypeStruct((2 * aggs, wide), jnp.float32),
        scratch_shapes=[
            pltpu.VMEM((4, sites, half, width), jnp.bfloat16),
            pltpu.VMEM(nulls.shape[1:], nulls.dtype),
        ]
        + grouped
        + [pltpu.SemaphoreType.DMA((5,))],
        compiler_params=middle,
        cost_estimate=pl.CostEstimate(flops=1000, bytes_accessed=1000, transcendentals=0),
        name="time_edge",
    )(nulls, edge_time, time_links)
    packed = pl.pallas_call(
        final_kernel,
        in_specs=[vmem] * 6,
        out_specs=vmem,
        out_shape=jax.ShapeDtypeStruct((shards * MOST, 2 * wide), jnp.bfloat16),
        compiler_params=modest,
        cost_estimate=pl.CostEstimate(flops=1000, bytes_accessed=1000, transcendentals=0),
        name="final",
    )(edge_space, adjoint, picks, time_low, time_high, space_low)
    arrived = lax.all_to_all(packed, "xyz", 0, 0, tiled=True)
    if shards * MOST == cap:
        result = arrived.astype(jnp.float32)
    else:
        my_list = lax.dynamic_index_in_dim(owner_lists, lax.axis_index("xyz"), 0, keepdims=False)
        source = jnp.maximum(my_list, 0) // local_count
        order = jnp.arange(cap, dtype=jnp.int32)
        same = (source[:, None] == source[None, :]) & (order[None, :] < order[:, None])
        offset = jnp.sum(same.astype(jnp.int32), axis=1)
        picked = arrived[source * MOST + offset].astype(jnp.float32)
        result = jnp.where((my_list >= 0)[:, None], picked, 0.0)
    return result[None]


def solution(mesh):
    return jax.shard_map(
        on_device,
        mesh=mesh,
        in_specs=(
            P("ta", "xyz", None, None, None),
            P("ta", "xyz", None, None, None),
            P("ta", "xyz", None, None, None),
            P(),
        ),
        out_specs=P("ta", "xyz", None),
        check_vma=False,
    )
```

```python
import jax
import jax.numpy as jnp
from jax import lax
from jax.experimental import pallas as pl
from jax.experimental.pallas import tpu as pltpu
from jax.sharding import PartitionSpec as P

ROW_DIMS = (((1,), (1,)), ((), ()))
MAT_DIMS = (((1,), (0,)), ((), ()))
SIDE = 4
MOST = 8


def shifted(array, axis, by):
    count = lax.axis_size(axis)
    return lax.ppermute(array, axis, [(i, (i + by) % count) for i in range(count)])


def dot(left, right, dims):
    return lax.dot_general(left, right, dims, preferred_element_type=jnp.float32)


def swapped(array):
    return pltpu.roll(array, array.shape[-1] // 2, axis=array.ndim - 1)


def lower_half(shape):
    return lax.broadcasted_iota(jnp.int32, shape, len(shape) - 1) < shape[-1] // 2


def signs(shape, dtype):
    return jnp.where(lower_half(shape), 1.0, -1.0).astype(dtype)


def image_item(links, lower, upper, slot, left_ref, right_ref):
    sites, vectors, width = lower.shape
    half = width // 2
    aggs = sites // SIDE
    sign = signs((vectors, width), jnp.bfloat16)
    zero = jnp.zeros((vectors, width), jnp.bfloat16)
    owner = lax.broadcasted_iota(jnp.int32, (half, 2 * aggs * vectors), 1) // (2 * vectors) % (aggs // 2)
    for part in range(SIDE):
        at = (slot * SIDE + part) * width
        mats = []
        plain, crossed = [], []
        for agg in range(aggs):
            site = agg * SIDE + part
            up = upper[site]
            pair = (up * sign, swapped(up))
            for rows, value in zip((plain, crossed), pair):
                rows.append(jnp.concatenate([value, zero] if agg % 2 == 0 else [zero, value], axis=1))
            if agg % 2 == 0:
                mats.append(jnp.concatenate([links[site], links[site + SIDE]], axis=1))
            low = lower[site]
            left_ref[pl.ds(agg * 2 * vectors, 2 * vectors), pl.ds(at, width)] = jnp.concatenate(
                [low, -sign * swapped(low)], axis=0
            )
        images = dot(jnp.concatenate(mats, axis=0), jnp.concatenate(plain + crossed, axis=0), ROW_DIMS)
        own = images[:half]
        for pair in range(1, aggs // 2):
            own = jnp.where(owner == pair, images[pair * half : (pair + 1) * half], own)
        own = own.astype(jnp.bfloat16)
        right_ref[pl.ds(at, half), :] = own[:, : aggs * vectors]
        right_ref[pl.ds(at + half, half), :] = own[:, aggs * vectors :]


def adjoint_item(links, lower, slot, left_ref):
    sites, vectors, width = lower.shape
    half = width // 2
    low = lower_half((vectors, width))
    sign = signs((vectors, width), jnp.float32)
    zero = jnp.zeros((vectors, width), jnp.bfloat16)
    for agg in range(sites // SIDE):
        rows = []
        mats = []
        for pair in range(SIDE // 2):
            at = agg * SIDE + 2 * pair
            lo_a, lo_b = lower[at], lower[at + 1]
            rows += [
                jnp.where(low, lo_a, zero),
                jnp.where(low, swapped(lo_a), zero),
                jnp.where(low, zero, swapped(lo_b)),
                jnp.where(low, zero, lo_b),
            ]
            mats.append(jnp.concatenate([links[at], links[at + 1]], axis=0))
        prod = dot(jnp.concatenate(rows, axis=0), jnp.concatenate(mats, axis=1), MAT_DIMS)
        for part in range(SIDE):
            top = part * 2 * vectors
            mine = prod[top : top + 2 * vectors, part // 2 * width : (part // 2 + 1) * width]
            adj = sign * mine[:vectors] + swapped(mine[vectors:])
            both = jnp.concatenate([adj, -sign * swapped(adj)], axis=0).astype(jnp.bfloat16)
            left_ref[pl.ds(agg * 2 * vectors, 2 * vectors), pl.ds((slot * SIDE + part) * width, width)] = both


def group_rows(left, right, dims, vectors):
    full = dot(left, right, dims)
    aggs = full.shape[1] // vectors
    lanes = lax.broadcasted_iota(jnp.int32, (2 * vectors, full.shape[1]), 1) // vectors
    own = jnp.zeros((2 * vectors, full.shape[1]), jnp.float32)
    for agg in range(aggs):
        own = jnp.where(lanes == agg, full[agg * 2 * vectors : (agg + 1) * 2 * vectors], own)
    pieces = []
    lane_group = lax.broadcasted_iota(jnp.int32, (aggs, full.shape[1]), 1) // vectors
    sub = lax.broadcasted_iota(jnp.int32, (aggs, full.shape[1]), 0)
    total = full.shape[1]
    for piece in range(2 * vectors // aggs):
        value = own[piece * aggs : (piece + 1) * aggs]
        step = 1
        while step < aggs:
            sub_bit = (sub // step) % 2
            lane_bit = (lane_group // step) % 2
            up = pltpu.roll(pltpu.roll(value, aggs - step, axis=0), step * vectors, axis=1)
            down = pltpu.roll(pltpu.roll(value, step, axis=0), total - step * vectors, axis=1)
            value = jnp.where(sub_bit == lane_bit, value, jnp.where(sub_bit == 0, up, down))
            step *= 2
        pieces.append(value)
    return jnp.concatenate(pieces, axis=1)


def slice_kernel(nulls, space_edge, time_edge, sems):
    copies = [
        pltpu.make_async_copy(nulls.at[:, pl.ds(0, 1)], space_edge, sems.at[0]),
        pltpu.make_async_copy(nulls.at[pl.ds(0, 1)], time_edge, sems.at[1]),
    ]
    for copy in copies:
        copy.start()
    for copy in copies:
        copy.wait()


def inner_kernel(place, lists, nulls, time_links, space_links, time_rows, space_rows, adjoint, picks, links, vecs, left, right, sems):
    time_count, space_count, sites, vectors, width = nulls.shape
    copies = []
    base = pltpu.make_async_copy(nulls, vecs, sems.at[12])
    base.start()

    def fetch(source):
        slot = len(copies)
        copy = pltpu.make_async_copy(source, links.at[slot], sems.at[slot])
        copy.start()
        copies.append(copy)

    for x in range(4):
        fetch(time_links.at[0, x])
    for t in range(4):
        fetch(space_links.at[t, 0])
    for t in range(4):
        fetch(space_links.at[t, 1])
    me = place[0]
    shards, cap = lists.shape
    count = picks.shape[2]
    lane = lax.broadcasted_iota(jnp.int32, (MOST, cap), 1)
    want = lax.broadcasted_iota(jnp.int32, (MOST, cap), 0)
    column = lax.broadcasted_iota(jnp.int32, (MOST, count), 1)
    quarter = count // 4
    turned = (column // quarter % 2) * 2 * quarter + (column // (2 * quarter)) * quarter + column % quarter
    for shard in range(shards):
        mine = jnp.broadcast_to(lists[pl.ds(jnp.bitwise_xor(me, shard), 1), :], (MOST, cap))
        before = jnp.where((mine >= 0) & (mine < me * count), 1, 0)
        start = jnp.sum(before.astype(jnp.float32), axis=1, keepdims=True).astype(jnp.int32)
        inside = (mine >= me * count) & (mine < (me + 1) * count)
        match = inside & (lane - start == want)
        chosen = jnp.sum(jnp.where(match, mine - me * count + 1, 0).astype(jnp.float32), axis=1, keepdims=True)
        chosen = chosen.astype(jnp.int32) - 1
        picks[0, pl.ds(shard * MOST, MOST), :] = jnp.where(column == chosen, 1.0, 0.0)
        picks[1, pl.ds(shard * MOST, MOST), :] = jnp.where(turned == chosen, 1.0, 0.0)
    base.wait()
    for a_x in range(2):
        copies[2 * a_x].wait()
        copies[2 * a_x + 1].wait()
        for c in range(2):
            x = 2 * a_x + c
            image_item(links.at[x], vecs.at[1, x], vecs.at[2, x], c, left, right)
        time_rows[pl.ds(a_x * 8, 8), :] = group_rows(left[...], right[...], MAT_DIMS, vectors)
    for a_t in range(2):
        copies[4 + 2 * a_t].wait()
        copies[5 + 2 * a_t].wait()
        for c in range(2):
            t = 2 * a_t + c
            image_item(links.at[4 + t], vecs.at[t, 1], vecs.at[t, 2], c, left, right)
        space_rows[pl.ds(a_t * 8, 8), :] = group_rows(left[...], right[...], MAT_DIMS, vectors)
    for t in range(4):
        copies[8 + t].wait()
    for t in range(4):
        adjoint_item(links.at[8 + t], vecs.at[t, 3], t % 2, adjoint.at[t // 2])


def time_edge_kernel(nulls, edge, time_links, time_rows, links, vecs, left, right, sems):
    vectors = nulls.shape[-2]
    copies = []
    base = pltpu.make_async_copy(nulls.at[3], vecs, sems.at[4])
    base.start()
    for x in range(4):
        copy = pltpu.make_async_copy(time_links.at[1, x], links.at[x], sems.at[x])
        copy.start()
        copies.append(copy)
    base.wait()
    for a_x in range(2):
        copies[2 * a_x].wait()
        copies[2 * a_x + 1].wait()
        for c in range(2):
            x = 2 * a_x + c
            image_item(links.at[x], vecs.at[x], edge.at[0, x], c, left, right)
        time_rows[pl.ds(a_x * 8, 8), :] = group_rows(left[...], right[...], MAT_DIMS, vectors)


def final_kernel(edge, adjoint, picks, time_low, time_high, space_low, *packed):
    sites, vectors, width = edge.shape[2:]
    aggs = sites // SIDE
    found = []
    for a_t in range(2):
        parts = []
        for c in range(2):
            for site in range(SIDE):
                rows = [edge[2 * a_t + c, 0, agg * SIDE + site] for agg in range(aggs)]
                parts.append(jnp.concatenate(rows, axis=0))
        found.append(group_rows(adjoint[a_t], jnp.concatenate(parts, axis=1), ROW_DIMS, vectors))
    time_rows = jnp.concatenate([time_low[...], time_high[...]], axis=0).astype(jnp.bfloat16)
    space_rows = jnp.concatenate([space_low[...]] + found, axis=0).astype(jnp.bfloat16)
    time_sent = dot(picks[0].astype(jnp.bfloat16), time_rows, MAT_DIMS)
    space_sent = dot(picks[1].astype(jnp.bfloat16), space_rows, MAT_DIMS)
    for turn, out in enumerate(packed):
        mine = slice(turn * MOST, (turn + 1) * MOST)
        out[...] = jnp.concatenate([time_sent[mine], space_sent[mine]], axis=1).astype(jnp.bfloat16)


def unpack_kernel(place, *refs):
    me = place[0]
    result = refs[-1]
    for turn, arrived in enumerate(refs[-2::-1]):
        source = jnp.bitwise_xor(me, turn)
        result[pl.ds(pl.multiple_of(source * MOST, MOST), MOST), :] = arrived[...].astype(jnp.float32)


def on_device(nulls, time_links, space_links, owner_lists):
    time_count, space_count, sites, vectors, width = nulls.shape
    shards, cap = owner_lists.shape
    aggs = sites // SIDE
    local_count = (time_count // 2) * (space_count // 2) * aggs
    wide = 2 * vectors * vectors
    place = lax.axis_index("xyz").astype(jnp.int32).reshape(1)
    vmem = pl.BlockSpec(memory_space=pltpu.VMEM)
    smem = pl.BlockSpec(memory_space=pltpu.SMEM)
    anywhere = pl.BlockSpec(memory_space=pl.ANY)
    outside = pl.BlockSpec(memory_space=pltpu.HBM)
    half = width // 2
    roomy = pltpu.CompilerParams(vmem_limit_bytes=54 * 1024 * 1024)
    middle = pltpu.CompilerParams(vmem_limit_bytes=52 * 1024 * 1024)
    modest = pltpu.CompilerParams(vmem_limit_bytes=24 * 1024 * 1024)
    grouped = [
        pltpu.VMEM((2 * vectors * aggs, 8 * width), jnp.bfloat16),
        pltpu.VMEM((8 * width, vectors * aggs), jnp.bfloat16),
    ]
    first = pltpu.CompilerParams(vmem_limit_bytes=52 * 1024 * 1024)
    space_edge, time_edge = pl.pallas_call(
        slice_kernel,
        in_specs=[outside],
        out_specs=[vmem] * 2,
        out_shape=[
            jax.ShapeDtypeStruct((time_count, 1, sites, vectors, width), nulls.dtype),
            jax.ShapeDtypeStruct((1, space_count, sites, vectors, width), nulls.dtype),
        ],
        scratch_shapes=[pltpu.SemaphoreType.DMA((2,))],
        compiler_params=first,
        cost_estimate=pl.CostEstimate(flops=1000, bytes_accessed=1000, transcendentals=0),
        name="slices",
    )(nulls)
    edge_time = shifted(time_edge, "ta", -1)
    edge_space = shifted(space_edge, "xyz", -1)
    time_low, space_low, adjoint, picks = pl.pallas_call(
        inner_kernel,
        in_specs=[smem, vmem, outside, outside, outside],
        out_specs=[vmem] * 4,
        out_shape=[
            jax.ShapeDtypeStruct((2 * aggs, wide), jnp.float32),
            jax.ShapeDtypeStruct((2 * aggs, wide), jnp.float32),
            jax.ShapeDtypeStruct((2, 2 * vectors * aggs, 8 * width), jnp.bfloat16),
            jax.ShapeDtypeStruct((2, shards * MOST, local_count), jnp.float32),
        ],
        scratch_shapes=[
            pltpu.VMEM((12, sites, half, width), jnp.bfloat16),
            pltpu.VMEM(nulls.shape, nulls.dtype),
        ]
        + grouped
        + [pltpu.SemaphoreType.DMA((13,))],
        compiler_params=roomy,
        cost_estimate=pl.CostEstimate(flops=1000, bytes_accessed=1000, transcendentals=0),
        name="inner",
    )(place, owner_lists, nulls, time_links, space_links)
    time_high = pl.pallas_call(
        time_edge_kernel,
        in_specs=[outside, vmem, outside],
        out_specs=vmem,
        out_shape=jax.ShapeDtypeStruct((2 * aggs, wide), jnp.float32),
        scratch_shapes=[
            pltpu.VMEM((4, sites, half, width), jnp.bfloat16),
            pltpu.VMEM(nulls.shape[1:], nulls.dtype),
        ]
        + grouped
        + [pltpu.SemaphoreType.DMA((5,))],
        compiler_params=middle,
        cost_estimate=pl.CostEstimate(flops=1000, bytes_accessed=1000, transcendentals=0),
        name="time_edge",
    )(nulls, edge_time, time_links)
    packed = pl.pallas_call(
        final_kernel,
        in_specs=[vmem] * 6,
        out_specs=[vmem] * shards,
        out_shape=[jax.ShapeDtypeStruct((MOST, 2 * wide), jnp.bfloat16)] * shards,
        compiler_params=modest,
        cost_estimate=pl.CostEstimate(flops=1000, bytes_accessed=1000, transcendentals=0),
        name="final",
    )(edge_space, adjoint, picks, time_low, time_high, space_low)
    turns = range(shards - 1, 0, -1)
    arrived = [lax.ppermute(packed[turn], "xyz", [(i, i ^ turn) for i in range(shards)]) for turn in turns]
    arrived.append(packed[0])
    arrived = pl.pallas_call(
        unpack_kernel,
        in_specs=[smem] + [vmem] * shards,
        out_specs=vmem,
        out_shape=jax.ShapeDtypeStruct((shards * MOST, 2 * wide), jnp.float32),
        compiler_params=modest,
        cost_estimate=pl.CostEstimate(flops=1000, bytes_accessed=1000, transcendentals=0),
        name="unpack",
    )(place, *arrived)
    if shards * MOST == cap:
        result = arrived
    else:
        my_list = lax.dynamic_index_in_dim(owner_lists, lax.axis_index("xyz"), 0, keepdims=False)
        source = jnp.maximum(my_list, 0) // local_count
        order = jnp.arange(cap, dtype=jnp.int32)
        same = (source[:, None] == source[None, :]) & (order[None, :] < order[:, None])
        offset = jnp.sum(same.astype(jnp.int32), axis=1)
        picked = arrived[source * MOST + offset]
        result = jnp.where((my_list >= 0)[:, None], picked, 0.0)
    return result[None]


def solution(mesh):
    return jax.shard_map(
        on_device,
        mesh=mesh,
        in_specs=(
            P("ta", "xyz", None, None, None),
            P("ta", "xyz", None, None, None),
            P("ta", "xyz", None, None, None),
            P(),
        ),
        out_specs=P("ta", "xyz", None),
        check_vma=False,
    )
```

```python
import jax
import jax.numpy as jnp
from jax import lax
from jax.experimental import pallas as pl
from jax.experimental.pallas import tpu as pltpu
from jax.sharding import PartitionSpec as P

ROW_DIMS = (((1,), (1,)), ((), ()))
MAT_DIMS = (((1,), (0,)), ((), ()))
SIDE = 4
MOST = 8


def shifted(array, axis, by):
    count = lax.axis_size(axis)
    return lax.ppermute(array, axis, [(i, (i + by) % count) for i in range(count)])


def crossed(array, axis, bits):
    return lax.ppermute(array, axis, [(i, i ^ bits) for i in range(lax.axis_size(axis))])


def dot(left, right, dims):
    return lax.dot_general(left, right, dims, preferred_element_type=jnp.float32)


def swapped(array):
    return pltpu.roll(array, array.shape[-1] // 2, axis=array.ndim - 1)


def lower_half(shape):
    return lax.broadcasted_iota(jnp.int32, shape, len(shape) - 1) < shape[-1] // 2


def signs(shape, dtype):
    return jnp.where(lower_half(shape), 1.0, -1.0).astype(dtype)


def image_item(links, lower, upper, slot, left_ref, right_ref):
    sites, vectors, width = lower.shape
    half = width // 2
    aggs = sites // SIDE
    sign = signs((vectors, width), jnp.bfloat16)
    zero = jnp.zeros((vectors, width), jnp.bfloat16)
    owner = lax.broadcasted_iota(jnp.int32, (half, 2 * aggs * vectors), 1) // (2 * vectors) % (aggs // 2)
    for part in range(SIDE):
        at = (slot * SIDE + part) * width
        mats = []
        plain, crossed = [], []
        for agg in range(aggs):
            site = agg * SIDE + part
            up = upper[site]
            pair = (up * sign, swapped(up))
            for rows, value in zip((plain, crossed), pair):
                rows.append(jnp.concatenate([value, zero] if agg % 2 == 0 else [zero, value], axis=1))
            if agg % 2 == 0:
                mats.append(jnp.concatenate([links[site], links[site + SIDE]], axis=1))
            low = lower[site]
            left_ref[pl.ds(agg * 2 * vectors, 2 * vectors), pl.ds(at, width)] = jnp.concatenate(
                [low, -sign * swapped(low)], axis=0
            )
        images = dot(jnp.concatenate(mats, axis=0), jnp.concatenate(plain + crossed, axis=0), ROW_DIMS)
        own = images[:half]
        for pair in range(1, aggs // 2):
            own = jnp.where(owner == pair, images[pair * half : (pair + 1) * half], own)
        own = own.astype(jnp.bfloat16)
        right_ref[pl.ds(at, half), :] = own[:, : aggs * vectors]
        right_ref[pl.ds(at + half, half), :] = own[:, aggs * vectors :]


def adjoint_item(links, lower, slot, left_ref):
    sites, vectors, width = lower.shape
    half = width // 2
    low = lower_half((vectors, width))
    sign = signs((vectors, width), jnp.float32)
    zero = jnp.zeros((vectors, width), jnp.bfloat16)
    for agg in range(sites // SIDE):
        rows = []
        mats = []
        for pair in range(SIDE // 2):
            at = agg * SIDE + 2 * pair
            lo_a, lo_b = lower[at], lower[at + 1]
            rows += [
                jnp.where(low, lo_a, zero),
                jnp.where(low, swapped(lo_a), zero),
                jnp.where(low, zero, swapped(lo_b)),
                jnp.where(low, zero, lo_b),
            ]
            mats.append(jnp.concatenate([links[at], links[at + 1]], axis=0))
        prod = dot(jnp.concatenate(rows, axis=0), jnp.concatenate(mats, axis=1), MAT_DIMS)
        for part in range(SIDE):
            top = part * 2 * vectors
            mine = prod[top : top + 2 * vectors, part // 2 * width : (part // 2 + 1) * width]
            adj = sign * mine[:vectors] + swapped(mine[vectors:])
            both = jnp.concatenate([adj, -sign * swapped(adj)], axis=0).astype(jnp.bfloat16)
            left_ref[pl.ds(agg * 2 * vectors, 2 * vectors), pl.ds((slot * SIDE + part) * width, width)] = both


def group_rows(left, right, dims, vectors):
    full = dot(left, right, dims)
    aggs = full.shape[1] // vectors
    lanes = lax.broadcasted_iota(jnp.int32, (2 * vectors, full.shape[1]), 1) // vectors
    own = jnp.zeros((2 * vectors, full.shape[1]), jnp.float32)
    for agg in range(aggs):
        own = jnp.where(lanes == agg, full[agg * 2 * vectors : (agg + 1) * 2 * vectors], own)
    pieces = []
    lane_group = lax.broadcasted_iota(jnp.int32, (aggs, full.shape[1]), 1) // vectors
    sub = lax.broadcasted_iota(jnp.int32, (aggs, full.shape[1]), 0)
    total = full.shape[1]
    for piece in range(2 * vectors // aggs):
        value = own[piece * aggs : (piece + 1) * aggs]
        step = 1
        while step < aggs:
            sub_bit = (sub // step) % 2
            lane_bit = (lane_group // step) % 2
            up = pltpu.roll(pltpu.roll(value, aggs - step, axis=0), step * vectors, axis=1)
            down = pltpu.roll(pltpu.roll(value, step, axis=0), total - step * vectors, axis=1)
            value = jnp.where(sub_bit == lane_bit, value, jnp.where(sub_bit == 0, up, down))
            step *= 2
        pieces.append(value)
    return jnp.concatenate(pieces, axis=1)


def slice_kernel(nulls, space_edge, time_edge, sems):
    copies = [
        pltpu.make_async_copy(nulls.at[:, pl.ds(0, 1)], space_edge, sems.at[0]),
        pltpu.make_async_copy(nulls.at[pl.ds(0, 1)], time_edge, sems.at[1]),
    ]
    for copy in copies:
        copy.start()
    for copy in copies:
        copy.wait()


def inner_kernel(place, lists, nulls, time_links, space_links, time_rows, space_rows, adjoint, picks, links, vecs, left, right, sems):
    time_count, space_count, sites, vectors, width = nulls.shape
    copies = []
    base = pltpu.make_async_copy(nulls, vecs, sems.at[12])
    base.start()

    def fetch(source):
        slot = len(copies)
        copy = pltpu.make_async_copy(source, links.at[slot], sems.at[slot])
        copy.start()
        copies.append(copy)

    for x in range(4):
        fetch(time_links.at[0, x])
    for t in range(4):
        fetch(space_links.at[t, 0])
    for t in range(4):
        fetch(space_links.at[t, 1])
    me = place[0]
    shards, cap = lists.shape
    count = picks.shape[2] // 2
    lane = lax.broadcasted_iota(jnp.int32, (MOST, cap), 1)
    want = lax.broadcasted_iota(jnp.int32, (MOST, cap), 0)
    column = lax.broadcasted_iota(jnp.int32, (MOST, 2 * count), 1)
    quarter = count // 4
    inside = column % count
    turned = (inside // quarter % 2) * 2 * quarter + (inside // (2 * quarter)) * quarter + inside % quarter
    own_column = column < count
    side = lax.rem(me, 2)
    for turn in range(shards // 2):
        owner = 2 * jnp.bitwise_xor(me // 2, turn) + side
        mine = jnp.broadcast_to(lists[pl.ds(owner, 1), :], (MOST, cap))
        for parity in range(2):
            source = me - side + parity
            before = jnp.where((mine >= 0) & (mine < source * count), 1, 0)
            start = jnp.sum(before.astype(jnp.float32), axis=1, keepdims=True).astype(jnp.int32)
            match = (mine >= source * count) & (mine < (source + 1) * count) & (lane - start == want)
            chosen = jnp.sum(jnp.where(match, mine - source * count + 1, 0).astype(jnp.float32), axis=1, keepdims=True)
            chosen = chosen.astype(jnp.int32) - 1
            here = own_column == (side == parity)
            rows = pl.ds((2 * turn + parity) * MOST, MOST)
            picks[0, rows, :] = jnp.where(here & (inside == chosen), 1.0, 0.0)
            picks[1, rows, :] = jnp.where(here & (turned == chosen), 1.0, 0.0)
    base.wait()
    for a_x in range(2):
        copies[2 * a_x].wait()
        copies[2 * a_x + 1].wait()
        for c in range(2):
            x = 2 * a_x + c
            image_item(links.at[x], vecs.at[1, x], vecs.at[2, x], c, left, right)
        time_rows[pl.ds(a_x * 8, 8), :] = group_rows(left[...], right[...], MAT_DIMS, vectors)
    for a_t in range(2):
        copies[4 + 2 * a_t].wait()
        copies[5 + 2 * a_t].wait()
        for c in range(2):
            t = 2 * a_t + c
            image_item(links.at[4 + t], vecs.at[t, 1], vecs.at[t, 2], c, left, right)
        space_rows[pl.ds(a_t * 8, 8), :] = group_rows(left[...], right[...], MAT_DIMS, vectors)
    for t in range(4):
        copies[8 + t].wait()
    for t in range(4):
        adjoint_item(links.at[8 + t], vecs.at[t, 3], t % 2, adjoint.at[t // 2])


def time_edge_kernel(nulls, edge, time_links, time_low, space_low, early, links, vecs, left, right, sems):
    vectors = nulls.shape[-2]
    copies = []
    base = pltpu.make_async_copy(nulls.at[3], vecs, sems.at[4])
    base.start()
    for x in range(4):
        copy = pltpu.make_async_copy(time_links.at[1, x], links.at[x], sems.at[x])
        copy.start()
        copies.append(copy)
    base.wait()
    found = []
    for a_x in range(2):
        copies[2 * a_x].wait()
        copies[2 * a_x + 1].wait()
        for c in range(2):
            x = 2 * a_x + c
            image_item(links.at[x], vecs.at[x], edge.at[0, x], c, left, right)
        found.append(group_rows(left[...], right[...], MAT_DIMS, vectors))
    early[...] = jnp.concatenate([time_low[...]] + found + [space_low[...]], axis=0).astype(jnp.bfloat16)


def final_kernel(edge, adjoint, late):
    sites, vectors, width = edge.shape[2:]
    aggs = sites // SIDE
    found = []
    for a_t in range(2):
        parts = []
        for c in range(2):
            for site in range(SIDE):
                rows = [edge[2 * a_t + c, 0, agg * SIDE + site] for agg in range(aggs)]
                parts.append(jnp.concatenate(rows, axis=0))
        found.append(group_rows(adjoint[a_t], jnp.concatenate(parts, axis=1), ROW_DIMS, vectors))
    late[...] = jnp.concatenate(found, axis=0).astype(jnp.bfloat16)


def pack_kernel(picks, early, early_other, late, late_other, *packed):
    half_count = late.shape[0]
    count = 2 * half_count
    time_rows = jnp.concatenate([early[pl.ds(0, count), :], early_other[pl.ds(0, count), :]], axis=0)
    space_rows = jnp.concatenate(
        [early[pl.ds(count, half_count), :], late[...], early_other[pl.ds(count, half_count), :], late_other[...]],
        axis=0,
    )
    time_sent = dot(picks[0].astype(jnp.bfloat16), time_rows, MAT_DIMS)
    space_sent = dot(picks[1].astype(jnp.bfloat16), space_rows, MAT_DIMS)
    for turn, out in enumerate(packed):
        mine = slice(turn * 2 * MOST, (turn + 1) * 2 * MOST)
        out[...] = jnp.concatenate([time_sent[mine], space_sent[mine]], axis=1).astype(jnp.bfloat16)


def unpack_kernel(place, *refs):
    pair = place[0] // 2
    result = refs[-1]
    for turn, arrived in enumerate(refs[-2::-1]):
        source = jnp.bitwise_xor(pair, turn)
        result[pl.ds(pl.multiple_of(source * 2 * MOST, 2 * MOST), 2 * MOST), :] = arrived[...].astype(jnp.float32)


def on_device(nulls, time_links, space_links, owner_lists):
    time_count, space_count, sites, vectors, width = nulls.shape
    shards, cap = owner_lists.shape
    aggs = sites // SIDE
    local_count = (time_count // 2) * (space_count // 2) * aggs
    wide = 2 * vectors * vectors
    place = lax.axis_index("xyz").astype(jnp.int32).reshape(1)
    vmem = pl.BlockSpec(memory_space=pltpu.VMEM)
    smem = pl.BlockSpec(memory_space=pltpu.SMEM)
    anywhere = pl.BlockSpec(memory_space=pl.ANY)
    outside = pl.BlockSpec(memory_space=pltpu.HBM)
    half = width // 2
    roomy = pltpu.CompilerParams(vmem_limit_bytes=54 * 1024 * 1024)
    middle = pltpu.CompilerParams(vmem_limit_bytes=52 * 1024 * 1024)
    modest = pltpu.CompilerParams(vmem_limit_bytes=24 * 1024 * 1024)
    grouped = [
        pltpu.VMEM((2 * vectors * aggs, 8 * width), jnp.bfloat16),
        pltpu.VMEM((8 * width, vectors * aggs), jnp.bfloat16),
    ]
    first = pltpu.CompilerParams(vmem_limit_bytes=52 * 1024 * 1024)
    space_edge, time_edge = pl.pallas_call(
        slice_kernel,
        in_specs=[outside],
        out_specs=[vmem] * 2,
        out_shape=[
            jax.ShapeDtypeStruct((time_count, 1, sites, vectors, width), nulls.dtype),
            jax.ShapeDtypeStruct((1, space_count, sites, vectors, width), nulls.dtype),
        ],
        scratch_shapes=[pltpu.SemaphoreType.DMA((2,))],
        compiler_params=first,
        cost_estimate=pl.CostEstimate(flops=1000, bytes_accessed=1000, transcendentals=0),
        name="slices",
    )(nulls)
    edge_time = shifted(time_edge, "ta", -1)
    edge_space = shifted(space_edge, "xyz", -1)
    time_low, space_low, adjoint, picks = pl.pallas_call(
        inner_kernel,
        in_specs=[smem, vmem, outside, outside, outside],
        out_specs=[vmem] * 4,
        out_shape=[
            jax.ShapeDtypeStruct((2 * aggs, wide), jnp.float32),
            jax.ShapeDtypeStruct((2 * aggs, wide), jnp.float32),
            jax.ShapeDtypeStruct((2, 2 * vectors * aggs, 8 * width), jnp.bfloat16),
            jax.ShapeDtypeStruct((2, shards * MOST, 2 * local_count), jnp.float32),
        ],
        scratch_shapes=[
            pltpu.VMEM((12, sites, half, width), jnp.bfloat16),
            pltpu.VMEM(nulls.shape, nulls.dtype),
        ]
        + grouped
        + [pltpu.SemaphoreType.DMA((13,))],
        compiler_params=roomy,
        cost_estimate=pl.CostEstimate(flops=1000, bytes_accessed=1000, transcendentals=0),
        name="inner",
    )(place, owner_lists, nulls, time_links, space_links)
    early = pl.pallas_call(
        time_edge_kernel,
        in_specs=[outside, vmem, outside, vmem, vmem],
        out_specs=vmem,
        out_shape=jax.ShapeDtypeStruct((6 * aggs, wide), jnp.bfloat16),
        scratch_shapes=[
            pltpu.VMEM((4, sites, half, width), jnp.bfloat16),
            pltpu.VMEM(nulls.shape[1:], nulls.dtype),
        ]
        + grouped
        + [pltpu.SemaphoreType.DMA((5,))],
        compiler_params=middle,
        cost_estimate=pl.CostEstimate(flops=1000, bytes_accessed=1000, transcendentals=0),
        name="time_edge",
    )(nulls, edge_time, time_links, time_low, space_low)
    late = pl.pallas_call(
        final_kernel,
        in_specs=[vmem] * 2,
        out_specs=vmem,
        out_shape=jax.ShapeDtypeStruct((2 * aggs, wide), jnp.bfloat16),
        compiler_params=modest,
        cost_estimate=pl.CostEstimate(flops=1000, bytes_accessed=1000, transcendentals=0),
        name="final",
    )(edge_space, adjoint)
    early_other = crossed(early, "xyz", 1)
    late_other = crossed(late, "xyz", 1)
    pairs = shards // 2
    packed = pl.pallas_call(
        pack_kernel,
        in_specs=[vmem] * 5,
        out_specs=[vmem] * pairs,
        out_shape=[jax.ShapeDtypeStruct((2 * MOST, 2 * wide), jnp.bfloat16)] * pairs,
        compiler_params=modest,
        cost_estimate=pl.CostEstimate(flops=1000, bytes_accessed=1000, transcendentals=0),
        name="pack",
    )(picks, early, early_other, late, late_other)
    arrived = [crossed(packed[turn], "xyz", 2 * turn) for turn in range(pairs - 1, 0, -1)]
    arrived.append(packed[0])
    arrived = pl.pallas_call(
        unpack_kernel,
        in_specs=[smem] + [vmem] * pairs,
        out_specs=vmem,
        out_shape=jax.ShapeDtypeStruct((shards * MOST, 2 * wide), jnp.float32),
        compiler_params=modest,
        cost_estimate=pl.CostEstimate(flops=1000, bytes_accessed=1000, transcendentals=0),
        name="unpack",
    )(place, *arrived)
    if shards * MOST == cap:
        result = arrived
    else:
        my_list = lax.dynamic_index_in_dim(owner_lists, lax.axis_index("xyz"), 0, keepdims=False)
        source = jnp.maximum(my_list, 0) // local_count
        order = jnp.arange(cap, dtype=jnp.int32)
        same = (source[:, None] == source[None, :]) & (order[None, :] < order[:, None])
        offset = jnp.sum(same.astype(jnp.int32), axis=1)
        picked = arrived[source * MOST + offset]
        result = jnp.where((my_list >= 0)[:, None], picked, 0.0)
    return result[None]


def solution(mesh):
    return jax.shard_map(
        on_device,
        mesh=mesh,
        in_specs=(
            P("ta", "xyz", None, None, None),
            P("ta", "xyz", None, None, None),
            P("ta", "xyz", None, None, None),
            P(),
        ),
        out_specs=P("ta", "xyz", None),
        check_vma=False,
    )
```

```python
import jax
import jax.numpy as jnp
from jax import lax
from jax.experimental import pallas as pl
from jax.experimental.pallas import tpu as pltpu
from jax.sharding import PartitionSpec as P

ROW_DIMS = (((1,), (1,)), ((), ()))
MAT_DIMS = (((1,), (0,)), ((), ()))
SIDE = 4
MOST = 8


def shifted(array, axis, by):
    count = lax.axis_size(axis)
    return lax.ppermute(array, axis, [(i, (i + by) % count) for i in range(count)])


def crossed(array, axis, bits):
    return lax.ppermute(array, axis, [(i, i ^ bits) for i in range(lax.axis_size(axis))])


def dot(left, right, dims):
    return lax.dot_general(left, right, dims, preferred_element_type=jnp.float32)


def swapped(array):
    return pltpu.roll(array, array.shape[-1] // 2, axis=array.ndim - 1)


def lower_half(shape):
    return lax.broadcasted_iota(jnp.int32, shape, len(shape) - 1) < shape[-1] // 2


def signs(shape, dtype):
    return jnp.where(lower_half(shape), 1.0, -1.0).astype(dtype)


def image_item(links, lower, upper, slot, left_ref, right_ref):
    sites, vectors, width = lower.shape
    half = width // 2
    aggs = sites // SIDE
    sign = signs((vectors, width), jnp.bfloat16)
    zero = jnp.zeros((vectors, width), jnp.bfloat16)
    owner = lax.broadcasted_iota(jnp.int32, (half, 2 * aggs * vectors), 1) // (2 * vectors) % (aggs // 2)
    for part in range(SIDE):
        at = (slot * SIDE + part) * width
        mats = []
        plain, crossed = [], []
        for agg in range(aggs):
            site = agg * SIDE + part
            up = upper[site]
            pair = (up * sign, swapped(up))
            for rows, value in zip((plain, crossed), pair):
                rows.append(jnp.concatenate([value, zero] if agg % 2 == 0 else [zero, value], axis=1))
            if agg % 2 == 0:
                mats.append(jnp.concatenate([links[site], links[site + SIDE]], axis=1))
            low = lower[site]
            left_ref[pl.ds(agg * 2 * vectors, 2 * vectors), pl.ds(at, width)] = jnp.concatenate(
                [low, -sign * swapped(low)], axis=0
            )
        images = dot(jnp.concatenate(mats, axis=0), jnp.concatenate(plain + crossed, axis=0), ROW_DIMS)
        own = images[:half]
        for pair in range(1, aggs // 2):
            own = jnp.where(owner == pair, images[pair * half : (pair + 1) * half], own)
        own = own.astype(jnp.bfloat16)
        right_ref[pl.ds(at, half), :] = own[:, : aggs * vectors]
        right_ref[pl.ds(at + half, half), :] = own[:, aggs * vectors :]


def adjoint_item(links, lower, slot, left_ref):
    sites, vectors, width = lower.shape
    half = width // 2
    low = lower_half((vectors, width))
    sign = signs((vectors, width), jnp.float32)
    zero = jnp.zeros((vectors, width), jnp.bfloat16)
    for agg in range(sites // SIDE):
        rows = []
        mats = []
        for pair in range(SIDE // 2):
            at = agg * SIDE + 2 * pair
            lo_a, lo_b = lower[at], lower[at + 1]
            rows += [
                jnp.where(low, lo_a, zero),
                jnp.where(low, swapped(lo_a), zero),
                jnp.where(low, zero, swapped(lo_b)),
                jnp.where(low, zero, lo_b),
            ]
            mats.append(jnp.concatenate([links[at], links[at + 1]], axis=0))
        prod = dot(jnp.concatenate(rows, axis=0), jnp.concatenate(mats, axis=1), MAT_DIMS)
        for part in range(SIDE):
            top = part * 2 * vectors
            mine = prod[top : top + 2 * vectors, part // 2 * width : (part // 2 + 1) * width]
            adj = sign * mine[:vectors] + swapped(mine[vectors:])
            both = jnp.concatenate([adj, -sign * swapped(adj)], axis=0).astype(jnp.bfloat16)
            left_ref[pl.ds(agg * 2 * vectors, 2 * vectors), pl.ds((slot * SIDE + part) * width, width)] = both


def group_rows(left, right, dims, vectors):
    full = dot(left, right, dims)
    aggs = full.shape[1] // vectors
    lanes = lax.broadcasted_iota(jnp.int32, (2 * vectors, full.shape[1]), 1) // vectors
    own = jnp.zeros((2 * vectors, full.shape[1]), jnp.float32)
    for agg in range(aggs):
        own = jnp.where(lanes == agg, full[agg * 2 * vectors : (agg + 1) * 2 * vectors], own)
    pieces = []
    lane_group = lax.broadcasted_iota(jnp.int32, (aggs, full.shape[1]), 1) // vectors
    sub = lax.broadcasted_iota(jnp.int32, (aggs, full.shape[1]), 0)
    total = full.shape[1]
    for piece in range(2 * vectors // aggs):
        value = own[piece * aggs : (piece + 1) * aggs]
        step = 1
        while step < aggs:
            sub_bit = (sub // step) % 2
            lane_bit = (lane_group // step) % 2
            up = pltpu.roll(pltpu.roll(value, aggs - step, axis=0), step * vectors, axis=1)
            down = pltpu.roll(pltpu.roll(value, step, axis=0), total - step * vectors, axis=1)
            value = jnp.where(sub_bit == lane_bit, value, jnp.where(sub_bit == 0, up, down))
            step *= 2
        pieces.append(value)
    return jnp.concatenate(pieces, axis=1)


def slice_kernel(nulls, space_edge, time_edge, sems):
    copies = [
        pltpu.make_async_copy(nulls.at[:, pl.ds(0, 1)], space_edge, sems.at[0]),
        pltpu.make_async_copy(nulls.at[pl.ds(0, 1)], time_edge, sems.at[1]),
    ]
    for copy in copies:
        copy.start()
    for copy in copies:
        copy.wait()


def inner_kernel(place, lists, nulls, time_links, space_links, early, adjoint, picks, links, vecs, left, right, sems):
    time_count, space_count, sites, vectors, width = nulls.shape
    copies = []
    base = pltpu.make_async_copy(nulls, vecs, sems.at[16])
    base.start()

    def fetch(source):
        slot = len(copies)
        copy = pltpu.make_async_copy(source, links.at[slot], sems.at[slot])
        copy.start()
        copies.append(copy)

    for x in range(4):
        fetch(time_links.at[0, x])
    for t in range(4):
        fetch(space_links.at[t, 0])
    for x in range(4):
        fetch(time_links.at[1, x])
    for t in range(4):
        fetch(space_links.at[t, 1])
    me = place[0]
    shards, cap = lists.shape
    count = picks.shape[2] // 2
    lane = lax.broadcasted_iota(jnp.int32, (MOST, cap), 1)
    want = lax.broadcasted_iota(jnp.int32, (MOST, cap), 0)
    column = lax.broadcasted_iota(jnp.int32, (MOST, 2 * count), 1)
    quarter = count // 4
    inside = column % count
    turned = (inside // quarter % 2) * 2 * quarter + (inside // (2 * quarter)) * quarter + inside % quarter
    own_column = column < count
    side = lax.rem(me, 2)
    for turn in range(shards // 2):
        owner = 2 * jnp.bitwise_xor(me // 2, turn) + side
        mine = jnp.broadcast_to(lists[pl.ds(owner, 1), :], (MOST, cap))
        for parity in range(2):
            source = me - side + parity
            before = jnp.where((mine >= 0) & (mine < source * count), 1, 0)
            start = jnp.sum(before.astype(jnp.float32), axis=1, keepdims=True).astype(jnp.int32)
            match = (mine >= source * count) & (mine < (source + 1) * count) & (lane - start == want)
            chosen = jnp.sum(jnp.where(match, mine - source * count + 1, 0).astype(jnp.float32), axis=1, keepdims=True)
            chosen = chosen.astype(jnp.int32) - 1
            here = own_column == (side == parity)
            rows = pl.ds((2 * turn + parity) * MOST, MOST)
            picks[0, rows, :] = jnp.where(here & (inside == chosen), 1.0, 0.0)
            picks[1, rows, :] = jnp.where(here & (turned == chosen), 1.0, 0.0)
    base.wait()
    found = []
    for a_x in range(2):
        copies[2 * a_x].wait()
        copies[2 * a_x + 1].wait()
        for c in range(2):
            x = 2 * a_x + c
            image_item(links.at[x], vecs.at[1, x], vecs.at[2, x], c, left, right)
        found.append(group_rows(left[...], right[...], MAT_DIMS, vectors))
    for a_t in range(2):
        copies[4 + 2 * a_t].wait()
        copies[5 + 2 * a_t].wait()
        for c in range(2):
            t = 2 * a_t + c
            image_item(links.at[4 + t], vecs.at[t, 1], vecs.at[t, 2], c, left, right)
        found.append(group_rows(left[...], right[...], MAT_DIMS, vectors))
    early[...] = jnp.concatenate(found, axis=0).astype(jnp.bfloat16)
    for x in range(4):
        copies[8 + x].wait()
    for x in range(4):
        adjoint_item(links.at[8 + x], vecs.at[3, x], x % 2, adjoint.at[x // 2])
    for t in range(4):
        copies[12 + t].wait()
    for t in range(4):
        adjoint_item(links.at[12 + t], vecs.at[t, 3], t % 2, adjoint.at[2 + t // 2])


def edge_rows(uppers, adjoint, vectors):
    parts = []
    for upper in uppers:
        sites = upper.shape[0]
        for site in range(SIDE):
            rows = [upper[agg * SIDE + site] for agg in range(sites // SIDE)]
            parts.append(jnp.concatenate(rows, axis=0))
    return group_rows(adjoint, jnp.concatenate(parts, axis=1), ROW_DIMS, vectors)


def final_kernel(time_edge, space_edge, adjoint, late):
    vectors = space_edge.shape[3]
    found = []
    for a_x in range(2):
        uppers = [time_edge.at[0, 2 * a_x + c] for c in range(2)]
        found.append(edge_rows(uppers, adjoint[a_x], vectors))
    for a_t in range(2):
        uppers = [space_edge.at[2 * a_t + c, 0] for c in range(2)]
        found.append(edge_rows(uppers, adjoint[2 + a_t], vectors))
    late[...] = jnp.concatenate(found, axis=0).astype(jnp.bfloat16)


def pack_kernel(picks, early, early_other, late, late_other, *packed):
    half_count = late.shape[0] // 2
    pieces = (early, late, early_other, late_other)
    for half, width in enumerate((late.shape[1],) * 2):
        rows = jnp.concatenate([piece[pl.ds(half * half_count, half_count), :] for piece in pieces], axis=0)
        sent = dot(picks[half].astype(jnp.bfloat16), rows, MAT_DIMS)
        for turn, out in enumerate(packed):
            mine = sent[turn * 2 * MOST : (turn + 1) * 2 * MOST]
            out[:, pl.ds(half * width, width)] = mine.astype(jnp.bfloat16)


def unpack_kernel(place, *refs):
    pair = place[0] // 2
    result = refs[-1]
    for turn, arrived in enumerate(refs[-2::-1]):
        source = jnp.bitwise_xor(pair, turn)
        result[pl.ds(pl.multiple_of(source * 2 * MOST, 2 * MOST), 2 * MOST), :] = arrived[...].astype(jnp.float32)


def on_device(nulls, time_links, space_links, owner_lists):
    time_count, space_count, sites, vectors, width = nulls.shape
    shards, cap = owner_lists.shape
    aggs = sites // SIDE
    local_count = (time_count // 2) * (space_count // 2) * aggs
    wide = 2 * vectors * vectors
    place = lax.axis_index("xyz").astype(jnp.int32).reshape(1)
    vmem = pl.BlockSpec(memory_space=pltpu.VMEM)
    smem = pl.BlockSpec(memory_space=pltpu.SMEM)
    anywhere = pl.BlockSpec(memory_space=pl.ANY)
    outside = pl.BlockSpec(memory_space=pltpu.HBM)
    half = width // 2
    roomy = pltpu.CompilerParams(vmem_limit_bytes=51 * 1024 * 1024)
    modest = pltpu.CompilerParams(vmem_limit_bytes=24 * 1024 * 1024)
    first = pltpu.CompilerParams(vmem_limit_bytes=52 * 1024 * 1024)
    space_edge, time_edge = pl.pallas_call(
        slice_kernel,
        in_specs=[outside],
        out_specs=[vmem] * 2,
        out_shape=[
            jax.ShapeDtypeStruct((time_count, 1, sites, vectors, width), nulls.dtype),
            jax.ShapeDtypeStruct((1, space_count, sites, vectors, width), nulls.dtype),
        ],
        scratch_shapes=[pltpu.SemaphoreType.DMA((2,))],
        compiler_params=first,
        cost_estimate=pl.CostEstimate(flops=1000, bytes_accessed=1000, transcendentals=0),
        name="slices",
    )(nulls)
    edge_time = shifted(time_edge, "ta", -1)
    edge_space = shifted(space_edge, "xyz", -1)
    early, adjoint, picks = pl.pallas_call(
        inner_kernel,
        in_specs=[smem, vmem, outside, outside, outside],
        out_specs=[vmem] * 3,
        out_shape=[
            jax.ShapeDtypeStruct((4 * aggs, wide), jnp.bfloat16),
            jax.ShapeDtypeStruct((4, 2 * vectors * aggs, 8 * width), jnp.bfloat16),
            jax.ShapeDtypeStruct((2, shards * MOST, 2 * local_count), jnp.float32),
        ],
        scratch_shapes=[
            pltpu.VMEM((16, sites, half, width), jnp.bfloat16),
            pltpu.VMEM(nulls.shape, nulls.dtype),
            pltpu.VMEM((2 * vectors * aggs, 8 * width), jnp.bfloat16),
            pltpu.VMEM((8 * width, vectors * aggs), jnp.bfloat16),
            pltpu.SemaphoreType.DMA((17,)),
        ],
        compiler_params=roomy,
        cost_estimate=pl.CostEstimate(flops=1000, bytes_accessed=1000, transcendentals=0),
        name="inner",
    )(place, owner_lists, nulls, time_links, space_links)
    late = pl.pallas_call(
        final_kernel,
        in_specs=[vmem] * 3,
        out_specs=vmem,
        out_shape=jax.ShapeDtypeStruct((4 * aggs, wide), jnp.bfloat16),
        compiler_params=modest,
        cost_estimate=pl.CostEstimate(flops=1000, bytes_accessed=1000, transcendentals=0),
        name="final",
    )(edge_time, edge_space, adjoint)
    early_other = crossed(early, "xyz", 1)
    late_other = crossed(late, "xyz", 1)
    pairs = shards // 2
    packed = pl.pallas_call(
        pack_kernel,
        in_specs=[vmem] * 5,
        out_specs=[vmem] * pairs,
        out_shape=[jax.ShapeDtypeStruct((2 * MOST, 2 * wide), jnp.bfloat16)] * pairs,
        compiler_params=modest,
        cost_estimate=pl.CostEstimate(flops=1000, bytes_accessed=1000, transcendentals=0),
        name="pack",
    )(picks, early, early_other, late, late_other)
    arrived = [crossed(packed[turn], "xyz", 2 * turn) for turn in range(pairs - 1, 0, -1)]
    arrived.append(packed[0])
    arrived = pl.pallas_call(
        unpack_kernel,
        in_specs=[smem] + [vmem] * pairs,
        out_specs=vmem,
        out_shape=jax.ShapeDtypeStruct((shards * MOST, 2 * wide), jnp.float32),
        compiler_params=modest,
        cost_estimate=pl.CostEstimate(flops=1000, bytes_accessed=1000, transcendentals=0),
        name="unpack",
    )(place, *arrived)
    if shards * MOST == cap:
        result = arrived
    else:
        my_list = lax.dynamic_index_in_dim(owner_lists, lax.axis_index("xyz"), 0, keepdims=False)
        source = jnp.maximum(my_list, 0) // local_count
        order = jnp.arange(cap, dtype=jnp.int32)
        same = (source[:, None] == source[None, :]) & (order[None, :] < order[:, None])
        offset = jnp.sum(same.astype(jnp.int32), axis=1)
        picked = arrived[source * MOST + offset]
        result = jnp.where((my_list >= 0)[:, None], picked, 0.0)
    return result[None]


def solution(mesh):
    return jax.shard_map(
        on_device,
        mesh=mesh,
        in_specs=(
            P("ta", "xyz", None, None, None),
            P("ta", "xyz", None, None, None),
            P("ta", "xyz", None, None, None),
            P(),
        ),
        out_specs=P("ta", "xyz", None),
        check_vma=False,
    )
```

```python
import jax
import jax.numpy as jnp
from jax import lax
from jax.experimental import pallas as pl
from jax.experimental.pallas import tpu as pltpu
from jax.sharding import PartitionSpec as P

ROW_DIMS = (((1,), (1,)), ((), ()))
MAT_DIMS = (((1,), (0,)), ((), ()))
SIDE = 4
MOST = 8


def shifted(array, axis, by):
    count = lax.axis_size(axis)
    return lax.ppermute(array, axis, [(i, (i + by) % count) for i in range(count)])


def crossed(array, axis, bits):
    return lax.ppermute(array, axis, [(i, i ^ bits) for i in range(lax.axis_size(axis))])


def dot(left, right, dims):
    return lax.dot_general(left, right, dims, preferred_element_type=jnp.float32)


def swapped(array):
    return pltpu.roll(array, array.shape[-1] // 2, axis=array.ndim - 1)


def lower_half(shape):
    return lax.broadcasted_iota(jnp.int32, shape, len(shape) - 1) < shape[-1] // 2


def signs(shape, dtype):
    return jnp.where(lower_half(shape), 1.0, -1.0).astype(dtype)


def image_item(links, lower, upper, slot, left_ref, right_ref):
    sites, vectors, width = lower.shape
    half = width // 2
    aggs = sites // SIDE
    sign = signs((vectors, width), jnp.bfloat16)
    zero = jnp.zeros((vectors, width), jnp.bfloat16)
    owner = lax.broadcasted_iota(jnp.int32, (half, 2 * aggs * vectors), 1) // (2 * vectors) % (aggs // 2)
    for part in range(SIDE):
        at = (slot * SIDE + part) * width
        mats = []
        plain, crossed = [], []
        for agg in range(aggs):
            site = agg * SIDE + part
            up = upper[site]
            pair = (up * sign, swapped(up))
            for rows, value in zip((plain, crossed), pair):
                rows.append(jnp.concatenate([value, zero] if agg % 2 == 0 else [zero, value], axis=1))
            if agg % 2 == 0:
                mats.append(jnp.concatenate([links[site], links[site + SIDE]], axis=1))
            low = lower[site]
            left_ref[pl.ds(agg * 2 * vectors, 2 * vectors), pl.ds(at, width)] = jnp.concatenate(
                [low, -sign * swapped(low)], axis=0
            )
        images = dot(jnp.concatenate(mats, axis=0), jnp.concatenate(plain + crossed, axis=0), ROW_DIMS)
        own = images[:half]
        for pair in range(1, aggs // 2):
            own = jnp.where(owner == pair, images[pair * half : (pair + 1) * half], own)
        own = own.astype(jnp.bfloat16)
        right_ref[pl.ds(at, half), :] = own[:, : aggs * vectors]
        right_ref[pl.ds(at + half, half), :] = own[:, aggs * vectors :]


def adjoint_item(links, lower, slot, left_ref):
    sites, vectors, width = lower.shape
    half = width // 2
    low = lower_half((vectors, width))
    sign = signs((vectors, width), jnp.float32)
    zero = jnp.zeros((vectors, width), jnp.bfloat16)
    for agg in range(sites // SIDE):
        rows = []
        mats = []
        for pair in range(SIDE // 2):
            at = agg * SIDE + 2 * pair
            lo_a, lo_b = lower[at], lower[at + 1]
            rows += [
                jnp.where(low, lo_a, zero),
                jnp.where(low, swapped(lo_a), zero),
                jnp.where(low, zero, swapped(lo_b)),
                jnp.where(low, zero, lo_b),
            ]
            mats.append(jnp.concatenate([links[at], links[at + 1]], axis=0))
        prod = dot(jnp.concatenate(rows, axis=0), jnp.concatenate(mats, axis=1), MAT_DIMS)
        for part in range(SIDE):
            top = part * 2 * vectors
            mine = prod[top : top + 2 * vectors, part // 2 * width : (part // 2 + 1) * width]
            adj = sign * mine[:vectors] + swapped(mine[vectors:])
            both = jnp.concatenate([adj, -sign * swapped(adj)], axis=0).astype(jnp.bfloat16)
            left_ref[pl.ds(agg * 2 * vectors, 2 * vectors), pl.ds((slot * SIDE + part) * width, width)] = both


def group_rows(left, right, dims, vectors):
    full = dot(left, right, dims)
    aggs = full.shape[1] // vectors
    lanes = lax.broadcasted_iota(jnp.int32, (2 * vectors, full.shape[1]), 1) // vectors
    own = jnp.zeros((2 * vectors, full.shape[1]), jnp.float32)
    for agg in range(aggs):
        own = jnp.where(lanes == agg, full[agg * 2 * vectors : (agg + 1) * 2 * vectors], own)
    pieces = []
    lane_group = lax.broadcasted_iota(jnp.int32, (aggs, full.shape[1]), 1) // vectors
    sub = lax.broadcasted_iota(jnp.int32, (aggs, full.shape[1]), 0)
    total = full.shape[1]
    for piece in range(2 * vectors // aggs):
        value = own[piece * aggs : (piece + 1) * aggs]
        step = 1
        while step < aggs:
            sub_bit = (sub // step) % 2
            lane_bit = (lane_group // step) % 2
            up = pltpu.roll(pltpu.roll(value, aggs - step, axis=0), step * vectors, axis=1)
            down = pltpu.roll(pltpu.roll(value, step, axis=0), total - step * vectors, axis=1)
            value = jnp.where(sub_bit == lane_bit, value, jnp.where(sub_bit == 0, up, down))
            step *= 2
        pieces.append(value)
    return jnp.concatenate(pieces, axis=1)


def space_slice_kernel(nulls, edge, sem):
    copy = pltpu.make_async_copy(nulls.at[:, pl.ds(0, 1)], edge, sem)
    copy.start()
    copy.wait()


def time_slice_kernel(nulls, edge, sem):
    copy = pltpu.make_async_copy(nulls.at[pl.ds(0, 1)], edge, sem)
    copy.start()
    copy.wait()


def inner_kernel(place, lists, nulls, time_links, space_links, early, adjoint, picks, links, vecs, left, right, sems):
    time_count, space_count, sites, vectors, width = nulls.shape
    copies = []
    base = pltpu.make_async_copy(nulls, vecs, sems.at[16])
    base.start()

    def fetch(source):
        slot = len(copies)
        copy = pltpu.make_async_copy(source, links.at[slot], sems.at[slot])
        copy.start()
        copies.append(copy)

    for x in range(4):
        fetch(time_links.at[0, x])
    for t in range(4):
        fetch(space_links.at[t, 0])
    for x in range(4):
        fetch(time_links.at[1, x])
    for t in range(4):
        fetch(space_links.at[t, 1])
    me = place[0]
    shards, cap = lists.shape
    count = picks.shape[2] // 2
    lane = lax.broadcasted_iota(jnp.int32, (MOST, cap), 1)
    want = lax.broadcasted_iota(jnp.int32, (MOST, cap), 0)
    column = lax.broadcasted_iota(jnp.int32, (MOST, 2 * count), 1)
    quarter = count // 4
    inside = column % count
    turned = (inside // quarter % 2) * 2 * quarter + (inside // (2 * quarter)) * quarter + inside % quarter
    own_column = column < count
    side = lax.rem(me, 2)
    for turn in range(shards // 2):
        owner = 2 * jnp.bitwise_xor(me // 2, turn) + side
        mine = jnp.broadcast_to(lists[pl.ds(owner, 1), :], (MOST, cap))
        for parity in range(2):
            source = me - side + parity
            before = jnp.where((mine >= 0) & (mine < source * count), 1, 0)
            start = jnp.sum(before.astype(jnp.float32), axis=1, keepdims=True).astype(jnp.int32)
            match = (mine >= source * count) & (mine < (source + 1) * count) & (lane - start == want)
            chosen = jnp.sum(jnp.where(match, mine - source * count + 1, 0).astype(jnp.float32), axis=1, keepdims=True)
            chosen = chosen.astype(jnp.int32) - 1
            here = own_column == (side == parity)
            rows = pl.ds((2 * turn + parity) * MOST, MOST)
            picks[0, rows, :] = jnp.where(here & (inside == chosen), 1.0, 0.0)
            picks[1, rows, :] = jnp.where(here & (turned == chosen), 1.0, 0.0)
    base.wait()
    found = []
    for a_x in range(2):
        copies[2 * a_x].wait()
        copies[2 * a_x + 1].wait()
        for c in range(2):
            x = 2 * a_x + c
            image_item(links.at[x], vecs.at[1, x], vecs.at[2, x], c, left, right)
        found.append(group_rows(left[...], right[...], MAT_DIMS, vectors))
    for a_t in range(2):
        copies[4 + 2 * a_t].wait()
        copies[5 + 2 * a_t].wait()
        for c in range(2):
            t = 2 * a_t + c
            image_item(links.at[4 + t], vecs.at[t, 1], vecs.at[t, 2], c, left, right)
        found.append(group_rows(left[...], right[...], MAT_DIMS, vectors))
    early[...] = jnp.concatenate(found, axis=0).astype(jnp.bfloat16)
    for x in range(4):
        copies[8 + x].wait()
    for x in range(4):
        adjoint_item(links.at[8 + x], vecs.at[3, x], x % 2, adjoint.at[x // 2])
    for t in range(4):
        copies[12 + t].wait()
    for t in range(4):
        adjoint_item(links.at[12 + t], vecs.at[t, 3], t % 2, adjoint.at[2 + t // 2])


def edge_rows(uppers, adjoint, vectors):
    parts = []
    for upper in uppers:
        sites = upper.shape[0]
        for site in range(SIDE):
            rows = [upper[agg * SIDE + site] for agg in range(sites // SIDE)]
            parts.append(jnp.concatenate(rows, axis=0))
    return group_rows(adjoint, jnp.concatenate(parts, axis=1), ROW_DIMS, vectors)


def final_kernel(space_edge, time_edge, adjoint, late):
    vectors = space_edge.shape[3]
    found = []
    for a_x in range(2):
        uppers = [time_edge.at[0, 2 * a_x + c] for c in range(2)]
        found.append(edge_rows(uppers, adjoint[a_x], vectors))
    for a_t in range(2):
        uppers = [space_edge.at[2 * a_t + c, 0] for c in range(2)]
        found.append(edge_rows(uppers, adjoint[2 + a_t], vectors))
    late[...] = jnp.concatenate(found, axis=0).astype(jnp.bfloat16)


def pack_kernel(picks, early, early_other, late, late_other, *packed):
    half_count = late.shape[0] // 2
    pieces = (early, late, early_other, late_other)
    for half, width in enumerate((late.shape[1],) * 2):
        rows = jnp.concatenate([piece[pl.ds(half * half_count, half_count), :] for piece in pieces], axis=0)
        sent = dot(picks[half].astype(jnp.bfloat16), rows, MAT_DIMS)
        for turn, out in enumerate(packed):
            mine = sent[turn * 2 * MOST : (turn + 1) * 2 * MOST]
            out[:, pl.ds(half * width, width)] = mine.astype(jnp.bfloat16)


def unpack_kernel(place, *refs):
    pair = place[0] // 2
    result = refs[-1]
    for turn, arrived in enumerate(refs[-2::-1]):
        source = jnp.bitwise_xor(pair, turn)
        result[pl.ds(pl.multiple_of(source * 2 * MOST, 2 * MOST), 2 * MOST), :] = arrived[...].astype(jnp.float32)


def on_device(nulls, time_links, space_links, owner_lists):
    time_count, space_count, sites, vectors, width = nulls.shape
    shards, cap = owner_lists.shape
    aggs = sites // SIDE
    local_count = (time_count // 2) * (space_count // 2) * aggs
    wide = 2 * vectors * vectors
    place = lax.axis_index("xyz").astype(jnp.int32).reshape(1)
    vmem = pl.BlockSpec(memory_space=pltpu.VMEM)
    smem = pl.BlockSpec(memory_space=pltpu.SMEM)
    anywhere = pl.BlockSpec(memory_space=pl.ANY)
    outside = pl.BlockSpec(memory_space=pltpu.HBM)
    half = width // 2
    roomy = pltpu.CompilerParams(vmem_limit_bytes=51 * 1024 * 1024)
    modest = pltpu.CompilerParams(vmem_limit_bytes=24 * 1024 * 1024)
    first = pltpu.CompilerParams(vmem_limit_bytes=52 * 1024 * 1024)
    space_edge = pl.pallas_call(
        space_slice_kernel,
        in_specs=[outside],
        out_specs=vmem,
        out_shape=jax.ShapeDtypeStruct((time_count, 1, sites, vectors, width), nulls.dtype),
        scratch_shapes=[pltpu.SemaphoreType.DMA],
        compiler_params=first,
        cost_estimate=pl.CostEstimate(flops=1000, bytes_accessed=1000, transcendentals=0),
        name="space_slice",
    )(nulls)
    time_edge = pl.pallas_call(
        time_slice_kernel,
        in_specs=[outside],
        out_specs=vmem,
        out_shape=jax.ShapeDtypeStruct((1, space_count, sites, vectors, width), nulls.dtype),
        scratch_shapes=[pltpu.SemaphoreType.DMA],
        compiler_params=first,
        cost_estimate=pl.CostEstimate(flops=1000, bytes_accessed=1000, transcendentals=0),
        name="time_slice",
    )(nulls)
    edge_time = shifted(time_edge, "ta", -1)
    edge_space = shifted(space_edge, "xyz", -1)
    early, adjoint, picks = pl.pallas_call(
        inner_kernel,
        in_specs=[smem, vmem, outside, outside, outside],
        out_specs=[vmem] * 3,
        out_shape=[
            jax.ShapeDtypeStruct((4 * aggs, wide), jnp.bfloat16),
            jax.ShapeDtypeStruct((4, 2 * vectors * aggs, 8 * width), jnp.bfloat16),
            jax.ShapeDtypeStruct((2, shards * MOST, 2 * local_count), jnp.float32),
        ],
        scratch_shapes=[
            pltpu.VMEM((16, sites, half, width), jnp.bfloat16),
            pltpu.VMEM(nulls.shape, nulls.dtype),
            pltpu.VMEM((2 * vectors * aggs, 8 * width), jnp.bfloat16),
            pltpu.VMEM((8 * width, vectors * aggs), jnp.bfloat16),
            pltpu.SemaphoreType.DMA((17,)),
        ],
        compiler_params=roomy,
        cost_estimate=pl.CostEstimate(flops=1000, bytes_accessed=1000, transcendentals=0),
        name="inner",
    )(place, owner_lists, nulls, time_links, space_links)
    late = pl.pallas_call(
        final_kernel,
        in_specs=[vmem] * 3,
        out_specs=vmem,
        out_shape=jax.ShapeDtypeStruct((4 * aggs, wide), jnp.bfloat16),
        compiler_params=modest,
        cost_estimate=pl.CostEstimate(flops=1000, bytes_accessed=1000, transcendentals=0),
        name="final",
    )(edge_space, edge_time, adjoint)
    early_other = crossed(early, "xyz", 1)
    late_other = crossed(late, "xyz", 1)
    pairs = shards // 2
    packed = pl.pallas_call(
        pack_kernel,
        in_specs=[vmem] * 5,
        out_specs=[vmem] * pairs,
        out_shape=[jax.ShapeDtypeStruct((2 * MOST, 2 * wide), jnp.bfloat16)] * pairs,
        compiler_params=modest,
        cost_estimate=pl.CostEstimate(flops=1000, bytes_accessed=1000, transcendentals=0),
        name="pack",
    )(picks, early, early_other, late, late_other)
    arrived = [crossed(packed[turn], "xyz", 2 * turn) for turn in range(pairs - 1, 0, -1)]
    arrived.append(packed[0])
    arrived = pl.pallas_call(
        unpack_kernel,
        in_specs=[smem] + [vmem] * pairs,
        out_specs=vmem,
        out_shape=jax.ShapeDtypeStruct((shards * MOST, 2 * wide), jnp.float32),
        compiler_params=modest,
        cost_estimate=pl.CostEstimate(flops=1000, bytes_accessed=1000, transcendentals=0),
        name="unpack",
    )(place, *arrived)
    if shards * MOST == cap:
        result = arrived
    else:
        my_list = lax.dynamic_index_in_dim(owner_lists, lax.axis_index("xyz"), 0, keepdims=False)
        source = jnp.maximum(my_list, 0) // local_count
        order = jnp.arange(cap, dtype=jnp.int32)
        same = (source[:, None] == source[None, :]) & (order[None, :] < order[:, None])
        offset = jnp.sum(same.astype(jnp.int32), axis=1)
        picked = arrived[source * MOST + offset]
        result = jnp.where((my_list >= 0)[:, None], picked, 0.0)
    return result[None]


def solution(mesh):
    return jax.shard_map(
        on_device,
        mesh=mesh,
        in_specs=(
            P("ta", "xyz", None, None, None),
            P("ta", "xyz", None, None, None),
            P("ta", "xyz", None, None, None),
            P(),
        ),
        out_specs=P("ta", "xyz", None),
        check_vma=False,
    )
```

```python
import jax
import jax.numpy as jnp
from jax import lax
from jax.experimental import pallas as pl
from jax.experimental.pallas import tpu as pltpu
from jax.sharding import PartitionSpec as P

ROW_DIMS = (((1,), (1,)), ((), ()))
MAT_DIMS = (((1,), (0,)), ((), ()))
SIDE = 4
MOST = 8


def shifted(array, axis, by):
    count = lax.axis_size(axis)
    return lax.ppermute(array, axis, [(i, (i + by) % count) for i in range(count)])


def crossed(array, axis, bits):
    return lax.ppermute(array, axis, [(i, i ^ bits) for i in range(lax.axis_size(axis))])


def pair_turns(pair, pairs):
    last = pairs - 1
    turns = [(pair, pair)]
    for step in range(1, last):
        inside = pair < last
        turns.append(
            (
                jnp.where(inside, lax.rem(pair + step, last), pair),
                jnp.where(inside, lax.rem(pair + last - step, last), pair),
            )
        )
    for other in range(last):
        partner = jnp.where(pair == last, other, jnp.where(pair == other, last, pair))
        turns.append((partner, partner))
    return turns


def delivered(packed, axis):
    shards = lax.axis_size(axis)
    last = shards // 2 - 1
    arrived = []
    for step in range(1, last):
        moves = [(2 * i + side, 2 * ((i + step) % last) + side) for i in range(last) for side in range(2)]
        arrived.append(lax.ppermute(packed[step], axis, moves))
    for other in range(last):
        moves = [(2 * i + side, 2 * j + side) for i, j in ((other, last), (last, other)) for side in range(2)]
        arrived.append(lax.ppermute(packed[last + other], axis, moves))
    return arrived + [packed[0]]


def dot(left, right, dims):
    return lax.dot_general(left, right, dims, preferred_element_type=jnp.float32)


def swapped(array):
    return pltpu.roll(array, array.shape[-1] // 2, axis=array.ndim - 1)


def lower_half(shape):
    return lax.broadcasted_iota(jnp.int32, shape, len(shape) - 1) < shape[-1] // 2


def signs(shape, dtype):
    return jnp.where(lower_half(shape), 1.0, -1.0).astype(dtype)


def image_item(links, lower, upper, slot, left_ref, right_ref):
    sites, vectors, width = lower.shape
    half = width // 2
    aggs = sites // SIDE
    sign = signs((vectors, width), jnp.bfloat16)
    zero = jnp.zeros((vectors, width), jnp.bfloat16)
    owner = lax.broadcasted_iota(jnp.int32, (half, 2 * aggs * vectors), 1) // (2 * vectors) % (aggs // 2)
    for part in range(SIDE):
        at = (slot * SIDE + part) * width
        mats = []
        plain, crossed = [], []
        for agg in range(aggs):
            site = agg * SIDE + part
            up = upper[site]
            pair = (up * sign, swapped(up))
            for rows, value in zip((plain, crossed), pair):
                rows.append(jnp.concatenate([value, zero] if agg % 2 == 0 else [zero, value], axis=1))
            if agg % 2 == 0:
                mats.append(jnp.concatenate([links[site], links[site + SIDE]], axis=1))
            low = lower[site]
            left_ref[pl.ds(agg * 2 * vectors, 2 * vectors), pl.ds(at, width)] = jnp.concatenate(
                [low, -sign * swapped(low)], axis=0
            )
        images = dot(jnp.concatenate(mats, axis=0), jnp.concatenate(plain + crossed, axis=0), ROW_DIMS)
        own = images[:half]
        for pair in range(1, aggs // 2):
            own = jnp.where(owner == pair, images[pair * half : (pair + 1) * half], own)
        own = own.astype(jnp.bfloat16)
        right_ref[pl.ds(at, half), :] = own[:, : aggs * vectors]
        right_ref[pl.ds(at + half, half), :] = own[:, aggs * vectors :]


def adjoint_item(links, lower, slot, left_ref):
    sites, vectors, width = lower.shape
    half = width // 2
    low = lower_half((vectors, width))
    sign = signs((vectors, width), jnp.float32)
    zero = jnp.zeros((vectors, width), jnp.bfloat16)
    for agg in range(sites // SIDE):
        rows = []
        mats = []
        for pair in range(SIDE // 2):
            at = agg * SIDE + 2 * pair
            lo_a, lo_b = lower[at], lower[at + 1]
            rows += [
                jnp.where(low, lo_a, zero),
                jnp.where(low, swapped(lo_a), zero),
                jnp.where(low, zero, swapped(lo_b)),
                jnp.where(low, zero, lo_b),
            ]
            mats.append(jnp.concatenate([links[at], links[at + 1]], axis=0))
        prod = dot(jnp.concatenate(rows, axis=0), jnp.concatenate(mats, axis=1), MAT_DIMS)
        for part in range(SIDE):
            top = part * 2 * vectors
            mine = prod[top : top + 2 * vectors, part // 2 * width : (part // 2 + 1) * width]
            adj = sign * mine[:vectors] + swapped(mine[vectors:])
            both = jnp.concatenate([adj, -sign * swapped(adj)], axis=0).astype(jnp.bfloat16)
            left_ref[pl.ds(agg * 2 * vectors, 2 * vectors), pl.ds((slot * SIDE + part) * width, width)] = both


def group_rows(left, right, dims, vectors):
    full = dot(left, right, dims)
    aggs = full.shape[1] // vectors
    lanes = lax.broadcasted_iota(jnp.int32, (2 * vectors, full.shape[1]), 1) // vectors
    own = jnp.zeros((2 * vectors, full.shape[1]), jnp.float32)
    for agg in range(aggs):
        own = jnp.where(lanes == agg, full[agg * 2 * vectors : (agg + 1) * 2 * vectors], own)
    pieces = []
    lane_group = lax.broadcasted_iota(jnp.int32, (aggs, full.shape[1]), 1) // vectors
    sub = lax.broadcasted_iota(jnp.int32, (aggs, full.shape[1]), 0)
    total = full.shape[1]
    for piece in range(2 * vectors // aggs):
        value = own[piece * aggs : (piece + 1) * aggs]
        step = 1
        while step < aggs:
            sub_bit = (sub // step) % 2
            lane_bit = (lane_group // step) % 2
            up = pltpu.roll(pltpu.roll(value, aggs - step, axis=0), step * vectors, axis=1)
            down = pltpu.roll(pltpu.roll(value, step, axis=0), total - step * vectors, axis=1)
            value = jnp.where(sub_bit == lane_bit, value, jnp.where(sub_bit == 0, up, down))
            step *= 2
        pieces.append(value)
    return jnp.concatenate(pieces, axis=1)


def space_slice_kernel(nulls, edge, sem):
    copy = pltpu.make_async_copy(nulls.at[:, pl.ds(0, 1)], edge, sem)
    copy.start()
    copy.wait()


def time_slice_kernel(nulls, edge, sem):
    copy = pltpu.make_async_copy(nulls.at[pl.ds(0, 1)], edge, sem)
    copy.start()
    copy.wait()


def inner_kernel(place, lists, nulls, time_links, space_links, early, adjoint, picks, links, vecs, left, right, sems):
    time_count, space_count, sites, vectors, width = nulls.shape
    copies = []
    base = pltpu.make_async_copy(nulls, vecs, sems.at[16])
    base.start()

    def fetch(source):
        slot = len(copies)
        copy = pltpu.make_async_copy(source, links.at[slot], sems.at[slot])
        copy.start()
        copies.append(copy)

    for x in range(4):
        fetch(time_links.at[0, x])
    for t in range(4):
        fetch(space_links.at[t, 0])
    for x in range(4):
        fetch(time_links.at[1, x])
    for t in range(4):
        fetch(space_links.at[t, 1])
    me = place[0]
    shards, cap = lists.shape
    count = picks.shape[2] // 2
    lane = lax.broadcasted_iota(jnp.int32, (MOST, cap), 1)
    want = lax.broadcasted_iota(jnp.int32, (MOST, cap), 0)
    column = lax.broadcasted_iota(jnp.int32, (MOST, 2 * count), 1)
    quarter = count // 4
    inside = column % count
    turned = (inside // quarter % 2) * 2 * quarter + (inside // (2 * quarter)) * quarter + inside % quarter
    own_column = column < count
    side = lax.rem(me, 2)
    for turn, (target, _) in enumerate(pair_turns(me // 2, shards // 2)):
        owner = 2 * target + side
        mine = jnp.broadcast_to(lists[pl.ds(owner, 1), :], (MOST, cap))
        for parity in range(2):
            source = me - side + parity
            before = jnp.where((mine >= 0) & (mine < source * count), 1, 0)
            start = jnp.sum(before.astype(jnp.float32), axis=1, keepdims=True).astype(jnp.int32)
            match = (mine >= source * count) & (mine < (source + 1) * count) & (lane - start == want)
            chosen = jnp.sum(jnp.where(match, mine - source * count + 1, 0).astype(jnp.float32), axis=1, keepdims=True)
            chosen = chosen.astype(jnp.int32) - 1
            here = own_column == (side == parity)
            rows = pl.ds((2 * turn + parity) * MOST, MOST)
            picks[0, rows, :] = jnp.where(here & (inside == chosen), 1.0, 0.0)
            picks[1, rows, :] = jnp.where(here & (turned == chosen), 1.0, 0.0)
    base.wait()
    found = []
    for a_x in range(2):
        copies[2 * a_x].wait()
        copies[2 * a_x + 1].wait()
        for c in range(2):
            x = 2 * a_x + c
            image_item(links.at[x], vecs.at[1, x], vecs.at[2, x], c, left, right)
        found.append(group_rows(left[...], right[...], MAT_DIMS, vectors))
    for a_t in range(2):
        copies[4 + 2 * a_t].wait()
        copies[5 + 2 * a_t].wait()
        for c in range(2):
            t = 2 * a_t + c
            image_item(links.at[4 + t], vecs.at[t, 1], vecs.at[t, 2], c, left, right)
        found.append(group_rows(left[...], right[...], MAT_DIMS, vectors))
    early[...] = jnp.concatenate(found, axis=0).astype(jnp.bfloat16)
    for x in range(4):
        copies[8 + x].wait()
    for x in range(4):
        adjoint_item(links.at[8 + x], vecs.at[3, x], x % 2, adjoint.at[x // 2])
    for t in range(4):
        copies[12 + t].wait()
    for t in range(4):
        adjoint_item(links.at[12 + t], vecs.at[t, 3], t % 2, adjoint.at[2 + t // 2])


def edge_rows(uppers, adjoint, vectors):
    parts = []
    for upper in uppers:
        sites = upper.shape[0]
        for site in range(SIDE):
            rows = [upper[agg * SIDE + site] for agg in range(sites // SIDE)]
            parts.append(jnp.concatenate(rows, axis=0))
    return group_rows(adjoint, jnp.concatenate(parts, axis=1), ROW_DIMS, vectors)


def final_kernel(space_edge, time_edge, adjoint, late):
    vectors = space_edge.shape[3]
    found = []
    for a_x in range(2):
        uppers = [time_edge.at[0, 2 * a_x + c] for c in range(2)]
        found.append(edge_rows(uppers, adjoint[a_x], vectors))
    for a_t in range(2):
        uppers = [space_edge.at[2 * a_t + c, 0] for c in range(2)]
        found.append(edge_rows(uppers, adjoint[2 + a_t], vectors))
    late[...] = jnp.concatenate(found, axis=0).astype(jnp.bfloat16)


def pack_kernel(picks, early, early_other, late, late_other, *packed):
    half_count = late.shape[0] // 2
    pieces = (early, late, early_other, late_other)
    for half, width in enumerate((late.shape[1],) * 2):
        rows = jnp.concatenate([piece[pl.ds(half * half_count, half_count), :] for piece in pieces], axis=0)
        sent = dot(picks[half].astype(jnp.bfloat16), rows, MAT_DIMS)
        for turn, out in enumerate(packed):
            mine = sent[turn * 2 * MOST : (turn + 1) * 2 * MOST]
            out[:, pl.ds(half * width, width)] = mine.astype(jnp.bfloat16)


def unpack_kernel(place, *refs):
    result = refs[-1]
    pairs = result.shape[0] // (2 * MOST)
    turns = pair_turns(place[0] // 2, pairs)
    for arrived, (_, source) in zip(refs[:-1], turns[1:] + turns[:1]):
        rows = pl.ds(pl.multiple_of(source * 2 * MOST, 2 * MOST), 2 * MOST)
        result[rows, :] = arrived[...].astype(jnp.float32)


def on_device(nulls, time_links, space_links, owner_lists):
    time_count, space_count, sites, vectors, width = nulls.shape
    shards, cap = owner_lists.shape
    aggs = sites // SIDE
    local_count = (time_count // 2) * (space_count // 2) * aggs
    wide = 2 * vectors * vectors
    turns = shards - 2
    place = lax.axis_index("xyz").astype(jnp.int32).reshape(1)
    vmem = pl.BlockSpec(memory_space=pltpu.VMEM)
    smem = pl.BlockSpec(memory_space=pltpu.SMEM)
    anywhere = pl.BlockSpec(memory_space=pl.ANY)
    outside = pl.BlockSpec(memory_space=pltpu.HBM)
    half = width // 2
    roomy = pltpu.CompilerParams(vmem_limit_bytes=51 * 1024 * 1024)
    modest = pltpu.CompilerParams(vmem_limit_bytes=24 * 1024 * 1024)
    first = pltpu.CompilerParams(vmem_limit_bytes=52 * 1024 * 1024)
    space_edge = pl.pallas_call(
        space_slice_kernel,
        in_specs=[outside],
        out_specs=vmem,
        out_shape=jax.ShapeDtypeStruct((time_count, 1, sites, vectors, width), nulls.dtype),
        scratch_shapes=[pltpu.SemaphoreType.DMA],
        compiler_params=first,
        cost_estimate=pl.CostEstimate(flops=1000, bytes_accessed=1000, transcendentals=0),
        name="space_slice",
    )(nulls)
    time_edge = pl.pallas_call(
        time_slice_kernel,
        in_specs=[outside],
        out_specs=vmem,
        out_shape=jax.ShapeDtypeStruct((1, space_count, sites, vectors, width), nulls.dtype),
        scratch_shapes=[pltpu.SemaphoreType.DMA],
        compiler_params=first,
        cost_estimate=pl.CostEstimate(flops=1000, bytes_accessed=1000, transcendentals=0),
        name="time_slice",
    )(nulls)
    edge_time = shifted(time_edge, "ta", -1)
    edge_space = shifted(space_edge, "xyz", -1)
    early, adjoint, picks = pl.pallas_call(
        inner_kernel,
        in_specs=[smem, vmem, outside, outside, outside],
        out_specs=[vmem] * 3,
        out_shape=[
            jax.ShapeDtypeStruct((4 * aggs, wide), jnp.bfloat16),
            jax.ShapeDtypeStruct((4, 2 * vectors * aggs, 8 * width), jnp.bfloat16),
            jax.ShapeDtypeStruct((2, turns * 2 * MOST, 2 * local_count), jnp.float32),
        ],
        scratch_shapes=[
            pltpu.VMEM((16, sites, half, width), jnp.bfloat16),
            pltpu.VMEM(nulls.shape, nulls.dtype),
            pltpu.VMEM((2 * vectors * aggs, 8 * width), jnp.bfloat16),
            pltpu.VMEM((8 * width, vectors * aggs), jnp.bfloat16),
            pltpu.SemaphoreType.DMA((17,)),
        ],
        compiler_params=roomy,
        cost_estimate=pl.CostEstimate(flops=1000, bytes_accessed=1000, transcendentals=0),
        name="inner",
    )(place, owner_lists, nulls, time_links, space_links)
    late = pl.pallas_call(
        final_kernel,
        in_specs=[vmem] * 3,
        out_specs=vmem,
        out_shape=jax.ShapeDtypeStruct((4 * aggs, wide), jnp.bfloat16),
        compiler_params=modest,
        cost_estimate=pl.CostEstimate(flops=1000, bytes_accessed=1000, transcendentals=0),
        name="final",
    )(edge_space, edge_time, adjoint)
    early_other = crossed(early, "xyz", 1)
    late_other = crossed(late, "xyz", 1)
    packed = pl.pallas_call(
        pack_kernel,
        in_specs=[vmem] * 5,
        out_specs=[vmem] * turns,
        out_shape=[jax.ShapeDtypeStruct((2 * MOST, 2 * wide), jnp.bfloat16)] * turns,
        compiler_params=modest,
        cost_estimate=pl.CostEstimate(flops=1000, bytes_accessed=1000, transcendentals=0),
        name="pack",
    )(picks, early, early_other, late, late_other)
    arrived = delivered(packed, "xyz")
    arrived = pl.pallas_call(
        unpack_kernel,
        in_specs=[smem] + [vmem] * turns,
        out_specs=vmem,
        out_shape=jax.ShapeDtypeStruct((shards * MOST, 2 * wide), jnp.float32),
        compiler_params=modest,
        cost_estimate=pl.CostEstimate(flops=1000, bytes_accessed=1000, transcendentals=0),
        name="unpack",
    )(place, *arrived)
    if shards * MOST == cap:
        result = arrived
    else:
        my_list = lax.dynamic_index_in_dim(owner_lists, lax.axis_index("xyz"), 0, keepdims=False)
        source = jnp.maximum(my_list, 0) // local_count
        order = jnp.arange(cap, dtype=jnp.int32)
        same = (source[:, None] == source[None, :]) & (order[None, :] < order[:, None])
        offset = jnp.sum(same.astype(jnp.int32), axis=1)
        picked = arrived[source * MOST + offset]
        result = jnp.where((my_list >= 0)[:, None], picked, 0.0)
    return result[None]


def solution(mesh):
    return jax.shard_map(
        on_device,
        mesh=mesh,
        in_specs=(
            P("ta", "xyz", None, None, None),
            P("ta", "xyz", None, None, None),
            P("ta", "xyz", None, None, None),
            P(),
        ),
        out_specs=P("ta", "xyz", None),
        check_vma=False,
    )
```

```python
import jax
import jax.numpy as jnp
from jax import lax
from jax.experimental import pallas as pl
from jax.experimental.pallas import tpu as pltpu
from jax.sharding import PartitionSpec as P

ROW_DIMS = (((1,), (1,)), ((), ()))
MAT_DIMS = (((1,), (0,)), ((), ()))
SIDE = 4
MOST = 8


def shifted(array, axis, by):
    count = lax.axis_size(axis)
    return lax.ppermute(array, axis, [(i, (i + by) % count) for i in range(count)])


def crossed(array, axis, bits):
    return lax.ppermute(array, axis, [(i, i ^ bits) for i in range(lax.axis_size(axis))])


def pair_turns(pair, pairs):
    last = pairs - 1
    turns = [(pair, pair)]
    for step in range(1, last):
        inside = pair < last
        turns.append(
            (
                jnp.where(inside, lax.rem(pair + step, last), pair),
                jnp.where(inside, lax.rem(pair + last - step, last), pair),
            )
        )
    for other in range(last):
        partner = jnp.where(pair == last, other, jnp.where(pair == other, last, pair))
        turns.append((partner, partner))
    return turns


def delivered(packed, axis):
    shards = lax.axis_size(axis)
    last = shards // 2 - 1
    arrived = []
    for step in range(1, last):
        targets = [(i + step) % last for i in range(last)] + [last]
        moves = [(2 * i + side, 2 * j + side) for i, j in enumerate(targets) for side in range(2)]
        arrived.append(lax.ppermute(packed[step], axis, moves))
    for other in range(last):
        targets = [last if i == other else other if i == last else i for i in range(last + 1)]
        moves = [(2 * i + side, 2 * j + side) for i, j in enumerate(targets) for side in range(2)]
        arrived.append(lax.ppermute(packed[last + other], axis, moves))
    return arrived + [packed[0]]


def dot(left, right, dims):
    return lax.dot_general(left, right, dims, preferred_element_type=jnp.float32)


def swapped(array):
    return pltpu.roll(array, array.shape[-1] // 2, axis=array.ndim - 1)


def lower_half(shape):
    return lax.broadcasted_iota(jnp.int32, shape, len(shape) - 1) < shape[-1] // 2


def signs(shape, dtype):
    return jnp.where(lower_half(shape), 1.0, -1.0).astype(dtype)


def image_item(links, lower, upper, slot, left_ref, right_ref):
    sites, vectors, width = lower.shape
    half = width // 2
    aggs = sites // SIDE
    sign = signs((vectors, width), jnp.bfloat16)
    zero = jnp.zeros((vectors, width), jnp.bfloat16)
    owner = lax.broadcasted_iota(jnp.int32, (half, 2 * aggs * vectors), 1) // (2 * vectors) % (aggs // 2)
    for part in range(SIDE):
        at = (slot * SIDE + part) * width
        mats = []
        plain, crossed = [], []
        for agg in range(aggs):
            site = agg * SIDE + part
            up = upper[site]
            pair = (up * sign, swapped(up))
            for rows, value in zip((plain, crossed), pair):
                rows.append(jnp.concatenate([value, zero] if agg % 2 == 0 else [zero, value], axis=1))
            if agg % 2 == 0:
                mats.append(jnp.concatenate([links[site], links[site + SIDE]], axis=1))
            low = lower[site]
            left_ref[pl.ds(agg * 2 * vectors, 2 * vectors), pl.ds(at, width)] = jnp.concatenate(
                [low, -sign * swapped(low)], axis=0
            )
        images = dot(jnp.concatenate(mats, axis=0), jnp.concatenate(plain + crossed, axis=0), ROW_DIMS)
        own = images[:half]
        for pair in range(1, aggs // 2):
            own = jnp.where(owner == pair, images[pair * half : (pair + 1) * half], own)
        own = own.astype(jnp.bfloat16)
        right_ref[pl.ds(at, half), :] = own[:, : aggs * vectors]
        right_ref[pl.ds(at + half, half), :] = own[:, aggs * vectors :]


def adjoint_item(links, lower, slot, left_ref):
    sites, vectors, width = lower.shape
    half = width // 2
    low = lower_half((vectors, width))
    sign = signs((vectors, width), jnp.float32)
    zero = jnp.zeros((vectors, width), jnp.bfloat16)
    for agg in range(sites // SIDE):
        rows = []
        mats = []
        for pair in range(SIDE // 2):
            at = agg * SIDE + 2 * pair
            lo_a, lo_b = lower[at], lower[at + 1]
            rows += [
                jnp.where(low, lo_a, zero),
                jnp.where(low, swapped(lo_a), zero),
                jnp.where(low, zero, swapped(lo_b)),
                jnp.where(low, zero, lo_b),
            ]
            mats.append(jnp.concatenate([links[at], links[at + 1]], axis=0))
        prod = dot(jnp.concatenate(rows, axis=0), jnp.concatenate(mats, axis=1), MAT_DIMS)
        for part in range(SIDE):
            top = part * 2 * vectors
            mine = prod[top : top + 2 * vectors, part // 2 * width : (part // 2 + 1) * width]
            adj = sign * mine[:vectors] + swapped(mine[vectors:])
            both = jnp.concatenate([adj, -sign * swapped(adj)], axis=0).astype(jnp.bfloat16)
            left_ref[pl.ds(agg * 2 * vectors, 2 * vectors), pl.ds((slot * SIDE + part) * width, width)] = both


def group_rows(left, right, dims, vectors):
    full = dot(left, right, dims)
    aggs = full.shape[1] // vectors
    lanes = lax.broadcasted_iota(jnp.int32, (2 * vectors, full.shape[1]), 1) // vectors
    own = jnp.zeros((2 * vectors, full.shape[1]), jnp.float32)
    for agg in range(aggs):
        own = jnp.where(lanes == agg, full[agg * 2 * vectors : (agg + 1) * 2 * vectors], own)
    pieces = []
    lane_group = lax.broadcasted_iota(jnp.int32, (aggs, full.shape[1]), 1) // vectors
    sub = lax.broadcasted_iota(jnp.int32, (aggs, full.shape[1]), 0)
    total = full.shape[1]
    for piece in range(2 * vectors // aggs):
        value = own[piece * aggs : (piece + 1) * aggs]
        step = 1
        while step < aggs:
            sub_bit = (sub // step) % 2
            lane_bit = (lane_group // step) % 2
            up = pltpu.roll(pltpu.roll(value, aggs - step, axis=0), step * vectors, axis=1)
            down = pltpu.roll(pltpu.roll(value, step, axis=0), total - step * vectors, axis=1)
            value = jnp.where(sub_bit == lane_bit, value, jnp.where(sub_bit == 0, up, down))
            step *= 2
        pieces.append(value)
    return jnp.concatenate(pieces, axis=1)


def space_slice_kernel(nulls, edge, sem):
    copy = pltpu.make_async_copy(nulls.at[:, pl.ds(0, 1)], edge, sem)
    copy.start()
    copy.wait()


def time_slice_kernel(nulls, edge, sem):
    copy = pltpu.make_async_copy(nulls.at[pl.ds(0, 1)], edge, sem)
    copy.start()
    copy.wait()


def inner_kernel(place, lists, nulls, time_links, space_links, early, adjoint, picks, links, vecs, left, right, sems):
    time_count, space_count, sites, vectors, width = nulls.shape
    copies = []
    base = pltpu.make_async_copy(nulls, vecs, sems.at[16])
    base.start()

    def fetch(source):
        slot = len(copies)
        copy = pltpu.make_async_copy(source, links.at[slot], sems.at[slot])
        copy.start()
        copies.append(copy)

    for x in range(4):
        fetch(time_links.at[0, x])
    for t in range(4):
        fetch(space_links.at[t, 0])
    for x in range(4):
        fetch(time_links.at[1, x])
    for t in range(4):
        fetch(space_links.at[t, 1])
    me = place[0]
    shards, cap = lists.shape
    count = picks.shape[2] // 2
    lane = lax.broadcasted_iota(jnp.int32, (MOST, cap), 1)
    want = lax.broadcasted_iota(jnp.int32, (MOST, cap), 0)
    column = lax.broadcasted_iota(jnp.int32, (MOST, 2 * count), 1)
    quarter = count // 4
    inside = column % count
    turned = (inside // quarter % 2) * 2 * quarter + (inside // (2 * quarter)) * quarter + inside % quarter
    own_column = column < count
    side = lax.rem(me, 2)
    for turn, (target, _) in enumerate(pair_turns(me // 2, shards // 2)):
        owner = 2 * target + side
        mine = jnp.broadcast_to(lists[pl.ds(owner, 1), :], (MOST, cap))
        for parity in range(2):
            source = me - side + parity
            before = jnp.where((mine >= 0) & (mine < source * count), 1, 0)
            start = jnp.sum(before.astype(jnp.float32), axis=1, keepdims=True).astype(jnp.int32)
            match = (mine >= source * count) & (mine < (source + 1) * count) & (lane - start == want)
            chosen = jnp.sum(jnp.where(match, mine - source * count + 1, 0).astype(jnp.float32), axis=1, keepdims=True)
            chosen = chosen.astype(jnp.int32) - 1
            here = own_column == (side == parity)
            rows = pl.ds((2 * turn + parity) * MOST, MOST)
            picks[0, rows, :] = jnp.where(here & (inside == chosen), 1.0, 0.0)
            picks[1, rows, :] = jnp.where(here & (turned == chosen), 1.0, 0.0)
    base.wait()
    found = []
    for a_x in range(2):
        copies[2 * a_x].wait()
        copies[2 * a_x + 1].wait()
        for c in range(2):
            x = 2 * a_x + c
            image_item(links.at[x], vecs.at[1, x], vecs.at[2, x], c, left, right)
        found.append(group_rows(left[...], right[...], MAT_DIMS, vectors))
    for a_t in range(2):
        copies[4 + 2 * a_t].wait()
        copies[5 + 2 * a_t].wait()
        for c in range(2):
            t = 2 * a_t + c
            image_item(links.at[4 + t], vecs.at[t, 1], vecs.at[t, 2], c, left, right)
        found.append(group_rows(left[...], right[...], MAT_DIMS, vectors))
    early[...] = jnp.concatenate(found, axis=0).astype(jnp.bfloat16)
    for x in range(4):
        copies[8 + x].wait()
    for x in range(4):
        adjoint_item(links.at[8 + x], vecs.at[3, x], x % 2, adjoint.at[x // 2])
    for t in range(4):
        copies[12 + t].wait()
    for t in range(4):
        adjoint_item(links.at[12 + t], vecs.at[t, 3], t % 2, adjoint.at[2 + t // 2])


def edge_rows(uppers, adjoint, vectors):
    parts = []
    for upper in uppers:
        sites = upper.shape[0]
        for site in range(SIDE):
            rows = [upper[agg * SIDE + site] for agg in range(sites // SIDE)]
            parts.append(jnp.concatenate(rows, axis=0))
    return group_rows(adjoint, jnp.concatenate(parts, axis=1), ROW_DIMS, vectors)


def final_kernel(space_edge, time_edge, adjoint, late):
    vectors = space_edge.shape[3]
    found = []
    for a_x in range(2):
        uppers = [time_edge.at[0, 2 * a_x + c] for c in range(2)]
        found.append(edge_rows(uppers, adjoint[a_x], vectors))
    for a_t in range(2):
        uppers = [space_edge.at[2 * a_t + c, 0] for c in range(2)]
        found.append(edge_rows(uppers, adjoint[2 + a_t], vectors))
    late[...] = jnp.concatenate(found, axis=0).astype(jnp.bfloat16)


def pack_kernel(picks, early, early_other, late, late_other, *packed):
    half_count = late.shape[0] // 2
    pieces = (early, late, early_other, late_other)
    for half, width in enumerate((late.shape[1],) * 2):
        rows = jnp.concatenate([piece[pl.ds(half * half_count, half_count), :] for piece in pieces], axis=0)
        sent = dot(picks[half].astype(jnp.bfloat16), rows, MAT_DIMS)
        for turn, out in enumerate(packed):
            mine = sent[turn * 2 * MOST : (turn + 1) * 2 * MOST]
            out[:, pl.ds(half * width, width)] = mine.astype(jnp.bfloat16)


def unpack_kernel(place, *refs):
    result = refs[-1]
    pairs = result.shape[0] // (2 * MOST)
    turns = pair_turns(place[0] // 2, pairs)
    for arrived, (_, source) in zip(refs[:-1], turns[1:] + turns[:1]):
        rows = pl.ds(pl.multiple_of(source * 2 * MOST, 2 * MOST), 2 * MOST)
        result[rows, :] = arrived[...].astype(jnp.float32)


def on_device(nulls, time_links, space_links, owner_lists):
    time_count, space_count, sites, vectors, width = nulls.shape
    shards, cap = owner_lists.shape
    aggs = sites // SIDE
    local_count = (time_count // 2) * (space_count // 2) * aggs
    wide = 2 * vectors * vectors
    turns = shards - 2
    place = lax.axis_index("xyz").astype(jnp.int32).reshape(1)
    vmem = pl.BlockSpec(memory_space=pltpu.VMEM)
    smem = pl.BlockSpec(memory_space=pltpu.SMEM)
    anywhere = pl.BlockSpec(memory_space=pl.ANY)
    outside = pl.BlockSpec(memory_space=pltpu.HBM)
    half = width // 2
    roomy = pltpu.CompilerParams(vmem_limit_bytes=51 * 1024 * 1024)
    modest = pltpu.CompilerParams(vmem_limit_bytes=24 * 1024 * 1024)
    first = pltpu.CompilerParams(vmem_limit_bytes=52 * 1024 * 1024)
    space_edge = pl.pallas_call(
        space_slice_kernel,
        in_specs=[outside],
        out_specs=vmem,
        out_shape=jax.ShapeDtypeStruct((time_count, 1, sites, vectors, width), nulls.dtype),
        scratch_shapes=[pltpu.SemaphoreType.DMA],
        compiler_params=first,
        cost_estimate=pl.CostEstimate(flops=1000, bytes_accessed=1000, transcendentals=0),
        name="space_slice",
    )(nulls)
    time_edge = pl.pallas_call(
        time_slice_kernel,
        in_specs=[outside],
        out_specs=vmem,
        out_shape=jax.ShapeDtypeStruct((1, space_count, sites, vectors, width), nulls.dtype),
        scratch_shapes=[pltpu.SemaphoreType.DMA],
        compiler_params=first,
        cost_estimate=pl.CostEstimate(flops=1000, bytes_accessed=1000, transcendentals=0),
        name="time_slice",
    )(nulls)
    edge_time = shifted(time_edge, "ta", -1)
    edge_space = shifted(space_edge, "xyz", -1)
    early, adjoint, picks = pl.pallas_call(
        inner_kernel,
        in_specs=[smem, vmem, outside, outside, outside],
        out_specs=[vmem] * 3,
        out_shape=[
            jax.ShapeDtypeStruct((4 * aggs, wide), jnp.bfloat16),
            jax.ShapeDtypeStruct((4, 2 * vectors * aggs, 8 * width), jnp.bfloat16),
            jax.ShapeDtypeStruct((2, turns * 2 * MOST, 2 * local_count), jnp.float32),
        ],
        scratch_shapes=[
            pltpu.VMEM((16, sites, half, width), jnp.bfloat16),
            pltpu.VMEM(nulls.shape, nulls.dtype),
            pltpu.VMEM((2 * vectors * aggs, 8 * width), jnp.bfloat16),
            pltpu.VMEM((8 * width, vectors * aggs), jnp.bfloat16),
            pltpu.SemaphoreType.DMA((17,)),
        ],
        compiler_params=roomy,
        cost_estimate=pl.CostEstimate(flops=1000, bytes_accessed=1000, transcendentals=0),
        name="inner",
    )(place, owner_lists, nulls, time_links, space_links)
    late = pl.pallas_call(
        final_kernel,
        in_specs=[vmem] * 3,
        out_specs=vmem,
        out_shape=jax.ShapeDtypeStruct((4 * aggs, wide), jnp.bfloat16),
        compiler_params=modest,
        cost_estimate=pl.CostEstimate(flops=1000, bytes_accessed=1000, transcendentals=0),
        name="final",
    )(edge_space, edge_time, adjoint)
    early_other = crossed(early, "xyz", 1)
    late_other = crossed(late, "xyz", 1)
    packed = pl.pallas_call(
        pack_kernel,
        in_specs=[vmem] * 5,
        out_specs=[vmem] * turns,
        out_shape=[jax.ShapeDtypeStruct((2 * MOST, 2 * wide), jnp.bfloat16)] * turns,
        compiler_params=modest,
        cost_estimate=pl.CostEstimate(flops=1000, bytes_accessed=1000, transcendentals=0),
        name="pack",
    )(picks, early, early_other, late, late_other)
    arrived = delivered(packed, "xyz")
    arrived = pl.pallas_call(
        unpack_kernel,
        in_specs=[smem] + [vmem] * turns,
        out_specs=vmem,
        out_shape=jax.ShapeDtypeStruct((shards * MOST, 2 * wide), jnp.float32),
        compiler_params=modest,
        cost_estimate=pl.CostEstimate(flops=1000, bytes_accessed=1000, transcendentals=0),
        name="unpack",
    )(place, *arrived)
    if shards * MOST == cap:
        result = arrived
    else:
        my_list = lax.dynamic_index_in_dim(owner_lists, lax.axis_index("xyz"), 0, keepdims=False)
        source = jnp.maximum(my_list, 0) // local_count
        order = jnp.arange(cap, dtype=jnp.int32)
        same = (source[:, None] == source[None, :]) & (order[None, :] < order[:, None])
        offset = jnp.sum(same.astype(jnp.int32), axis=1)
        picked = arrived[source * MOST + offset]
        result = jnp.where((my_list >= 0)[:, None], picked, 0.0)
    return result[None]


def solution(mesh):
    return jax.shard_map(
        on_device,
        mesh=mesh,
        in_specs=(
            P("ta", "xyz", None, None, None),
            P("ta", "xyz", None, None, None),
            P("ta", "xyz", None, None, None),
            P(),
        ),
        out_specs=P("ta", "xyz", None),
        check_vma=False,
    )
```

```python
import jax
import jax.numpy as jnp
from jax import lax
from jax.experimental import pallas as pl
from jax.experimental.pallas import tpu as pltpu
from jax.sharding import PartitionSpec as P

ROW_DIMS = (((1,), (1,)), ((), ()))
MAT_DIMS = (((1,), (0,)), ((), ()))
SIDE = 4
MOST = 8


def shifted(array, axis, by):
    count = lax.axis_size(axis)
    return lax.ppermute(array, axis, [(i, (i + by) % count) for i in range(count)])


def crossed(array, axis, bits):
    return lax.ppermute(array, axis, [(i, i ^ bits) for i in range(lax.axis_size(axis))])


def dot(left, right, dims):
    return lax.dot_general(left, right, dims, preferred_element_type=jnp.float32)


def swapped(array):
    return pltpu.roll(array, array.shape[-1] // 2, axis=array.ndim - 1)


def lower_half(shape):
    return lax.broadcasted_iota(jnp.int32, shape, len(shape) - 1) < shape[-1] // 2


def signs(shape, dtype):
    return jnp.where(lower_half(shape), 1.0, -1.0).astype(dtype)


def image_item(links, lower, upper, slot, left_ref, right_ref):
    sites, vectors, width = lower.shape
    half = width // 2
    aggs = sites // SIDE
    sign = signs((vectors, width), jnp.bfloat16)
    zero = jnp.zeros((vectors, width), jnp.bfloat16)
    owner = lax.broadcasted_iota(jnp.int32, (half, 2 * aggs * vectors), 1) // (2 * vectors) % (aggs // 2)
    for part in range(SIDE):
        at = (slot * SIDE + part) * width
        mats = []
        plain, crossed = [], []
        for agg in range(aggs):
            site = agg * SIDE + part
            up = upper[site]
            pair = (up * sign, swapped(up))
            for rows, value in zip((plain, crossed), pair):
                rows.append(jnp.concatenate([value, zero] if agg % 2 == 0 else [zero, value], axis=1))
            if agg % 2 == 0:
                mats.append(jnp.concatenate([links[site], links[site + SIDE]], axis=1))
            low = lower[site]
            left_ref[pl.ds(agg * 2 * vectors, 2 * vectors), pl.ds(at, width)] = jnp.concatenate(
                [low, -sign * swapped(low)], axis=0
            )
        images = dot(jnp.concatenate(mats, axis=0), jnp.concatenate(plain + crossed, axis=0), ROW_DIMS)
        own = images[:half]
        for pair in range(1, aggs // 2):
            own = jnp.where(owner == pair, images[pair * half : (pair + 1) * half], own)
        own = own.astype(jnp.bfloat16)
        right_ref[pl.ds(at, half), :] = own[:, : aggs * vectors]
        right_ref[pl.ds(at + half, half), :] = own[:, aggs * vectors :]


def adjoint_item(links, lower, slot, left_ref):
    sites, vectors, width = lower.shape
    half = width // 2
    low = lower_half((vectors, width))
    sign = signs((vectors, width), jnp.float32)
    zero = jnp.zeros((vectors, width), jnp.bfloat16)
    for agg in range(sites // SIDE):
        rows = []
        mats = []
        for pair in range(SIDE // 2):
            at = agg * SIDE + 2 * pair
            lo_a, lo_b = lower[at], lower[at + 1]
            rows += [
                jnp.where(low, lo_a, zero),
                jnp.where(low, swapped(lo_a), zero),
                jnp.where(low, zero, swapped(lo_b)),
                jnp.where(low, zero, lo_b),
            ]
            mats.append(jnp.concatenate([links[at], links[at + 1]], axis=0))
        prod = dot(jnp.concatenate(rows, axis=0), jnp.concatenate(mats, axis=1), MAT_DIMS)
        for part in range(SIDE):
            top = part * 2 * vectors
            mine = prod[top : top + 2 * vectors, part // 2 * width : (part // 2 + 1) * width]
            adj = sign * mine[:vectors] + swapped(mine[vectors:])
            both = jnp.concatenate([adj, -sign * swapped(adj)], axis=0).astype(jnp.bfloat16)
            left_ref[pl.ds(agg * 2 * vectors, 2 * vectors), pl.ds((slot * SIDE + part) * width, width)] = both


def group_rows(left, right, dims, vectors):
    full = dot(left, right, dims)
    aggs = full.shape[1] // vectors
    lanes = lax.broadcasted_iota(jnp.int32, (2 * vectors, full.shape[1]), 1) // vectors
    own = jnp.zeros((2 * vectors, full.shape[1]), jnp.float32)
    for agg in range(aggs):
        own = jnp.where(lanes == agg, full[agg * 2 * vectors : (agg + 1) * 2 * vectors], own)
    pieces = []
    lane_group = lax.broadcasted_iota(jnp.int32, (aggs, full.shape[1]), 1) // vectors
    sub = lax.broadcasted_iota(jnp.int32, (aggs, full.shape[1]), 0)
    total = full.shape[1]
    for piece in range(2 * vectors // aggs):
        value = own[piece * aggs : (piece + 1) * aggs]
        step = 1
        while step < aggs:
            sub_bit = (sub // step) % 2
            lane_bit = (lane_group // step) % 2
            up = pltpu.roll(pltpu.roll(value, aggs - step, axis=0), step * vectors, axis=1)
            down = pltpu.roll(pltpu.roll(value, step, axis=0), total - step * vectors, axis=1)
            value = jnp.where(sub_bit == lane_bit, value, jnp.where(sub_bit == 0, up, down))
            step *= 2
        pieces.append(value)
    return jnp.concatenate(pieces, axis=1)


def space_slice_kernel(nulls, edge, sem):
    copy = pltpu.make_async_copy(nulls.at[:, pl.ds(0, 1)], edge, sem)
    copy.start()
    copy.wait()


def time_slice_kernel(nulls, edge, sem):
    copy = pltpu.make_async_copy(nulls.at[pl.ds(0, 1)], edge, sem)
    copy.start()
    copy.wait()


def inner_kernel(place, lists, nulls, time_links, space_links, early, adjoint, picks, links, vecs, left, right, sems):
    time_count, space_count, sites, vectors, width = nulls.shape
    copies = []
    base = pltpu.make_async_copy(nulls, vecs, sems.at[16])
    base.start()

    def fetch(source):
        slot = len(copies)
        copy = pltpu.make_async_copy(source, links.at[slot], sems.at[slot])
        copy.start()
        copies.append(copy)

    for x in range(4):
        fetch(time_links.at[0, x])
    for t in range(4):
        fetch(space_links.at[t, 0])
    for x in range(4):
        fetch(time_links.at[1, x])
    for t in range(4):
        fetch(space_links.at[t, 1])
    me = place[0]
    shards, cap = lists.shape
    count = picks.shape[2] // 2
    lane = lax.broadcasted_iota(jnp.int32, (MOST, cap), 1)
    want = lax.broadcasted_iota(jnp.int32, (MOST, cap), 0)
    column = lax.broadcasted_iota(jnp.int32, (MOST, 2 * count), 1)
    quarter = count // 4
    inside = column % count
    turned = (inside // quarter % 2) * 2 * quarter + (inside // (2 * quarter)) * quarter + inside % quarter
    own_column = column < count
    side = lax.rem(me, 2)
    for turn in range(shards // 2):
        owner = 2 * turn + side
        mine = jnp.broadcast_to(lists[pl.ds(owner, 1), :], (MOST, cap))
        for parity in range(2):
            source = me - side + parity
            before = jnp.where((mine >= 0) & (mine < source * count), 1, 0)
            start = jnp.sum(before.astype(jnp.float32), axis=1, keepdims=True).astype(jnp.int32)
            match = (mine >= source * count) & (mine < (source + 1) * count) & (lane - start == want)
            chosen = jnp.sum(jnp.where(match, mine - source * count + 1, 0).astype(jnp.float32), axis=1, keepdims=True)
            chosen = chosen.astype(jnp.int32) - 1
            here = own_column == (side == parity)
            rows = pl.ds((2 * turn + parity) * MOST, MOST)
            picks[0, rows, :] = jnp.where(here & (inside == chosen), 1.0, 0.0)
            picks[1, rows, :] = jnp.where(here & (turned == chosen), 1.0, 0.0)
    base.wait()
    found = []
    for a_x in range(2):
        copies[2 * a_x].wait()
        copies[2 * a_x + 1].wait()
        for c in range(2):
            x = 2 * a_x + c
            image_item(links.at[x], vecs.at[1, x], vecs.at[2, x], c, left, right)
        found.append(group_rows(left[...], right[...], MAT_DIMS, vectors))
    for a_t in range(2):
        copies[4 + 2 * a_t].wait()
        copies[5 + 2 * a_t].wait()
        for c in range(2):
            t = 2 * a_t + c
            image_item(links.at[4 + t], vecs.at[t, 1], vecs.at[t, 2], c, left, right)
        found.append(group_rows(left[...], right[...], MAT_DIMS, vectors))
    early[...] = jnp.concatenate(found, axis=0).astype(jnp.bfloat16)
    for x in range(4):
        copies[8 + x].wait()
    for x in range(4):
        adjoint_item(links.at[8 + x], vecs.at[3, x], x % 2, adjoint.at[x // 2])
    for t in range(4):
        copies[12 + t].wait()
    for t in range(4):
        adjoint_item(links.at[12 + t], vecs.at[t, 3], t % 2, adjoint.at[2 + t // 2])


def edge_rows(uppers, adjoint, vectors):
    parts = []
    for upper in uppers:
        sites = upper.shape[0]
        for site in range(SIDE):
            rows = [upper[agg * SIDE + site] for agg in range(sites // SIDE)]
            parts.append(jnp.concatenate(rows, axis=0))
    return group_rows(adjoint, jnp.concatenate(parts, axis=1), ROW_DIMS, vectors)


def final_kernel(space_edge, time_edge, adjoint, late):
    vectors = space_edge.shape[3]
    found = []
    for a_x in range(2):
        uppers = [time_edge.at[0, 2 * a_x + c] for c in range(2)]
        found.append(edge_rows(uppers, adjoint[a_x], vectors))
    for a_t in range(2):
        uppers = [space_edge.at[2 * a_t + c, 0] for c in range(2)]
        found.append(edge_rows(uppers, adjoint[2 + a_t], vectors))
    late[...] = jnp.concatenate(found, axis=0).astype(jnp.bfloat16)


def pack_kernel(picks, early, early_other, late, late_other, packed):
    half_count = late.shape[0] // 2
    pieces = (early, late, early_other, late_other)
    for half, width in enumerate((late.shape[1],) * 2):
        rows = jnp.concatenate([piece[pl.ds(half * half_count, half_count), :] for piece in pieces], axis=0)
        sent = dot(picks[half].astype(jnp.bfloat16), rows, MAT_DIMS)
        packed[:, pl.ds(half * width, width)] = sent.astype(jnp.bfloat16)


def on_device(nulls, time_links, space_links, owner_lists):
    time_count, space_count, sites, vectors, width = nulls.shape
    shards, cap = owner_lists.shape
    aggs = sites // SIDE
    local_count = (time_count // 2) * (space_count // 2) * aggs
    wide = 2 * vectors * vectors
    place = lax.axis_index("xyz").astype(jnp.int32).reshape(1)
    vmem = pl.BlockSpec(memory_space=pltpu.VMEM)
    smem = pl.BlockSpec(memory_space=pltpu.SMEM)
    anywhere = pl.BlockSpec(memory_space=pl.ANY)
    outside = pl.BlockSpec(memory_space=pltpu.HBM)
    half = width // 2
    roomy = pltpu.CompilerParams(vmem_limit_bytes=51 * 1024 * 1024)
    modest = pltpu.CompilerParams(vmem_limit_bytes=24 * 1024 * 1024)
    first = pltpu.CompilerParams(vmem_limit_bytes=52 * 1024 * 1024)
    space_edge = pl.pallas_call(
        space_slice_kernel,
        in_specs=[outside],
        out_specs=vmem,
        out_shape=jax.ShapeDtypeStruct((time_count, 1, sites, vectors, width), nulls.dtype),
        scratch_shapes=[pltpu.SemaphoreType.DMA],
        compiler_params=first,
        cost_estimate=pl.CostEstimate(flops=1000, bytes_accessed=1000, transcendentals=0),
        name="space_slice",
    )(nulls)
    time_edge = pl.pallas_call(
        time_slice_kernel,
        in_specs=[outside],
        out_specs=vmem,
        out_shape=jax.ShapeDtypeStruct((1, space_count, sites, vectors, width), nulls.dtype),
        scratch_shapes=[pltpu.SemaphoreType.DMA],
        compiler_params=first,
        cost_estimate=pl.CostEstimate(flops=1000, bytes_accessed=1000, transcendentals=0),
        name="time_slice",
    )(nulls)
    edge_time = shifted(time_edge, "ta", -1)
    edge_space = shifted(space_edge, "xyz", -1)
    early, adjoint, picks = pl.pallas_call(
        inner_kernel,
        in_specs=[smem, vmem, outside, outside, outside],
        out_specs=[vmem] * 3,
        out_shape=[
            jax.ShapeDtypeStruct((4 * aggs, wide), jnp.bfloat16),
            jax.ShapeDtypeStruct((4, 2 * vectors * aggs, 8 * width), jnp.bfloat16),
            jax.ShapeDtypeStruct((2, shards * MOST, 2 * local_count), jnp.float32),
        ],
        scratch_shapes=[
            pltpu.VMEM((16, sites, half, width), jnp.bfloat16),
            pltpu.VMEM(nulls.shape, nulls.dtype),
            pltpu.VMEM((2 * vectors * aggs, 8 * width), jnp.bfloat16),
            pltpu.VMEM((8 * width, vectors * aggs), jnp.bfloat16),
            pltpu.SemaphoreType.DMA((17,)),
        ],
        compiler_params=roomy,
        cost_estimate=pl.CostEstimate(flops=1000, bytes_accessed=1000, transcendentals=0),
        name="inner",
    )(place, owner_lists, nulls, time_links, space_links)
    late = pl.pallas_call(
        final_kernel,
        in_specs=[vmem] * 3,
        out_specs=vmem,
        out_shape=jax.ShapeDtypeStruct((4 * aggs, wide), jnp.bfloat16),
        compiler_params=modest,
        cost_estimate=pl.CostEstimate(flops=1000, bytes_accessed=1000, transcendentals=0),
        name="final",
    )(edge_space, edge_time, adjoint)
    early_other = crossed(early, "xyz", 1)
    late_other = crossed(late, "xyz", 1)
    packed = pl.pallas_call(
        pack_kernel,
        in_specs=[vmem] * 5,
        out_specs=vmem,
        out_shape=jax.ShapeDtypeStruct((shards * MOST, 2 * wide), jnp.bfloat16),
        compiler_params=modest,
        cost_estimate=pl.CostEstimate(flops=1000, bytes_accessed=1000, transcendentals=0),
        name="pack",
    )(picks, early, early_other, late, late_other)
    groups = [list(range(side, shards, 2)) for side in range(2)]
    arrived = lax.all_to_all(packed, "xyz", 0, 0, axis_index_groups=groups, tiled=True).astype(jnp.float32)
    if shards * MOST == cap:
        result = arrived
    else:
        my_list = lax.dynamic_index_in_dim(owner_lists, lax.axis_index("xyz"), 0, keepdims=False)
        source = jnp.maximum(my_list, 0) // local_count
        order = jnp.arange(cap, dtype=jnp.int32)
        same = (source[:, None] == source[None, :]) & (order[None, :] < order[:, None])
        offset = jnp.sum(same.astype(jnp.int32), axis=1)
        picked = arrived[source * MOST + offset]
        result = jnp.where((my_list >= 0)[:, None], picked, 0.0)
    return result[None]


def solution(mesh):
    return jax.shard_map(
        on_device,
        mesh=mesh,
        in_specs=(
            P("ta", "xyz", None, None, None),
            P("ta", "xyz", None, None, None),
            P("ta", "xyz", None, None, None),
            P(),
        ),
        out_specs=P("ta", "xyz", None),
        check_vma=False,
    )
```

```python
import functools

import jax
import jax.numpy as jnp
from jax import lax
from jax.experimental import pallas as pl
from jax.experimental.pallas import tpu as pltpu
from jax.sharding import PartitionSpec as P

ROW_DIMS = (((1,), (1,)), ((), ()))
MAT_DIMS = (((1,), (0,)), ((), ()))
SIDE = 4
MOST = 8


def shifted(array, axis, by):
    count = lax.axis_size(axis)
    return lax.ppermute(array, axis, [(i, (i + by) % count) for i in range(count)])


def crossed(array, axis, bits):
    return lax.ppermute(array, axis, [(i, i ^ bits) for i in range(lax.axis_size(axis))])


def dot(left, right, dims):
    return lax.dot_general(left, right, dims, preferred_element_type=jnp.float32)


def swapped(array):
    return pltpu.roll(array, array.shape[-1] // 2, axis=array.ndim - 1)


def lower_half(shape):
    return lax.broadcasted_iota(jnp.int32, shape, len(shape) - 1) < shape[-1] // 2


def signs(shape, dtype):
    return jnp.where(lower_half(shape), 1.0, -1.0).astype(dtype)


def image_item(links, lower, upper, slot, left_ref, right_ref):
    sites, vectors, width = lower.shape
    half = width // 2
    aggs = sites // SIDE
    sign = signs((vectors, width), jnp.bfloat16)
    zero = jnp.zeros((vectors, width), jnp.bfloat16)
    owner = lax.broadcasted_iota(jnp.int32, (half, 2 * aggs * vectors), 1) // (2 * vectors) % (aggs // 2)
    for part in range(SIDE):
        at = (slot * SIDE + part) * width
        mats = []
        plain, crossed = [], []
        for agg in range(aggs):
            site = agg * SIDE + part
            up = upper[site]
            pair = (up * sign, swapped(up))
            for rows, value in zip((plain, crossed), pair):
                rows.append(jnp.concatenate([value, zero] if agg % 2 == 0 else [zero, value], axis=1))
            if agg % 2 == 0:
                mats.append(jnp.concatenate([links[site], links[site + SIDE]], axis=1))
            low = lower[site]
            left_ref[pl.ds(agg * 2 * vectors, 2 * vectors), pl.ds(at, width)] = jnp.concatenate(
                [low, -sign * swapped(low)], axis=0
            )
        images = dot(jnp.concatenate(mats, axis=0), jnp.concatenate(plain + crossed, axis=0), ROW_DIMS)
        own = images[:half]
        for pair in range(1, aggs // 2):
            own = jnp.where(owner == pair, images[pair * half : (pair + 1) * half], own)
        own = own.astype(jnp.bfloat16)
        right_ref[pl.ds(at, half), :] = own[:, : aggs * vectors]
        right_ref[pl.ds(at + half, half), :] = own[:, aggs * vectors :]


def adjoint_item(links, lower, slot, left_ref):
    sites, vectors, width = lower.shape
    half = width // 2
    low = lower_half((vectors, width))
    sign = signs((vectors, width), jnp.float32)
    zero = jnp.zeros((vectors, width), jnp.bfloat16)
    for agg in range(sites // SIDE):
        rows = []
        mats = []
        for pair in range(SIDE // 2):
            at = agg * SIDE + 2 * pair
            lo_a, lo_b = lower[at], lower[at + 1]
            rows += [
                jnp.where(low, lo_a, zero),
                jnp.where(low, swapped(lo_a), zero),
                jnp.where(low, zero, swapped(lo_b)),
                jnp.where(low, zero, lo_b),
            ]
            mats.append(jnp.concatenate([links[at], links[at + 1]], axis=0))
        prod = dot(jnp.concatenate(rows, axis=0), jnp.concatenate(mats, axis=1), MAT_DIMS)
        for part in range(SIDE):
            top = part * 2 * vectors
            mine = prod[top : top + 2 * vectors, part // 2 * width : (part // 2 + 1) * width]
            adj = sign * mine[:vectors] + swapped(mine[vectors:])
            both = jnp.concatenate([adj, -sign * swapped(adj)], axis=0).astype(jnp.bfloat16)
            left_ref[pl.ds(agg * 2 * vectors, 2 * vectors), pl.ds((slot * SIDE + part) * width, width)] = both


def group_rows(left, right, dims, vectors):
    full = dot(left, right, dims)
    aggs = full.shape[1] // vectors
    lanes = lax.broadcasted_iota(jnp.int32, (2 * vectors, full.shape[1]), 1) // vectors
    own = jnp.zeros((2 * vectors, full.shape[1]), jnp.float32)
    for agg in range(aggs):
        own = jnp.where(lanes == agg, full[agg * 2 * vectors : (agg + 1) * 2 * vectors], own)
    pieces = []
    lane_group = lax.broadcasted_iota(jnp.int32, (aggs, full.shape[1]), 1) // vectors
    sub = lax.broadcasted_iota(jnp.int32, (aggs, full.shape[1]), 0)
    total = full.shape[1]
    for piece in range(2 * vectors // aggs):
        value = own[piece * aggs : (piece + 1) * aggs]
        step = 1
        while step < aggs:
            sub_bit = (sub // step) % 2
            lane_bit = (lane_group // step) % 2
            up = pltpu.roll(pltpu.roll(value, aggs - step, axis=0), step * vectors, axis=1)
            down = pltpu.roll(pltpu.roll(value, step, axis=0), total - step * vectors, axis=1)
            value = jnp.where(sub_bit == lane_bit, value, jnp.where(sub_bit == 0, up, down))
            step *= 2
        pieces.append(value)
    return jnp.concatenate(pieces, axis=1)


def slice_kernel(nulls, *refs, sources):
    edges, sems = refs[:-1], refs[-1]
    copies = []
    for edge, (start, count, at, space) in zip(edges, sources):
        for row in range(count):
            source = nulls.at[pl.ds(start + row, 1), pl.ds(at, space)]
            copies.append(pltpu.make_async_copy(source, edge.at[pl.ds(row, 1)], sems.at[len(copies)]))
    for copy in copies:
        copy.start()
    for copy in copies:
        copy.wait()


def inner_kernel(place, lists, nulls, time_links, space_links, early, adjoint, picks, links, vecs, left, right, sems):
    time_count, space_count, sites, vectors, width = nulls.shape
    copies = []
    base = pltpu.make_async_copy(nulls, vecs, sems.at[16])
    base.start()

    def fetch(source):
        slot = len(copies)
        copy = pltpu.make_async_copy(source, links.at[slot], sems.at[slot])
        copy.start()
        copies.append(copy)

    for x in range(4):
        fetch(time_links.at[0, x])
    for t in range(4):
        fetch(space_links.at[t, 0])
    for x in range(4):
        fetch(time_links.at[1, x])
    for t in range(4):
        fetch(space_links.at[t, 1])
    me = place[0]
    shards, cap = lists.shape
    count = picks.shape[2] // 2
    lane = lax.broadcasted_iota(jnp.int32, (MOST, cap), 1)
    want = lax.broadcasted_iota(jnp.int32, (MOST, cap), 0)
    column = lax.broadcasted_iota(jnp.int32, (MOST, 2 * count), 1)
    quarter = count // 4
    inside = column % count
    turned = (inside // quarter % 2) * 2 * quarter + (inside // (2 * quarter)) * quarter + inside % quarter
    own_column = column < count
    side = lax.rem(me, 2)
    for turn in range(shards // 2):
        owner = 2 * jnp.bitwise_xor(me // 2, turn) + side
        mine = jnp.broadcast_to(lists[pl.ds(owner, 1), :], (MOST, cap))
        for parity in range(2):
            source = me - side + parity
            before = jnp.where((mine >= 0) & (mine < source * count), 1, 0)
            start = jnp.sum(before.astype(jnp.float32), axis=1, keepdims=True).astype(jnp.int32)
            match = (mine >= source * count) & (mine < (source + 1) * count) & (lane - start == want)
            chosen = jnp.sum(jnp.where(match, mine - source * count + 1, 0).astype(jnp.float32), axis=1, keepdims=True)
            chosen = chosen.astype(jnp.int32) - 1
            here = own_column == (side == parity)
            rows = pl.ds((2 * turn + parity) * MOST, MOST)
            picks[0, rows, :] = jnp.where(here & (inside == chosen), 1.0, 0.0)
            picks[1, rows, :] = jnp.where(here & (turned == chosen), 1.0, 0.0)
    base.wait()
    found = []
    for a_x in range(2):
        copies[2 * a_x].wait()
        copies[2 * a_x + 1].wait()
        for c in range(2):
            x = 2 * a_x + c
            image_item(links.at[x], vecs.at[1, x], vecs.at[2, x], c, left, right)
        found.append(group_rows(left[...], right[...], MAT_DIMS, vectors))
    for a_t in range(2):
        copies[4 + 2 * a_t].wait()
        copies[5 + 2 * a_t].wait()
        for c in range(2):
            t = 2 * a_t + c
            image_item(links.at[4 + t], vecs.at[t, 1], vecs.at[t, 2], c, left, right)
        found.append(group_rows(left[...], right[...], MAT_DIMS, vectors))
    early[...] = jnp.concatenate(found, axis=0).astype(jnp.bfloat16)
    for x in range(4):
        copies[8 + x].wait()
    for x in range(4):
        adjoint_item(links.at[8 + x], vecs.at[3, x], x % 2, adjoint.at[x // 2])
    for t in range(4):
        copies[12 + t].wait()
    for t in range(4):
        adjoint_item(links.at[12 + t], vecs.at[t, 3], t % 2, adjoint.at[2 + t // 2])


def edge_rows(uppers, adjoint, vectors):
    parts = []
    for upper in uppers:
        sites = upper.shape[0]
        for site in range(SIDE):
            rows = [upper[agg * SIDE + site] for agg in range(sites // SIDE)]
            parts.append(jnp.concatenate(rows, axis=0))
    return group_rows(adjoint, jnp.concatenate(parts, axis=1), ROW_DIMS, vectors)


def middle_kernel(space_edge, time_first, time_second, adjoint, found):
    vectors = space_edge.shape[3]
    rows = []
    for a_x, time_edge in enumerate((time_first, time_second)):
        uppers = [time_edge.at[0, c] for c in range(2)]
        rows.append(edge_rows(uppers, adjoint[a_x], vectors))
    rows.append(edge_rows([space_edge.at[c, 0] for c in range(2)], adjoint[2], vectors))
    found[...] = jnp.concatenate(rows, axis=0)


def final_kernel(space_edge, adjoint, found, late):
    vectors = space_edge.shape[3]
    rows = edge_rows([space_edge.at[c, 0] for c in range(2)], adjoint[3], vectors)
    late[...] = jnp.concatenate([found[...], rows], axis=0).astype(jnp.bfloat16)


def pack_kernel(picks, early, early_other, late, late_other, *packed):
    half_count = late.shape[0] // 2
    pieces = (early, late, early_other, late_other)
    for half, width in enumerate((late.shape[1],) * 2):
        rows = jnp.concatenate([piece[pl.ds(half * half_count, half_count), :] for piece in pieces], axis=0)
        sent = dot(picks[half].astype(jnp.bfloat16), rows, MAT_DIMS)
        for turn, out in enumerate(packed):
            mine = sent[turn * 2 * MOST : (turn + 1) * 2 * MOST]
            out[:, pl.ds(half * width, width)] = mine.astype(jnp.bfloat16)


def unpack_kernel(place, *refs, turns):
    pair = place[0] // 2
    result = refs[-1]
    for turn, arrived in zip(turns, refs[:-1]):
        source = jnp.bitwise_xor(pair, turn)
        result[pl.ds(pl.multiple_of(source * 2 * MOST, 2 * MOST), 2 * MOST), :] = arrived[...].astype(jnp.float32)


def finish_kernel(place, arrived, unfinished, result, rows, sem, turn):
    source = jnp.bitwise_xor(place[0] // 2, turn)
    rows[...] = arrived[...].astype(jnp.float32)
    copy = pltpu.make_async_copy(
        rows, result.at[pl.ds(pl.multiple_of(source * 2 * MOST, 2 * MOST), 2 * MOST)], sem
    )
    copy.start()
    copy.wait()


def on_device(nulls, time_links, space_links, owner_lists):
    time_count, space_count, sites, vectors, width = nulls.shape
    shards, cap = owner_lists.shape
    aggs = sites // SIDE
    local_count = (time_count // 2) * (space_count // 2) * aggs
    wide = 2 * vectors * vectors
    place = lax.axis_index("xyz").astype(jnp.int32).reshape(1)
    vmem = pl.BlockSpec(memory_space=pltpu.VMEM)
    smem = pl.BlockSpec(memory_space=pltpu.SMEM)
    anywhere = pl.BlockSpec(memory_space=pl.ANY)
    outside = pl.BlockSpec(memory_space=pltpu.HBM)
    half = width // 2
    roomy = pltpu.CompilerParams(vmem_limit_bytes=51 * 1024 * 1024)
    modest = pltpu.CompilerParams(vmem_limit_bytes=24 * 1024 * 1024)
    first = pltpu.CompilerParams(vmem_limit_bytes=52 * 1024 * 1024)
    tiny = pl.CostEstimate(flops=1000, bytes_accessed=1000, transcendentals=0)
    half_time = time_count // 2

    def sliced(name, *sources):
        shapes = [(count, space, sites, vectors, width) for _, count, _, space in sources]
        return pl.pallas_call(
            functools.partial(slice_kernel, sources=sources),
            in_specs=[outside],
            out_specs=[vmem] * len(sources),
            out_shape=[jax.ShapeDtypeStruct(shape, nulls.dtype) for shape in shapes],
            scratch_shapes=[pltpu.SemaphoreType.DMA((sum(source[1] for source in sources),))],
            compiler_params=first,
            cost_estimate=tiny,
            name=name,
        )(nulls)

    half_space = space_count // 2
    (space_first,) = sliced("slice_first", (0, half_time, 0, 1))
    space_second, time_first, time_second = sliced(
        "slice_rest", (half_time, half_time, 0, 1), (0, 1, 0, half_space), (0, 1, half_space, half_space)
    )
    edge_first = shifted(space_first, "xyz", -1)
    edge_times = [shifted(time_first, "ta", -1), shifted(time_second, "ta", -1)]
    edge_second = shifted(space_second, "xyz", -1)
    early, adjoint, picks = pl.pallas_call(
        inner_kernel,
        in_specs=[smem, vmem, outside, outside, outside],
        out_specs=[vmem] * 3,
        out_shape=[
            jax.ShapeDtypeStruct((4 * aggs, wide), jnp.bfloat16),
            jax.ShapeDtypeStruct((4, 2 * vectors * aggs, 8 * width), jnp.bfloat16),
            jax.ShapeDtypeStruct((2, shards * MOST, 2 * local_count), jnp.float32),
        ],
        scratch_shapes=[
            pltpu.VMEM((16, sites, half, width), jnp.bfloat16),
            pltpu.VMEM(nulls.shape, nulls.dtype),
            pltpu.VMEM((2 * vectors * aggs, 8 * width), jnp.bfloat16),
            pltpu.VMEM((8 * width, vectors * aggs), jnp.bfloat16),
            pltpu.SemaphoreType.DMA((17,)),
        ],
        compiler_params=roomy,
        cost_estimate=tiny,
        name="inner",
    )(place, owner_lists, nulls, time_links, space_links)
    found = pl.pallas_call(
        middle_kernel,
        in_specs=[vmem] * 4,
        out_specs=vmem,
        out_shape=jax.ShapeDtypeStruct((3 * aggs, wide), jnp.float32),
        compiler_params=modest,
        cost_estimate=tiny,
        name="middle",
    )(edge_first, *edge_times, adjoint)
    late = pl.pallas_call(
        final_kernel,
        in_specs=[vmem] * 3,
        out_specs=vmem,
        out_shape=jax.ShapeDtypeStruct((4 * aggs, wide), jnp.bfloat16),
        compiler_params=modest,
        cost_estimate=tiny,
        name="final",
    )(edge_second, adjoint, found)
    early_other = crossed(early, "xyz", 1)
    late_other = crossed(late, "xyz", 1)
    pairs = shards // 2
    packed = pl.pallas_call(
        pack_kernel,
        in_specs=[vmem] * 5,
        out_specs=[vmem] * pairs,
        out_shape=[jax.ShapeDtypeStruct((2 * MOST, 2 * wide), jnp.bfloat16)] * pairs,
        compiler_params=modest,
        cost_estimate=tiny,
        name="pack",
    )(picks, early, early_other, late, late_other)
    turns = list(range(2, pairs)) + [1]
    arrived = [crossed(packed[turn], "xyz", 2 * turn) for turn in turns]
    whole = jax.ShapeDtypeStruct((shards * MOST, 2 * wide), jnp.float32)
    unfinished = pl.pallas_call(
        functools.partial(unpack_kernel, turns=[0] + turns[:-1]),
        in_specs=[smem] + [vmem] * (pairs - 1),
        out_specs=vmem,
        out_shape=whole,
        compiler_params=modest,
        cost_estimate=tiny,
        name="unpack",
    )(place, packed[0], *arrived[:-1])
    arrived = pl.pallas_call(
        functools.partial(finish_kernel, turn=turns[-1]),
        in_specs=[smem, vmem, outside],
        out_specs=outside,
        out_shape=whole,
        scratch_shapes=[pltpu.VMEM((2 * MOST, 2 * wide), jnp.float32), pltpu.SemaphoreType.DMA],
        input_output_aliases={2: 0},
        compiler_params=modest,
        cost_estimate=tiny,
        name="finish",
    )(place, arrived[-1], unfinished)
    if shards * MOST == cap:
        result = arrived
    else:
        my_list = lax.dynamic_index_in_dim(owner_lists, lax.axis_index("xyz"), 0, keepdims=False)
        source = jnp.maximum(my_list, 0) // local_count
        order = jnp.arange(cap, dtype=jnp.int32)
        same = (source[:, None] == source[None, :]) & (order[None, :] < order[:, None])
        offset = jnp.sum(same.astype(jnp.int32), axis=1)
        picked = arrived[source * MOST + offset]
        result = jnp.where((my_list >= 0)[:, None], picked, 0.0)
    return result[None]


def solution(mesh):
    return jax.shard_map(
        on_device,
        mesh=mesh,
        in_specs=(
            P("ta", "xyz", None, None, None),
            P("ta", "xyz", None, None, None),
            P("ta", "xyz", None, None, None),
            P(),
        ),
        out_specs=P("ta", "xyz", None),
        check_vma=False,
    )
```

```python
import functools

import jax
import jax.numpy as jnp
from jax import lax
from jax.experimental import pallas as pl
from jax.experimental.pallas import tpu as pltpu
from jax.sharding import PartitionSpec as P

ROW_DIMS = (((1,), (1,)), ((), ()))
MAT_DIMS = (((1,), (0,)), ((), ()))
SIDE = 4
MOST = 8


def shifted(array, axis, by):
    count = lax.axis_size(axis)
    return lax.ppermute(array, axis, [(i, (i + by) % count) for i in range(count)])


def crossed(array, axis, bits):
    return lax.ppermute(array, axis, [(i, i ^ bits) for i in range(lax.axis_size(axis))])


def dot(left, right, dims):
    return lax.dot_general(left, right, dims, preferred_element_type=jnp.float32)


def swapped(array):
    return pltpu.roll(array, array.shape[-1] // 2, axis=array.ndim - 1)


def lower_half(shape):
    return lax.broadcasted_iota(jnp.int32, shape, len(shape) - 1) < shape[-1] // 2


def signs(shape, dtype):
    return jnp.where(lower_half(shape), 1.0, -1.0).astype(dtype)


def image_item(links, lower, upper, slot, left_ref, right_ref):
    sites, vectors, width = lower.shape
    half = width // 2
    aggs = sites // SIDE
    lanes = aggs * vectors
    sign = signs((vectors, width), jnp.bfloat16)
    zero = jnp.zeros((vectors, width), jnp.bfloat16)
    owner = lax.broadcasted_iota(jnp.int32, (half, 2 * lanes), 1) // (2 * vectors) % (aggs // 2)
    for part in range(SIDE):
        at = (slot * SIDE + part) * width
        mats = []
        plain, crossed = [], []
        for agg in range(aggs):
            site = agg * SIDE + part
            up = upper[site]
            pair = (up * sign, swapped(up))
            for rows, value in zip((plain, crossed), pair):
                rows.append(jnp.concatenate([value, zero] if agg % 2 == 0 else [zero, value], axis=1))
            if agg % 2 == 0:
                mats.append(jnp.concatenate([links[site], links[site + SIDE]], axis=1))
            left_ref[pl.ds(agg * vectors, vectors), pl.ds(at, width)] = lower[site]
        images = dot(jnp.concatenate(mats, axis=0), jnp.concatenate(plain + crossed, axis=0), ROW_DIMS)
        own = images[:half]
        for pair in range(1, aggs // 2):
            own = jnp.where(owner == pair, images[pair * half : (pair + 1) * half], own)
        own = own.astype(jnp.bfloat16)
        right_ref[pl.ds(at, half), :] = own
        right_ref[pl.ds(at + half, half), :] = jnp.concatenate([own[:, lanes:], -own[:, :lanes]], axis=1)


def adjoint_item(links, lower, slot, left_ref):
    sites, vectors, width = lower.shape
    half = width // 2
    low = lower_half((vectors, width))
    sign = signs((vectors, width), jnp.float32)
    zero = jnp.zeros((vectors, width), jnp.bfloat16)
    for agg in range(sites // SIDE):
        rows = []
        mats = []
        for pair in range(SIDE // 2):
            at = agg * SIDE + 2 * pair
            lo_a, lo_b = lower[at], lower[at + 1]
            rows += [
                jnp.where(low, lo_a, zero),
                jnp.where(low, swapped(lo_a), zero),
                jnp.where(low, zero, swapped(lo_b)),
                jnp.where(low, zero, lo_b),
            ]
            mats.append(jnp.concatenate([links[at], links[at + 1]], axis=0))
        prod = dot(jnp.concatenate(rows, axis=0), jnp.concatenate(mats, axis=1), MAT_DIMS)
        for part in range(SIDE):
            top = part * 2 * vectors
            mine = prod[top : top + 2 * vectors, part // 2 * width : (part // 2 + 1) * width]
            adj = sign * mine[:vectors] + swapped(mine[vectors:])
            left_ref[pl.ds(agg * vectors, vectors), pl.ds((slot * SIDE + part) * width, width)] = adj.astype(jnp.bfloat16)


def group_rows(left, right, dims, vectors):
    full = dot(left, right, dims)
    total = full.shape[1] // 2
    aggs = total // vectors
    lanes = lax.broadcasted_iota(jnp.int32, (vectors, 2 * total), 1) // vectors % aggs
    own = full[:vectors]
    for agg in range(1, aggs):
        own = jnp.where(lanes == agg, full[agg * vectors : (agg + 1) * vectors], own)
    pieces = []
    lane_group = lax.broadcasted_iota(jnp.int32, (aggs, total), 1) // vectors
    sub = lax.broadcasted_iota(jnp.int32, (aggs, total), 0)
    for piece in range(2 * vectors // aggs):
        part, row = divmod(piece * aggs, vectors)
        value = own[row : row + aggs, part * total : (part + 1) * total]
        step = 1
        while step < aggs:
            sub_bit = (sub // step) % 2
            lane_bit = (lane_group // step) % 2
            up = pltpu.roll(pltpu.roll(value, aggs - step, axis=0), step * vectors, axis=1)
            down = pltpu.roll(pltpu.roll(value, step, axis=0), total - step * vectors, axis=1)
            value = jnp.where(sub_bit == lane_bit, value, jnp.where(sub_bit == 0, up, down))
            step *= 2
        pieces.append(value)
    return jnp.concatenate(pieces, axis=1)


def slice_kernel(nulls, *refs, sources):
    edges, sems = refs[:-1], refs[-1]
    copies = []
    for edge, (start, count, at, space) in zip(edges, sources):
        for row in range(count):
            source = nulls.at[pl.ds(start + row, 1), pl.ds(at, space)]
            copies.append(pltpu.make_async_copy(source, edge.at[pl.ds(row, 1)], sems.at[len(copies)]))
    for copy in copies:
        copy.start()
    for copy in copies:
        copy.wait()


def choose_rows(place, lists, picks):
    me = place[0]
    shards, cap = lists.shape
    count = picks.shape[2] // 2
    lane = lax.broadcasted_iota(jnp.int32, (MOST, cap), 1)
    want = lax.broadcasted_iota(jnp.int32, (MOST, cap), 0)
    column = lax.broadcasted_iota(jnp.int32, (MOST, 2 * count), 1)
    quarter = count // 4
    inside = column % count
    turned = (inside // quarter % 2) * 2 * quarter + (inside // (2 * quarter)) * quarter + inside % quarter
    own_column = column < count
    side = lax.rem(me, 2)
    for turn in range(shards // 2):
        owner = 2 * jnp.bitwise_xor(me // 2, turn) + side
        mine = jnp.broadcast_to(lists[pl.ds(owner, 1), :], (MOST, cap))
        for parity in range(2):
            source = me - side + parity
            before = jnp.where((mine >= 0) & (mine < source * count), 1, 0)
            start = jnp.sum(before.astype(jnp.float32), axis=1, keepdims=True).astype(jnp.int32)
            match = (mine >= source * count) & (mine < (source + 1) * count) & (lane - start == want)
            chosen = jnp.sum(jnp.where(match, mine - source * count + 1, 0).astype(jnp.float32), axis=1, keepdims=True)
            chosen = chosen.astype(jnp.int32) - 1
            here = own_column == (side == parity)
            rows = pl.ds((2 * turn + parity) * MOST, MOST)
            picks[0, rows, :] = jnp.where(here & (inside == chosen), 1.0, 0.0)
            picks[1, rows, :] = jnp.where(here & (turned == chosen), 1.0, 0.0)


def inner_kernel(nulls, time_links, space_links, early, adjoint, links, vecs, left, right, sems):
    time_count, space_count, sites, vectors, width = nulls.shape
    copies = []
    bases = [pltpu.make_async_copy(nulls.at[t], vecs.at[t], sems.at[16 + t]) for t in range(4)]
    bases[1].start()
    bases[2].start()

    def fetch(source):
        slot = len(copies)
        copy = pltpu.make_async_copy(source, links.at[slot], sems.at[slot])
        copy.start()
        copies.append(copy)

    for x in range(4):
        fetch(time_links.at[0, x])
    bases[0].start()
    bases[3].start()
    for t in range(4):
        fetch(space_links.at[t, 0])
    for x in range(4):
        fetch(time_links.at[1, x])
    for t in range(4):
        fetch(space_links.at[t, 1])
    bases[1].wait()
    bases[2].wait()
    found = []
    for a_x in range(2):
        copies[2 * a_x].wait()
        copies[2 * a_x + 1].wait()
        for c in range(2):
            x = 2 * a_x + c
            image_item(links.at[x], vecs.at[1, x], vecs.at[2, x], c, left, right)
        found.append(group_rows(left[...], right[...], MAT_DIMS, vectors))
    bases[0].wait()
    bases[3].wait()
    for a_t in range(2):
        copies[4 + 2 * a_t].wait()
        copies[5 + 2 * a_t].wait()
        for c in range(2):
            t = 2 * a_t + c
            image_item(links.at[4 + t], vecs.at[t, 1], vecs.at[t, 2], c, left, right)
        found.append(group_rows(left[...], right[...], MAT_DIMS, vectors))
    early[...] = jnp.concatenate(found, axis=0).astype(jnp.bfloat16)
    for x in range(4):
        copies[8 + x].wait()
    for x in range(4):
        adjoint_item(links.at[8 + x], vecs.at[3, x], x % 2, adjoint.at[x // 2])
    for t in range(4):
        copies[12 + t].wait()
    for t in range(4):
        adjoint_item(links.at[12 + t], vecs.at[t, 3], t % 2, adjoint.at[2 + t // 2])


def edge_rows(uppers, adjoint, vectors):
    width = uppers[0].shape[-1]
    sign = signs((vectors, width), jnp.bfloat16)
    parts = []
    for upper in uppers:
        sites = upper.shape[0]
        for site in range(SIDE):
            rows = [upper[agg * SIDE + site] for agg in range(sites // SIDE)]
            turned = [sign * swapped(row) for row in rows]
            parts.append(jnp.concatenate(rows + turned, axis=0))
    return group_rows(adjoint, jnp.concatenate(parts, axis=1), ROW_DIMS, vectors)


def middle_kernel(place, lists, space_edge, time_first, time_second, adjoint, found, picks):
    choose_rows(place, lists, picks)
    vectors = space_edge.shape[3]
    rows = []
    for a_x, time_edge in enumerate((time_first, time_second)):
        uppers = [time_edge.at[0, c] for c in range(2)]
        rows.append(edge_rows(uppers, adjoint[a_x], vectors))
    rows.append(edge_rows([space_edge.at[c, 0] for c in range(2)], adjoint[2], vectors))
    found[...] = jnp.concatenate(rows, axis=0)


def final_kernel(space_edge, adjoint, found, late):
    vectors = space_edge.shape[3]
    rows = edge_rows([space_edge.at[c, 0] for c in range(2)], adjoint[3], vectors)
    late[...] = jnp.concatenate([found[...], rows], axis=0).astype(jnp.bfloat16)


def pack_kernel(picks, early, early_other, late, late_other, *packed):
    half_count = late.shape[0] // 2
    pieces = (early, late, early_other, late_other)
    for half, width in enumerate((late.shape[1],) * 2):
        rows = jnp.concatenate([piece[pl.ds(half * half_count, half_count), :] for piece in pieces], axis=0)
        sent = dot(picks[half].astype(jnp.bfloat16), rows, MAT_DIMS)
        for turn, out in enumerate(packed):
            mine = sent[turn * 2 * MOST : (turn + 1) * 2 * MOST]
            out[:, pl.ds(half * width, width)] = mine.astype(jnp.bfloat16)


def unpack_kernel(place, *refs, turns):
    pair = place[0] // 2
    result = refs[-1]
    for turn, arrived in zip(turns, refs[:-1]):
        source = jnp.bitwise_xor(pair, turn)
        result[pl.ds(pl.multiple_of(source * 2 * MOST, 2 * MOST), 2 * MOST), :] = arrived[...].astype(jnp.float32)


def on_device(nulls, time_links, space_links, owner_lists):
    time_count, space_count, sites, vectors, width = nulls.shape
    shards, cap = owner_lists.shape
    aggs = sites // SIDE
    local_count = (time_count // 2) * (space_count // 2) * aggs
    wide = 2 * vectors * vectors
    place = lax.axis_index("xyz").astype(jnp.int32).reshape(1)
    vmem = pl.BlockSpec(memory_space=pltpu.VMEM)
    smem = pl.BlockSpec(memory_space=pltpu.SMEM)
    anywhere = pl.BlockSpec(memory_space=pl.ANY)
    outside = pl.BlockSpec(memory_space=pltpu.HBM)
    half = width // 2
    roomy = pltpu.CompilerParams(vmem_limit_bytes=51 * 1024 * 1024)
    modest = pltpu.CompilerParams(vmem_limit_bytes=24 * 1024 * 1024)
    first = pltpu.CompilerParams(vmem_limit_bytes=52 * 1024 * 1024)
    tiny = pl.CostEstimate(flops=1000, bytes_accessed=1000, transcendentals=0)
    half_time = time_count // 2

    def sliced(name, *sources):
        shapes = [(count, space, sites, vectors, width) for _, count, _, space in sources]
        return pl.pallas_call(
            functools.partial(slice_kernel, sources=sources),
            in_specs=[outside],
            out_specs=[vmem] * len(sources),
            out_shape=[jax.ShapeDtypeStruct(shape, nulls.dtype) for shape in shapes],
            scratch_shapes=[pltpu.SemaphoreType.DMA((sum(source[1] for source in sources),))],
            compiler_params=first,
            cost_estimate=tiny,
            name=name,
        )(nulls)

    half_space = space_count // 2
    space_first, space_second, time_first, time_second = sliced(
        "slices",
        (0, half_time, 0, 1),
        (half_time, half_time, 0, 1),
        (0, 1, 0, half_space),
        (0, 1, half_space, half_space),
    )
    edge_first = shifted(space_first, "xyz", -1)
    edge_times = [shifted(time_first, "ta", -1), shifted(time_second, "ta", -1)]
    edge_second = shifted(space_second, "xyz", -1)
    early, adjoint = pl.pallas_call(
        inner_kernel,
        in_specs=[outside] * 3,
        out_specs=[vmem] * 2,
        out_shape=[
            jax.ShapeDtypeStruct((4 * aggs, wide), jnp.bfloat16),
            jax.ShapeDtypeStruct((4, vectors * aggs, 8 * width), jnp.bfloat16),
        ],
        scratch_shapes=[
            pltpu.VMEM((16, sites, half, width), jnp.bfloat16),
            pltpu.VMEM(nulls.shape, nulls.dtype),
            pltpu.VMEM((vectors * aggs, 8 * width), jnp.bfloat16),
            pltpu.VMEM((8 * width, 2 * vectors * aggs), jnp.bfloat16),
            pltpu.SemaphoreType.DMA((20,)),
        ],
        compiler_params=roomy,
        cost_estimate=tiny,
        name="inner",
    )(nulls, time_links, space_links)
    found, picks = pl.pallas_call(
        middle_kernel,
        in_specs=[smem] + [vmem] * 5,
        out_specs=[vmem] * 2,
        out_shape=[
            jax.ShapeDtypeStruct((3 * aggs, wide), jnp.float32),
            jax.ShapeDtypeStruct((2, shards * MOST, 2 * local_count), jnp.float32),
        ],
        compiler_params=modest,
        cost_estimate=tiny,
        name="middle",
    )(place, owner_lists, edge_first, *edge_times, adjoint)
    late = pl.pallas_call(
        final_kernel,
        in_specs=[vmem] * 3,
        out_specs=vmem,
        out_shape=jax.ShapeDtypeStruct((4 * aggs, wide), jnp.bfloat16),
        compiler_params=modest,
        cost_estimate=tiny,
        name="final",
    )(edge_second, adjoint, found)
    early_other = crossed(early, "xyz", 1)
    late_other = crossed(late, "xyz", 1)
    pairs = shards // 2
    packed = pl.pallas_call(
        pack_kernel,
        in_specs=[vmem] * 5,
        out_specs=[vmem] * pairs,
        out_shape=[jax.ShapeDtypeStruct((2 * MOST, 2 * wide), jnp.bfloat16)] * pairs,
        compiler_params=modest,
        cost_estimate=tiny,
        name="pack",
    )(picks, early, early_other, late, late_other)
    turns = list(range(2, pairs)) + [1]
    arrived = [crossed(packed[turn], "xyz", 2 * turn) for turn in turns]
    arrived = pl.pallas_call(
        functools.partial(unpack_kernel, turns=turns + [0]),
        in_specs=[smem] + [vmem] * pairs,
        out_specs=vmem,
        out_shape=jax.ShapeDtypeStruct((shards * MOST, 2 * wide), jnp.float32),
        compiler_params=modest,
        cost_estimate=tiny,
        name="unpack",
    )(place, *arrived, packed[0])
    if shards * MOST == cap:
        result = arrived
    else:
        my_list = lax.dynamic_index_in_dim(owner_lists, lax.axis_index("xyz"), 0, keepdims=False)
        source = jnp.maximum(my_list, 0) // local_count
        order = jnp.arange(cap, dtype=jnp.int32)
        same = (source[:, None] == source[None, :]) & (order[None, :] < order[:, None])
        offset = jnp.sum(same.astype(jnp.int32), axis=1)
        picked = arrived[source * MOST + offset]
        result = jnp.where((my_list >= 0)[:, None], picked, 0.0)
    return result[None]


def solution(mesh):
    return jax.shard_map(
        on_device,
        mesh=mesh,
        in_specs=(
            P("ta", "xyz", None, None, None),
            P("ta", "xyz", None, None, None),
            P("ta", "xyz", None, None, None),
            P(),
        ),
        out_specs=P("ta", "xyz", None),
        check_vma=False,
    )
```

```python
import functools

import jax
import jax.numpy as jnp
from jax import lax
from jax.experimental import pallas as pl
from jax.experimental.pallas import tpu as pltpu
from jax.sharding import PartitionSpec as P

ROW_DIMS = (((1,), (1,)), ((), ()))
MAT_DIMS = (((1,), (0,)), ((), ()))
SIDE = 4
MOST = 8


def shifted(array, axis, by):
    count = lax.axis_size(axis)
    return lax.ppermute(array, axis, [(i, (i + by) % count) for i in range(count)])


def crossed(array, axis, bits):
    return lax.ppermute(array, axis, [(i, i ^ bits) for i in range(lax.axis_size(axis))])


def dot(left, right, dims):
    return lax.dot_general(left, right, dims, preferred_element_type=jnp.float32)


def swapped(array):
    return pltpu.roll(array, array.shape[-1] // 2, axis=array.ndim - 1)


def lower_half(shape):
    return lax.broadcasted_iota(jnp.int32, shape, len(shape) - 1) < shape[-1] // 2


def signs(shape, dtype):
    return jnp.where(lower_half(shape), 1.0, -1.0).astype(dtype)


def image_item(links, lower, upper, slot, left_ref, right_ref):
    sites, vectors, width = lower.shape
    half = width // 2
    aggs = sites // SIDE
    lanes = aggs * vectors
    sign = signs((vectors, width), jnp.bfloat16)
    zero = jnp.zeros((vectors, width), jnp.bfloat16)
    owner = lax.broadcasted_iota(jnp.int32, (half, 2 * lanes), 1) // (2 * vectors) % (aggs // 2)
    for part in range(SIDE):
        at = (slot * SIDE + part) * width
        mats = []
        plain, crossed = [], []
        for agg in range(aggs):
            site = agg * SIDE + part
            up = upper[site]
            pair = (up * sign, swapped(up))
            for rows, value in zip((plain, crossed), pair):
                rows.append(jnp.concatenate([value, zero] if agg % 2 == 0 else [zero, value], axis=1))
            if agg % 2 == 0:
                mats.append(jnp.concatenate([links[site], links[site + SIDE]], axis=1))
            left_ref[pl.ds(agg * vectors, vectors), pl.ds(at, width)] = lower[site]
        images = dot(jnp.concatenate(mats, axis=0), jnp.concatenate(plain + crossed, axis=0), ROW_DIMS)
        own = images[:half]
        for pair in range(1, aggs // 2):
            own = jnp.where(owner == pair, images[pair * half : (pair + 1) * half], own)
        own = own.astype(jnp.bfloat16)
        right_ref[pl.ds(at, half), :] = own
        right_ref[pl.ds(at + half, half), :] = jnp.concatenate([own[:, lanes:], -own[:, :lanes]], axis=1)


def adjoint_item(links, lower, slot, left_ref):
    sites, vectors, width = lower.shape
    half = width // 2
    low = lower_half((vectors, width))
    sign = signs((vectors, width), jnp.float32)
    zero = jnp.zeros((vectors, width), jnp.bfloat16)
    for agg in range(sites // SIDE):
        rows = []
        mats = []
        for pair in range(SIDE // 2):
            at = agg * SIDE + 2 * pair
            lo_a, lo_b = lower[at], lower[at + 1]
            rows += [
                jnp.where(low, lo_a, zero),
                jnp.where(low, swapped(lo_a), zero),
                jnp.where(low, zero, swapped(lo_b)),
                jnp.where(low, zero, lo_b),
            ]
            mats.append(jnp.concatenate([links[at], links[at + 1]], axis=0))
        prod = dot(jnp.concatenate(rows, axis=0), jnp.concatenate(mats, axis=1), MAT_DIMS)
        for part in range(SIDE):
            top = part * 2 * vectors
            mine = prod[top : top + 2 * vectors, part // 2 * width : (part // 2 + 1) * width]
            adj = sign * mine[:vectors] + swapped(mine[vectors:])
            left_ref[pl.ds(agg * vectors, vectors), pl.ds((slot * SIDE + part) * width, width)] = adj.astype(jnp.bfloat16)


def group_rows(left, right, dims, vectors):
    full = dot(left, right, dims)
    total = full.shape[1] // 2
    aggs = total // vectors
    lanes = lax.broadcasted_iota(jnp.int32, (vectors, 2 * total), 1) // vectors % aggs
    own = full[:vectors]
    for agg in range(1, aggs):
        own = jnp.where(lanes == agg, full[agg * vectors : (agg + 1) * vectors], own)
    pieces = []
    lane_group = lax.broadcasted_iota(jnp.int32, (aggs, total), 1) // vectors
    sub = lax.broadcasted_iota(jnp.int32, (aggs, total), 0)
    for piece in range(2 * vectors // aggs):
        part, row = divmod(piece * aggs, vectors)
        value = own[row : row + aggs, part * total : (part + 1) * total]
        step = 1
        while step < aggs:
            sub_bit = (sub // step) % 2
            lane_bit = (lane_group // step) % 2
            up = pltpu.roll(pltpu.roll(value, aggs - step, axis=0), step * vectors, axis=1)
            down = pltpu.roll(pltpu.roll(value, step, axis=0), total - step * vectors, axis=1)
            value = jnp.where(sub_bit == lane_bit, value, jnp.where(sub_bit == 0, up, down))
            step *= 2
        pieces.append(value)
    return jnp.concatenate(pieces, axis=1)


def slice_kernel(nulls, *refs, sources):
    edges, sems = refs[:-1], refs[-1]
    copies = []
    for edge, (start, count, at, space) in zip(edges, sources):
        for row in range(count):
            source = nulls.at[pl.ds(start + row, 1), pl.ds(at, space)]
            copies.append(pltpu.make_async_copy(source, edge.at[pl.ds(row, 1)], sems.at[len(copies)]))
    for copy in copies:
        copy.start()
    for copy in copies:
        copy.wait()


def choose_rows(place, lists, picks):
    me = place[0]
    shards, cap = lists.shape
    count = picks.shape[2] // 2
    lane = lax.broadcasted_iota(jnp.int32, (MOST, cap), 1)
    want = lax.broadcasted_iota(jnp.int32, (MOST, cap), 0)
    column = lax.broadcasted_iota(jnp.int32, (MOST, 2 * count), 1)
    quarter = count // 4
    inside = column % count
    turned = (inside // quarter % 2) * 2 * quarter + (inside // (2 * quarter)) * quarter + inside % quarter
    own_column = column < count
    side = lax.rem(me, 2)
    for turn in range(shards // 2):
        owner = 2 * jnp.bitwise_xor(me // 2, turn) + side
        mine = jnp.broadcast_to(lists[pl.ds(owner, 1), :], (MOST, cap))
        for parity in range(2):
            source = me - side + parity
            before = jnp.where((mine >= 0) & (mine < source * count), 1, 0)
            start = jnp.sum(before.astype(jnp.float32), axis=1, keepdims=True).astype(jnp.int32)
            match = (mine >= source * count) & (mine < (source + 1) * count) & (lane - start == want)
            chosen = jnp.sum(jnp.where(match, mine - source * count + 1, 0).astype(jnp.float32), axis=1, keepdims=True)
            chosen = chosen.astype(jnp.int32) - 1
            here = own_column == (side == parity)
            rows = pl.ds((2 * turn + parity) * MOST, MOST)
            picks[0, rows, :] = jnp.where(here & (inside == chosen), 1.0, 0.0)
            picks[1, rows, :] = jnp.where(here & (turned == chosen), 1.0, 0.0)


def inner_kernel(nulls, time_links, space_links, early, adjoint, links, vecs, left, right, sems):
    time_count, space_count, sites, vectors, width = nulls.shape
    copies = []
    bases = [pltpu.make_async_copy(nulls.at[t], vecs.at[t], sems.at[16 + t]) for t in range(4)]
    bases[1].start()
    bases[2].start()

    def fetch(source):
        slot = len(copies)
        copy = pltpu.make_async_copy(source, links.at[slot], sems.at[slot])
        copy.start()
        copies.append(copy)

    for x in range(4):
        fetch(time_links.at[0, x])
    bases[0].start()
    bases[3].start()
    for t in range(4):
        fetch(space_links.at[t, 0])
    for x in range(4):
        fetch(time_links.at[1, x])
    for t in range(4):
        fetch(space_links.at[t, 1])
    bases[1].wait()
    bases[2].wait()
    for a_x in range(2):
        copies[2 * a_x].wait()
        copies[2 * a_x + 1].wait()
        for c in range(2):
            x = 2 * a_x + c
            image_item(links.at[x], vecs.at[1, x], vecs.at[2, x], c, left.at[a_x], right.at[a_x])
    bases[0].wait()
    bases[3].wait()
    for a_t in range(2):
        copies[4 + 2 * a_t].wait()
        copies[5 + 2 * a_t].wait()
        for c in range(2):
            t = 2 * a_t + c
            image_item(links.at[4 + t], vecs.at[t, 1], vecs.at[t, 2], c, left.at[2 + a_t], right.at[2 + a_t])
    found = [group_rows(left[group], right[group], MAT_DIMS, vectors) for group in range(4)]
    early[...] = jnp.concatenate(found, axis=0).astype(jnp.bfloat16)
    for x in range(4):
        copies[8 + x].wait()
    for x in range(4):
        adjoint_item(links.at[8 + x], vecs.at[3, x], x % 2, adjoint.at[x // 2])
    for t in range(4):
        copies[12 + t].wait()
    for t in range(4):
        adjoint_item(links.at[12 + t], vecs.at[t, 3], t % 2, adjoint.at[2 + t // 2])


def edge_rows(uppers, adjoint, vectors):
    width = uppers[0].shape[-1]
    sign = signs((vectors, width), jnp.bfloat16)
    parts = []
    for upper in uppers:
        sites = upper.shape[0]
        for site in range(SIDE):
            rows = [upper[agg * SIDE + site] for agg in range(sites // SIDE)]
            turned = [sign * swapped(row) for row in rows]
            parts.append(jnp.concatenate(rows + turned, axis=0))
    return group_rows(adjoint, jnp.concatenate(parts, axis=1), ROW_DIMS, vectors)


def middle_kernel(place, lists, space_edge, time_first, time_second, adjoint, found, picks):
    choose_rows(place, lists, picks)
    vectors = space_edge.shape[3]
    rows = []
    for a_x, time_edge in enumerate((time_first, time_second)):
        uppers = [time_edge.at[0, c] for c in range(2)]
        rows.append(edge_rows(uppers, adjoint[a_x], vectors))
    rows.append(edge_rows([space_edge.at[c, 0] for c in range(2)], adjoint[2], vectors))
    found[...] = jnp.concatenate(rows, axis=0)


def final_kernel(space_edge, adjoint, found, late):
    vectors = space_edge.shape[3]
    rows = edge_rows([space_edge.at[c, 0] for c in range(2)], adjoint[3], vectors)
    late[...] = jnp.concatenate([found[...], rows], axis=0).astype(jnp.bfloat16)


def pack_kernel(picks, early, early_other, late, late_other, *packed):
    half_count = late.shape[0] // 2
    pieces = (early, late, early_other, late_other)
    for half, width in enumerate((late.shape[1],) * 2):
        rows = jnp.concatenate([piece[pl.ds(half * half_count, half_count), :] for piece in pieces], axis=0)
        sent = dot(picks[half].astype(jnp.bfloat16), rows, MAT_DIMS)
        for turn, out in enumerate(packed):
            mine = sent[turn * 2 * MOST : (turn + 1) * 2 * MOST]
            out[:, pl.ds(half * width, width)] = mine.astype(jnp.bfloat16)


def unpack_kernel(place, *refs, turns):
    pair = place[0] // 2
    result, rows, sems = refs[-3:]
    copies = []
    for slot, turn in enumerate(turns):
        source = jnp.bitwise_xor(pair, turn)
        rows[slot] = refs[slot][...].astype(jnp.float32)
        target = result.at[pl.ds(pl.multiple_of(source * 2 * MOST, 2 * MOST), 2 * MOST)]
        copies.append(pltpu.make_async_copy(rows.at[slot], target, sems.at[slot]))
        copies[-1].start()
    for copy in copies:
        copy.wait()


def on_device(nulls, time_links, space_links, owner_lists):
    time_count, space_count, sites, vectors, width = nulls.shape
    shards, cap = owner_lists.shape
    aggs = sites // SIDE
    local_count = (time_count // 2) * (space_count // 2) * aggs
    wide = 2 * vectors * vectors
    place = lax.axis_index("xyz").astype(jnp.int32).reshape(1)
    vmem = pl.BlockSpec(memory_space=pltpu.VMEM)
    smem = pl.BlockSpec(memory_space=pltpu.SMEM)
    anywhere = pl.BlockSpec(memory_space=pl.ANY)
    outside = pl.BlockSpec(memory_space=pltpu.HBM)
    half = width // 2
    roomy = pltpu.CompilerParams(vmem_limit_bytes=51 * 1024 * 1024)
    modest = pltpu.CompilerParams(vmem_limit_bytes=24 * 1024 * 1024)
    first = pltpu.CompilerParams(vmem_limit_bytes=52 * 1024 * 1024)
    tiny = pl.CostEstimate(flops=1000, bytes_accessed=1000, transcendentals=0)
    half_time = time_count // 2

    def sliced(name, *sources):
        shapes = [(count, space, sites, vectors, width) for _, count, _, space in sources]
        return pl.pallas_call(
            functools.partial(slice_kernel, sources=sources),
            in_specs=[outside],
            out_specs=[vmem] * len(sources),
            out_shape=[jax.ShapeDtypeStruct(shape, nulls.dtype) for shape in shapes],
            scratch_shapes=[pltpu.SemaphoreType.DMA((sum(source[1] for source in sources),))],
            compiler_params=first,
            cost_estimate=tiny,
            name=name,
        )(nulls)

    half_space = space_count // 2
    (space_first,) = sliced("slice_first", (0, half_time, 0, 1))
    space_second, time_first, time_second = sliced(
        "slice_rest", (half_time, half_time, 0, 1), (0, 1, 0, half_space), (0, 1, half_space, half_space)
    )
    edge_first = shifted(space_first, "xyz", -1)
    edge_times = [shifted(time_first, "ta", -1), shifted(time_second, "ta", -1)]
    edge_second = shifted(space_second, "xyz", -1)
    early, adjoint = pl.pallas_call(
        inner_kernel,
        in_specs=[outside] * 3,
        out_specs=[vmem] * 2,
        out_shape=[
            jax.ShapeDtypeStruct((4 * aggs, wide), jnp.bfloat16),
            jax.ShapeDtypeStruct((4, vectors * aggs, 8 * width), jnp.bfloat16),
        ],
        scratch_shapes=[
            pltpu.VMEM((16, sites, half, width), jnp.bfloat16),
            pltpu.VMEM(nulls.shape, nulls.dtype),
            pltpu.VMEM((4, vectors * aggs, 8 * width), jnp.bfloat16),
            pltpu.VMEM((4, 8 * width, 2 * vectors * aggs), jnp.bfloat16),
            pltpu.SemaphoreType.DMA((20,)),
        ],
        compiler_params=roomy,
        cost_estimate=tiny,
        name="inner",
    )(nulls, time_links, space_links)
    found, picks = pl.pallas_call(
        middle_kernel,
        in_specs=[smem] + [vmem] * 5,
        out_specs=[vmem] * 2,
        out_shape=[
            jax.ShapeDtypeStruct((3 * aggs, wide), jnp.float32),
            jax.ShapeDtypeStruct((2, shards * MOST, 2 * local_count), jnp.float32),
        ],
        compiler_params=modest,
        cost_estimate=tiny,
        name="middle",
    )(place, owner_lists, edge_first, *edge_times, adjoint)
    late = pl.pallas_call(
        final_kernel,
        in_specs=[vmem] * 3,
        out_specs=vmem,
        out_shape=jax.ShapeDtypeStruct((4 * aggs, wide), jnp.bfloat16),
        compiler_params=modest,
        cost_estimate=tiny,
        name="final",
    )(edge_second, adjoint, found)
    early_other = crossed(early, "xyz", 1)
    late_other = crossed(late, "xyz", 1)
    pairs = shards // 2
    packed = pl.pallas_call(
        pack_kernel,
        in_specs=[vmem] * 5,
        out_specs=[vmem] * pairs,
        out_shape=[jax.ShapeDtypeStruct((2 * MOST, 2 * wide), jnp.bfloat16)] * pairs,
        compiler_params=modest,
        cost_estimate=tiny,
        name="pack",
    )(picks, early, early_other, late, late_other)
    turns = list(range(2, pairs)) + [1]
    arrived = [crossed(packed[turn], "xyz", 2 * turn) for turn in turns]
    arrived = pl.pallas_call(
        functools.partial(unpack_kernel, turns=turns + [0]),
        in_specs=[smem] + [vmem] * pairs,
        out_specs=outside,
        out_shape=jax.ShapeDtypeStruct((shards * MOST, 2 * wide), jnp.float32),
        scratch_shapes=[
            pltpu.VMEM((pairs, 2 * MOST, 2 * wide), jnp.float32),
            pltpu.SemaphoreType.DMA((pairs,)),
        ],
        compiler_params=modest,
        cost_estimate=tiny,
        name="unpack",
    )(place, *arrived, packed[0])
    if shards * MOST == cap:
        result = arrived
    else:
        my_list = lax.dynamic_index_in_dim(owner_lists, lax.axis_index("xyz"), 0, keepdims=False)
        source = jnp.maximum(my_list, 0) // local_count
        order = jnp.arange(cap, dtype=jnp.int32)
        same = (source[:, None] == source[None, :]) & (order[None, :] < order[:, None])
        offset = jnp.sum(same.astype(jnp.int32), axis=1)
        picked = arrived[source * MOST + offset]
        result = jnp.where((my_list >= 0)[:, None], picked, 0.0)
    return result[None]


def solution(mesh):
    return jax.shard_map(
        on_device,
        mesh=mesh,
        in_specs=(
            P("ta", "xyz", None, None, None),
            P("ta", "xyz", None, None, None),
            P("ta", "xyz", None, None, None),
            P(),
        ),
        out_specs=P("ta", "xyz", None),
        check_vma=False,
    )
```

```python
import functools

import jax
import jax.numpy as jnp
from jax import lax
from jax.experimental import pallas as pl
from jax.experimental.pallas import tpu as pltpu
from jax.sharding import PartitionSpec as P

ROW_DIMS = (((1,), (1,)), ((), ()))
MAT_DIMS = (((1,), (0,)), ((), ()))
SIDE = 4
MOST = 8


def shifted(array, axis, by):
    count = lax.axis_size(axis)
    return lax.ppermute(array, axis, [(i, (i + by) % count) for i in range(count)])


def crossed(array, axis, bits):
    return lax.ppermute(array, axis, [(i, i ^ bits) for i in range(lax.axis_size(axis))])


def dot(left, right, dims):
    return lax.dot_general(left, right, dims, preferred_element_type=jnp.float32)


def swapped(array):
    return pltpu.roll(array, array.shape[-1] // 2, axis=array.ndim - 1)


def lower_half(shape):
    return lax.broadcasted_iota(jnp.int32, shape, len(shape) - 1) < shape[-1] // 2


def signs(shape, dtype):
    return jnp.where(lower_half(shape), 1.0, -1.0).astype(dtype)


def image_item(links, lower, upper, slot, left_ref, right_ref):
    sites, vectors, width = lower.shape
    half = width // 2
    aggs = sites // SIDE
    lanes = aggs * vectors
    sign = signs((vectors, width), jnp.bfloat16)
    zero = jnp.zeros((vectors, width), jnp.bfloat16)
    owner = lax.broadcasted_iota(jnp.int32, (half, 2 * lanes), 1) // (2 * vectors) % (aggs // 2)
    for part in range(SIDE):
        at = (slot * SIDE + part) * width
        mats = []
        plain, crossed = [], []
        for agg in range(aggs):
            site = agg * SIDE + part
            up = upper[site]
            pair = (up * sign, swapped(up))
            for rows, value in zip((plain, crossed), pair):
                rows.append(jnp.concatenate([value, zero] if agg % 2 == 0 else [zero, value], axis=1))
            if agg % 2 == 0:
                mats.append(jnp.concatenate([links[site], links[site + SIDE]], axis=1))
            left_ref[pl.ds(agg * vectors, vectors), pl.ds(at, width)] = lower[site]
        images = dot(jnp.concatenate(mats, axis=0), jnp.concatenate(plain + crossed, axis=0), ROW_DIMS)
        own = images[:half]
        for pair in range(1, aggs // 2):
            own = jnp.where(owner == pair, images[pair * half : (pair + 1) * half], own)
        own = own.astype(jnp.bfloat16)
        right_ref[pl.ds(at, half), :] = own
        right_ref[pl.ds(at + half, half), :] = jnp.concatenate([own[:, lanes:], -own[:, :lanes]], axis=1)


def adjoint_item(links, lower, slot, left_ref):
    sites, vectors, width = lower.shape
    half = width // 2
    low = lower_half((vectors, width))
    sign = signs((vectors, width), jnp.float32)
    zero = jnp.zeros((vectors, width), jnp.bfloat16)
    for agg in range(sites // SIDE):
        rows = []
        mats = []
        for pair in range(SIDE // 2):
            at = agg * SIDE + 2 * pair
            lo_a, lo_b = lower[at], lower[at + 1]
            rows += [
                jnp.where(low, lo_a, zero),
                jnp.where(low, swapped(lo_a), zero),
                jnp.where(low, zero, swapped(lo_b)),
                jnp.where(low, zero, lo_b),
            ]
            mats.append(jnp.concatenate([links[at], links[at + 1]], axis=0))
        prod = dot(jnp.concatenate(rows, axis=0), jnp.concatenate(mats, axis=1), MAT_DIMS)
        for part in range(SIDE):
            top = part * 2 * vectors
            mine = prod[top : top + 2 * vectors, part // 2 * width : (part // 2 + 1) * width]
            adj = sign * mine[:vectors] + swapped(mine[vectors:])
            left_ref[pl.ds(agg * vectors, vectors), pl.ds((slot * SIDE + part) * width, width)] = adj.astype(jnp.bfloat16)


def group_rows(left, right, dims, vectors):
    full = dot(left, right, dims)
    total = full.shape[1] // 2
    aggs = total // vectors
    lanes = lax.broadcasted_iota(jnp.int32, (vectors, 2 * total), 1) // vectors % aggs
    own = full[:vectors]
    for agg in range(1, aggs):
        own = jnp.where(lanes == agg, full[agg * vectors : (agg + 1) * vectors], own)
    pieces = []
    lane_group = lax.broadcasted_iota(jnp.int32, (aggs, total), 1) // vectors
    sub = lax.broadcasted_iota(jnp.int32, (aggs, total), 0)
    for piece in range(2 * vectors // aggs):
        part, row = divmod(piece * aggs, vectors)
        value = own[row : row + aggs, part * total : (part + 1) * total]
        step = 1
        while step < aggs:
            sub_bit = (sub // step) % 2
            lane_bit = (lane_group // step) % 2
            up = pltpu.roll(pltpu.roll(value, aggs - step, axis=0), step * vectors, axis=1)
            down = pltpu.roll(pltpu.roll(value, step, axis=0), total - step * vectors, axis=1)
            value = jnp.where(sub_bit == lane_bit, value, jnp.where(sub_bit == 0, up, down))
            step *= 2
        pieces.append(value)
    return jnp.concatenate(pieces, axis=1)


def slice_kernel(nulls, *refs, sources):
    edges, sems = refs[:-1], refs[-1]
    copies = []
    for edge, (start, count, at, space) in zip(edges, sources):
        quarter = edge.shape[2] // 4
        for row in range(count):
            for part in range(4):
                span = pl.ds(part * quarter, quarter)
                source = nulls.at[pl.ds(start + row, 1), pl.ds(at, space), span]
                target = edge.at[pl.ds(row, 1), :, span]
                copies.append(pltpu.make_async_copy(source, target, sems.at[len(copies)]))
    for copy in copies:
        copy.start()
    for copy in copies:
        copy.wait()


def choose_rows(place, lists, picks):
    me = place[0]
    shards, cap = lists.shape
    count = picks.shape[2] // 2
    lane = lax.broadcasted_iota(jnp.int32, (MOST, cap), 1)
    want = lax.broadcasted_iota(jnp.int32, (MOST, cap), 0)
    column = lax.broadcasted_iota(jnp.int32, (MOST, 2 * count), 1)
    quarter = count // 4
    inside = column % count
    turned = (inside // quarter % 2) * 2 * quarter + (inside // (2 * quarter)) * quarter + inside % quarter
    own_column = column < count
    side = lax.rem(me, 2)
    for turn in range(shards // 2):
        owner = 2 * jnp.bitwise_xor(me // 2, turn) + side
        mine = jnp.broadcast_to(lists[pl.ds(owner, 1), :], (MOST, cap))
        for parity in range(2):
            source = me - side + parity
            before = jnp.where((mine >= 0) & (mine < source * count), 1, 0)
            start = jnp.sum(before.astype(jnp.float32), axis=1, keepdims=True).astype(jnp.int32)
            match = (mine >= source * count) & (mine < (source + 1) * count) & (lane - start == want)
            chosen = jnp.sum(jnp.where(match, mine - source * count + 1, 0).astype(jnp.float32), axis=1, keepdims=True)
            chosen = chosen.astype(jnp.int32) - 1
            here = own_column == (side == parity)
            rows = pl.ds((2 * turn + parity) * MOST, MOST)
            picks[0, rows, :] = jnp.where(here & (inside == chosen), 1.0, 0.0)
            picks[1, rows, :] = jnp.where(here & (turned == chosen), 1.0, 0.0)


def inner_kernel(nulls, time_links, space_links, early, adjoint, links, vecs, left, right, sems):
    time_count, space_count, sites, vectors, width = nulls.shape
    copies = []
    bases = [pltpu.make_async_copy(nulls.at[t], vecs.at[t], sems.at[16 + t]) for t in range(4)]
    bases[1].start()
    bases[2].start()

    def fetch(source):
        slot = len(copies)
        copy = pltpu.make_async_copy(source, links.at[slot], sems.at[slot])
        copy.start()
        copies.append(copy)

    for x in range(4):
        fetch(time_links.at[0, x])
    bases[0].start()
    bases[3].start()
    for t in range(4):
        fetch(space_links.at[t, 0])
    for x in range(4):
        fetch(time_links.at[1, x])
    for t in range(4):
        fetch(space_links.at[t, 1])
    bases[1].wait()
    bases[2].wait()
    for a_x in range(2):
        copies[2 * a_x].wait()
        copies[2 * a_x + 1].wait()
        for c in range(2):
            x = 2 * a_x + c
            image_item(links.at[x], vecs.at[1, x], vecs.at[2, x], c, left.at[a_x], right.at[a_x])
    bases[0].wait()
    bases[3].wait()
    for a_t in range(2):
        copies[4 + 2 * a_t].wait()
        copies[5 + 2 * a_t].wait()
        for c in range(2):
            t = 2 * a_t + c
            image_item(links.at[4 + t], vecs.at[t, 1], vecs.at[t, 2], c, left.at[2 + a_t], right.at[2 + a_t])
    found = [group_rows(left[group], right[group], MAT_DIMS, vectors) for group in range(4)]
    early[...] = jnp.concatenate(found, axis=0)
    for x in range(4):
        copies[8 + x].wait()
    for x in range(4):
        adjoint_item(links.at[8 + x], vecs.at[3, x], x % 2, adjoint.at[x // 2])
    for t in range(4):
        copies[12 + t].wait()
    for t in range(4):
        adjoint_item(links.at[12 + t], vecs.at[t, 3], t % 2, adjoint.at[2 + t // 2])


def edge_rows(uppers, adjoint, vectors):
    width = uppers[0].shape[-1]
    sign = signs((vectors, width), jnp.bfloat16)
    parts = []
    for upper in uppers:
        sites = upper.shape[0]
        for site in range(SIDE):
            rows = [upper[agg * SIDE + site] for agg in range(sites // SIDE)]
            turned = [sign * swapped(row) for row in rows]
            parts.append(jnp.concatenate(rows + turned, axis=0))
    return group_rows(adjoint, jnp.concatenate(parts, axis=1), ROW_DIMS, vectors)


def middle_kernel(place, lists, space_edge, time_first, time_second, adjoint, found, picks):
    choose_rows(place, lists, picks)
    vectors = space_edge.shape[3]
    rows = []
    for a_x, time_edge in enumerate((time_first, time_second)):
        uppers = [time_edge.at[0, c] for c in range(2)]
        rows.append(edge_rows(uppers, adjoint[a_x], vectors))
    rows.append(edge_rows([space_edge.at[c, 0] for c in range(2)], adjoint[2], vectors))
    found[...] = jnp.concatenate(rows, axis=0)


def final_kernel(space_edge, adjoint, early, found, late):
    vectors = space_edge.shape[3]
    rows = edge_rows([space_edge.at[c, 0] for c in range(2)], adjoint[3], vectors)
    late[...] = jnp.concatenate([early[...], found[...], rows], axis=0).astype(jnp.bfloat16)


def pack_kernel(picks, late, late_other, *packed):
    quarter, width = late.shape[0] // 4, late.shape[1]
    for half in range(2):
        spans = [pl.ds((half + 2 * part) * quarter, quarter) for part in range(2)]
        rows = jnp.concatenate([piece[span, :] for piece in (late, late_other) for span in spans], axis=0)
        sent = dot(picks[half].astype(jnp.bfloat16), rows, MAT_DIMS)
        for turn, out in enumerate(packed):
            mine = sent[turn * 2 * MOST : (turn + 1) * 2 * MOST]
            out[:, pl.ds(half * width, width)] = mine.astype(jnp.bfloat16)


def unpack_kernel(place, *refs, turns):
    pair = place[0] // 2
    result, rows, sems = refs[-3:]
    copies = []
    for slot, turn in enumerate(turns):
        source = jnp.bitwise_xor(pair, turn)
        rows[slot] = refs[slot][...].astype(jnp.float32)
        target = result.at[pl.ds(pl.multiple_of(source * 2 * MOST, 2 * MOST), 2 * MOST)]
        copies.append(pltpu.make_async_copy(rows.at[slot], target, sems.at[slot]))
        copies[-1].start()
    for copy in copies:
        copy.wait()


def on_device(nulls, time_links, space_links, owner_lists):
    time_count, space_count, sites, vectors, width = nulls.shape
    shards, cap = owner_lists.shape
    aggs = sites // SIDE
    local_count = (time_count // 2) * (space_count // 2) * aggs
    wide = 2 * vectors * vectors
    place = lax.axis_index("xyz").astype(jnp.int32).reshape(1)
    vmem = pl.BlockSpec(memory_space=pltpu.VMEM)
    smem = pl.BlockSpec(memory_space=pltpu.SMEM)
    anywhere = pl.BlockSpec(memory_space=pl.ANY)
    outside = pl.BlockSpec(memory_space=pltpu.HBM)
    half = width // 2
    roomy = pltpu.CompilerParams(vmem_limit_bytes=51 * 1024 * 1024)
    modest = pltpu.CompilerParams(vmem_limit_bytes=24 * 1024 * 1024)
    first = pltpu.CompilerParams(vmem_limit_bytes=52 * 1024 * 1024)
    tiny = pl.CostEstimate(flops=1000, bytes_accessed=1000, transcendentals=0)
    half_time = time_count // 2

    def sliced(name, *sources):
        shapes = [(count, space, sites, vectors, width) for _, count, _, space in sources]
        return pl.pallas_call(
            functools.partial(slice_kernel, sources=sources),
            in_specs=[outside],
            out_specs=[vmem] * len(sources),
            out_shape=[jax.ShapeDtypeStruct(shape, nulls.dtype) for shape in shapes],
            scratch_shapes=[pltpu.SemaphoreType.DMA((4 * sum(source[1] for source in sources),))],
            compiler_params=first,
            cost_estimate=tiny,
            name=name,
        )(nulls)

    half_space = space_count // 2
    (space_first,) = sliced("slice_first", (0, half_time, 0, 1))
    space_second, time_first, time_second = sliced(
        "slice_rest", (half_time, half_time, 0, 1), (0, 1, 0, half_space), (0, 1, half_space, half_space)
    )
    edge_first = shifted(space_first, "xyz", -1)
    edge_times = [shifted(time_first, "ta", -1), shifted(time_second, "ta", -1)]
    edge_second = shifted(space_second, "xyz", -1)
    early, adjoint = pl.pallas_call(
        inner_kernel,
        in_specs=[outside] * 3,
        out_specs=[vmem] * 2,
        out_shape=[
            jax.ShapeDtypeStruct((4 * aggs, wide), jnp.float32),
            jax.ShapeDtypeStruct((4, vectors * aggs, 8 * width), jnp.bfloat16),
        ],
        scratch_shapes=[
            pltpu.VMEM((16, sites, half, width), jnp.bfloat16),
            pltpu.VMEM(nulls.shape, nulls.dtype),
            pltpu.VMEM((4, vectors * aggs, 8 * width), jnp.bfloat16),
            pltpu.VMEM((4, 8 * width, 2 * vectors * aggs), jnp.bfloat16),
            pltpu.SemaphoreType.DMA((20,)),
        ],
        compiler_params=roomy,
        cost_estimate=tiny,
        name="inner",
    )(nulls, time_links, space_links)
    found, picks = pl.pallas_call(
        middle_kernel,
        in_specs=[smem] + [vmem] * 5,
        out_specs=[vmem] * 2,
        out_shape=[
            jax.ShapeDtypeStruct((3 * aggs, wide), jnp.float32),
            jax.ShapeDtypeStruct((2, shards * MOST, 2 * local_count), jnp.float32),
        ],
        compiler_params=modest,
        cost_estimate=tiny,
        name="middle",
    )(place, owner_lists, edge_first, *edge_times, adjoint)
    late = pl.pallas_call(
        final_kernel,
        in_specs=[vmem] * 4,
        out_specs=vmem,
        out_shape=jax.ShapeDtypeStruct((8 * aggs, wide), jnp.bfloat16),
        compiler_params=modest,
        cost_estimate=tiny,
        name="final",
    )(edge_second, adjoint, early, found)
    late_other = crossed(late, "xyz", 1)
    pairs = shards // 2
    packed = pl.pallas_call(
        pack_kernel,
        in_specs=[vmem] * 3,
        out_specs=[vmem] * pairs,
        out_shape=[jax.ShapeDtypeStruct((2 * MOST, 2 * wide), jnp.bfloat16)] * pairs,
        compiler_params=modest,
        cost_estimate=tiny,
        name="pack",
    )(picks, late, late_other)
    turns = list(range(2, pairs)) + [1]
    arrived = [crossed(packed[turn], "xyz", 2 * turn) for turn in turns]
    arrived = pl.pallas_call(
        functools.partial(unpack_kernel, turns=turns + [0]),
        in_specs=[smem] + [vmem] * pairs,
        out_specs=outside,
        out_shape=jax.ShapeDtypeStruct((shards * MOST, 2 * wide), jnp.float32),
        scratch_shapes=[
            pltpu.VMEM((pairs, 2 * MOST, 2 * wide), jnp.float32),
            pltpu.SemaphoreType.DMA((pairs,)),
        ],
        compiler_params=modest,
        cost_estimate=tiny,
        name="unpack",
    )(place, *arrived, packed[0])
    if shards * MOST == cap:
        result = arrived
    else:
        my_list = lax.dynamic_index_in_dim(owner_lists, lax.axis_index("xyz"), 0, keepdims=False)
        source = jnp.maximum(my_list, 0) // local_count
        order = jnp.arange(cap, dtype=jnp.int32)
        same = (source[:, None] == source[None, :]) & (order[None, :] < order[:, None])
        offset = jnp.sum(same.astype(jnp.int32), axis=1)
        picked = arrived[source * MOST + offset]
        result = jnp.where((my_list >= 0)[:, None], picked, 0.0)
    return result[None]


def solution(mesh):
    return jax.shard_map(
        on_device,
        mesh=mesh,
        in_specs=(
            P("ta", "xyz", None, None, None),
            P("ta", "xyz", None, None, None),
            P("ta", "xyz", None, None, None),
            P(),
        ),
        out_specs=P("ta", "xyz", None),
        check_vma=False,
    )
```

```python
import functools

import jax
import jax.numpy as jnp
from jax import lax
from jax.experimental import pallas as pl
from jax.experimental.pallas import tpu as pltpu
from jax.sharding import PartitionSpec as P

ROW_DIMS = (((1,), (1,)), ((), ()))
MAT_DIMS = (((1,), (0,)), ((), ()))
SIDE = 4
MOST = 8


def shifted(array, axis, by):
    count = lax.axis_size(axis)
    return lax.ppermute(array, axis, [(i, (i + by) % count) for i in range(count)])


def crossed(array, axis, bits):
    return lax.ppermute(array, axis, [(i, i ^ bits) for i in range(lax.axis_size(axis))])


def dot(left, right, dims):
    return lax.dot_general(left, right, dims, preferred_element_type=jnp.float32)


def swapped(array):
    return pltpu.roll(array, array.shape[-1] // 2, axis=array.ndim - 1)


def lower_half(shape):
    return lax.broadcasted_iota(jnp.int32, shape, len(shape) - 1) < shape[-1] // 2


def signs(shape, dtype):
    return jnp.where(lower_half(shape), 1.0, -1.0).astype(dtype)


def image_item(links, lower, upper, slot, left_ref, right_ref):
    sites, vectors, width = lower.shape
    half = width // 2
    aggs = sites // SIDE
    lanes = aggs * vectors
    sign = signs((vectors, width), jnp.bfloat16)
    zero = jnp.zeros((vectors, width), jnp.bfloat16)
    owner = lax.broadcasted_iota(jnp.int32, (half, 2 * lanes), 1) // (2 * vectors) % (aggs // 2)
    for part in range(SIDE):
        at = (slot * SIDE + part) * width
        mats = []
        plain, crossed = [], []
        for agg in range(aggs):
            site = agg * SIDE + part
            up = upper[site]
            pair = (up * sign, swapped(up))
            for rows, value in zip((plain, crossed), pair):
                rows.append(jnp.concatenate([value, zero] if agg % 2 == 0 else [zero, value], axis=1))
            if agg % 2 == 0:
                mats.append(jnp.concatenate([links[site], links[site + SIDE]], axis=1))
            left_ref[pl.ds(agg * vectors, vectors), pl.ds(at, width)] = lower[site]
        images = dot(jnp.concatenate(mats, axis=0), jnp.concatenate(plain + crossed, axis=0), ROW_DIMS)
        own = images[:half]
        for pair in range(1, aggs // 2):
            own = jnp.where(owner == pair, images[pair * half : (pair + 1) * half], own)
        own = own.astype(jnp.bfloat16)
        right_ref[pl.ds(at, half), :] = own
        right_ref[pl.ds(at + half, half), :] = jnp.concatenate([own[:, lanes:], -own[:, :lanes]], axis=1)


def adjoint_item(links, lower, slot, left_ref):
    sites, vectors, width = lower.shape
    half = width // 2
    low = lower_half((vectors, width))
    sign = signs((vectors, width), jnp.float32)
    zero = jnp.zeros((vectors, width), jnp.bfloat16)
    for agg in range(sites // SIDE):
        rows = []
        mats = []
        for pair in range(SIDE // 2):
            at = agg * SIDE + 2 * pair
            lo_a, lo_b = lower[at], lower[at + 1]
            rows += [
                jnp.where(low, lo_a, zero),
                jnp.where(low, swapped(lo_a), zero),
                jnp.where(low, zero, swapped(lo_b)),
                jnp.where(low, zero, lo_b),
            ]
            mats.append(jnp.concatenate([links[at], links[at + 1]], axis=0))
        prod = dot(jnp.concatenate(rows, axis=0), jnp.concatenate(mats, axis=1), MAT_DIMS)
        for part in range(SIDE):
            top = part * 2 * vectors
            mine = prod[top : top + 2 * vectors, part // 2 * width : (part // 2 + 1) * width]
            adj = sign * mine[:vectors] + swapped(mine[vectors:])
            left_ref[pl.ds(agg * vectors, vectors), pl.ds((slot * SIDE + part) * width, width)] = adj.astype(jnp.bfloat16)


def group_rows(left, right, dims, vectors):
    full = dot(left, right, dims)
    total = full.shape[1] // 2
    aggs = total // vectors
    lanes = lax.broadcasted_iota(jnp.int32, (vectors, 2 * total), 1) // vectors % aggs
    own = full[:vectors]
    for agg in range(1, aggs):
        own = jnp.where(lanes == agg, full[agg * vectors : (agg + 1) * vectors], own)
    pieces = []
    lane_group = lax.broadcasted_iota(jnp.int32, (aggs, total), 1) // vectors
    sub = lax.broadcasted_iota(jnp.int32, (aggs, total), 0)
    for piece in range(2 * vectors // aggs):
        part, row = divmod(piece * aggs, vectors)
        value = own[row : row + aggs, part * total : (part + 1) * total]
        step = 1
        while step < aggs:
            sub_bit = (sub // step) % 2
            lane_bit = (lane_group // step) % 2
            up = pltpu.roll(pltpu.roll(value, aggs - step, axis=0), step * vectors, axis=1)
            down = pltpu.roll(pltpu.roll(value, step, axis=0), total - step * vectors, axis=1)
            value = jnp.where(sub_bit == lane_bit, value, jnp.where(sub_bit == 0, up, down))
            step *= 2
        pieces.append(value)
    return jnp.concatenate(pieces, axis=1)


def slice_kernel(nulls, *refs, sources):
    edges, sems = refs[:-1], refs[-1]
    copies = []
    for edge, (start, count, at, space) in zip(edges, sources):
        for row in range(count):
            source = nulls.at[pl.ds(start + row, 1), pl.ds(at, space)]
            copies.append(pltpu.make_async_copy(source, edge.at[pl.ds(row, 1)], sems.at[len(copies)]))
    for copy in copies:
        copy.start()
    for copy in copies:
        copy.wait()


def choose_rows(place, lists, picks):
    me = place[0]
    shards, cap = lists.shape
    count = picks.shape[2] // 2
    lane = lax.broadcasted_iota(jnp.int32, (MOST, cap), 1)
    want = lax.broadcasted_iota(jnp.int32, (MOST, cap), 0)
    column = lax.broadcasted_iota(jnp.int32, (MOST, 2 * count), 1)
    quarter = count // 4
    inside = column % count
    turned = (inside // quarter % 2) * 2 * quarter + (inside // (2 * quarter)) * quarter + inside % quarter
    own_column = column < count
    side = lax.rem(me, 2)
    for turn in range(shards // 2):
        owner = 2 * jnp.bitwise_xor(me // 2, turn) + side
        mine = jnp.broadcast_to(lists[pl.ds(owner, 1), :], (MOST, cap))
        for parity in range(2):
            source = me - side + parity
            before = jnp.where((mine >= 0) & (mine < source * count), 1, 0)
            start = jnp.sum(before.astype(jnp.float32), axis=1, keepdims=True).astype(jnp.int32)
            match = (mine >= source * count) & (mine < (source + 1) * count) & (lane - start == want)
            chosen = jnp.sum(jnp.where(match, mine - source * count + 1, 0).astype(jnp.float32), axis=1, keepdims=True)
            chosen = chosen.astype(jnp.int32) - 1
            here = own_column == (side == parity)
            rows = pl.ds((2 * turn + parity) * MOST, MOST)
            picks[0, rows, :] = jnp.where(here & (inside == chosen), 1.0, 0.0)
            picks[1, rows, :] = jnp.where(here & (turned == chosen), 1.0, 0.0)


def inner_work(nulls, time_links, space_links, early, adjoint, links, vecs, left, right, sems):
    time_count, space_count, sites, vectors, width = nulls.shape
    copies = []
    bases = [pltpu.make_async_copy(nulls.at[t], vecs.at[t], sems.at[16 + t]) for t in range(4)]
    bases[1].start()
    bases[2].start()

    def fetch(source):
        slot = len(copies)
        copy = pltpu.make_async_copy(source, links.at[slot], sems.at[slot])
        copy.start()
        copies.append(copy)

    for x in range(4):
        fetch(time_links.at[0, x])
    bases[0].start()
    bases[3].start()
    for t in range(4):
        fetch(space_links.at[t, 0])
    for x in range(4):
        fetch(time_links.at[1, x])
    for t in range(4):
        fetch(space_links.at[t, 1])
    bases[1].wait()
    bases[2].wait()
    for a_x in range(2):
        copies[2 * a_x].wait()
        copies[2 * a_x + 1].wait()
        for c in range(2):
            x = 2 * a_x + c
            image_item(links.at[x], vecs.at[1, x], vecs.at[2, x], c, left.at[a_x], right.at[a_x])
    bases[0].wait()
    bases[3].wait()
    for a_t in range(2):
        copies[4 + 2 * a_t].wait()
        copies[5 + 2 * a_t].wait()
        for c in range(2):
            t = 2 * a_t + c
            image_item(links.at[4 + t], vecs.at[t, 1], vecs.at[t, 2], c, left.at[2 + a_t], right.at[2 + a_t])
    found = [group_rows(left[group], right[group], MAT_DIMS, vectors) for group in range(4)]
    early[...] = jnp.concatenate(found, axis=0).astype(jnp.bfloat16)
    for x in range(4):
        copies[8 + x].wait()
    for x in range(4):
        adjoint_item(links.at[8 + x], vecs.at[3, x], x % 2, adjoint.at[x // 2])
    for t in range(4):
        copies[12 + t].wait()
    for t in range(4):
        adjoint_item(links.at[12 + t], vecs.at[t, 3], t % 2, adjoint.at[2 + t // 2])


def before_kernel(group, nulls, time_links, space_links, edge, *refs):
    half = edge.shape[0]
    sem = refs[-1]
    copies = [
        pltpu.make_async_copy(nulls.at[pl.ds(half + row, 1), pl.ds(0, 1)], edge.at[pl.ds(row, 1)], sem.at[row])
        for row in range(half)
    ]
    for copy in copies:
        copy.start()

    @pl.when(lax.rem(group[0], 2) == 1)
    def _():
        inner_work(nulls, time_links, space_links, *refs[:-1])

    for copy in copies:
        copy.wait()


def after_kernel(group, nulls, time_links, space_links, early_before, adjoint_before, early, adjoint, *refs):
    @pl.when(lax.rem(group[0], 2) == 0)
    def _():
        inner_work(nulls, time_links, space_links, early, adjoint, *refs)

    @pl.when(lax.rem(group[0], 2) == 1)
    def _():
        early[...] = early_before[...]
        adjoint[...] = adjoint_before[...]


def edge_rows(uppers, adjoint, vectors):
    width = uppers[0].shape[-1]
    sign = signs((vectors, width), jnp.bfloat16)
    parts = []
    for upper in uppers:
        sites = upper.shape[0]
        for site in range(SIDE):
            rows = [upper[agg * SIDE + site] for agg in range(sites // SIDE)]
            turned = [sign * swapped(row) for row in rows]
            parts.append(jnp.concatenate(rows + turned, axis=0))
    return group_rows(adjoint, jnp.concatenate(parts, axis=1), ROW_DIMS, vectors)


def middle_kernel(place, lists, space_edge, time_first, time_second, adjoint, found, picks):
    choose_rows(place, lists, picks)
    vectors = space_edge.shape[3]
    rows = []
    for a_x, time_edge in enumerate((time_first, time_second)):
        uppers = [time_edge.at[0, c] for c in range(2)]
        rows.append(edge_rows(uppers, adjoint[a_x], vectors))
    rows.append(edge_rows([space_edge.at[c, 0] for c in range(2)], adjoint[2], vectors))
    found[...] = jnp.concatenate(rows, axis=0)


def final_kernel(space_edge, adjoint, found, late):
    vectors = space_edge.shape[3]
    rows = edge_rows([space_edge.at[c, 0] for c in range(2)], adjoint[3], vectors)
    late[...] = jnp.concatenate([found[...], rows], axis=0).astype(jnp.bfloat16)


def pack_kernel(picks, early, early_other, late, late_other, *packed):
    half_count = late.shape[0] // 2
    pieces = (early, late, early_other, late_other)
    for half, width in enumerate((late.shape[1],) * 2):
        rows = jnp.concatenate([piece[pl.ds(half * half_count, half_count), :] for piece in pieces], axis=0)
        sent = dot(picks[half].astype(jnp.bfloat16), rows, MAT_DIMS)
        for turn, out in enumerate(packed):
            mine = sent[turn * 2 * MOST : (turn + 1) * 2 * MOST]
            out[:, pl.ds(half * width, width)] = mine.astype(jnp.bfloat16)


def unpack_kernel(place, *refs, turns):
    pair = place[0] // 2
    result, rows, sems = refs[-3:]
    copies = []
    for slot, turn in enumerate(turns):
        source = jnp.bitwise_xor(pair, turn)
        rows[slot] = refs[slot][...].astype(jnp.float32)
        target = result.at[pl.ds(pl.multiple_of(source * 2 * MOST, 2 * MOST), 2 * MOST)]
        copies.append(pltpu.make_async_copy(rows.at[slot], target, sems.at[slot]))
        copies[-1].start()
    for copy in copies:
        copy.wait()


def on_device(nulls, time_links, space_links, owner_lists):
    time_count, space_count, sites, vectors, width = nulls.shape
    shards, cap = owner_lists.shape
    aggs = sites // SIDE
    local_count = (time_count // 2) * (space_count // 2) * aggs
    wide = 2 * vectors * vectors
    place = lax.axis_index("xyz").astype(jnp.int32).reshape(1)
    group = lax.axis_index("ta").astype(jnp.int32).reshape(1)
    vmem = pl.BlockSpec(memory_space=pltpu.VMEM)
    smem = pl.BlockSpec(memory_space=pltpu.SMEM)
    anywhere = pl.BlockSpec(memory_space=pl.ANY)
    outside = pl.BlockSpec(memory_space=pltpu.HBM)
    half = width // 2
    roomy = pltpu.CompilerParams(vmem_limit_bytes=51 * 1024 * 1024)
    modest = pltpu.CompilerParams(vmem_limit_bytes=24 * 1024 * 1024)
    first = pltpu.CompilerParams(vmem_limit_bytes=52 * 1024 * 1024)
    tiny = pl.CostEstimate(flops=1000, bytes_accessed=1000, transcendentals=0)
    half_time = time_count // 2

    def sliced(name, *sources):
        shapes = [(count, space, sites, vectors, width) for _, count, _, space in sources]
        return pl.pallas_call(
            functools.partial(slice_kernel, sources=sources),
            in_specs=[outside],
            out_specs=[vmem] * len(sources),
            out_shape=[jax.ShapeDtypeStruct(shape, nulls.dtype) for shape in shapes],
            scratch_shapes=[pltpu.SemaphoreType.DMA((sum(source[1] for source in sources),))],
            compiler_params=first,
            cost_estimate=tiny,
            name=name,
        )(nulls)

    half_space = space_count // 2
    space_first, time_first, time_second = sliced(
        "slices", (0, half_time, 0, 1), (0, 1, 0, half_space), (0, 1, half_space, half_space)
    )
    edge_first = shifted(space_first, "xyz", -1)
    edge_times = [shifted(time_first, "ta", -1), shifted(time_second, "ta", -1)]
    inner_out = [
        jax.ShapeDtypeStruct((4 * aggs, wide), jnp.bfloat16),
        jax.ShapeDtypeStruct((4, vectors * aggs, 8 * width), jnp.bfloat16),
    ]
    inner_scratch = [
        pltpu.VMEM((16, sites, half, width), jnp.bfloat16),
        pltpu.VMEM(nulls.shape, nulls.dtype),
        pltpu.VMEM((4, vectors * aggs, 8 * width), jnp.bfloat16),
        pltpu.VMEM((4, 8 * width, 2 * vectors * aggs), jnp.bfloat16),
        pltpu.SemaphoreType.DMA((20,)),
    ]
    space_second, early_one, adjoint_one = pl.pallas_call(
        before_kernel,
        in_specs=[smem] + [outside] * 3,
        out_specs=[vmem] * 3,
        out_shape=[jax.ShapeDtypeStruct(space_first.shape, nulls.dtype)] + inner_out,
        scratch_shapes=inner_scratch + [pltpu.SemaphoreType.DMA((half_time,))],
        compiler_params=roomy,
        cost_estimate=tiny,
        name="before",
    )(group, nulls, time_links, space_links)
    edge_second = shifted(space_second, "xyz", -1)
    early, adjoint = pl.pallas_call(
        after_kernel,
        in_specs=[smem] + [outside] * 3 + [vmem] * 2,
        out_specs=[vmem] * 2,
        out_shape=inner_out,
        scratch_shapes=inner_scratch,
        compiler_params=roomy,
        cost_estimate=tiny,
        name="after",
    )(group, nulls, time_links, space_links, early_one, adjoint_one)
    found, picks = pl.pallas_call(
        middle_kernel,
        in_specs=[smem] + [vmem] * 5,
        out_specs=[vmem] * 2,
        out_shape=[
            jax.ShapeDtypeStruct((3 * aggs, wide), jnp.float32),
            jax.ShapeDtypeStruct((2, shards * MOST, 2 * local_count), jnp.float32),
        ],
        compiler_params=modest,
        cost_estimate=tiny,
        name="middle",
    )(place, owner_lists, edge_first, *edge_times, adjoint)
    late = pl.pallas_call(
        final_kernel,
        in_specs=[vmem] * 3,
        out_specs=vmem,
        out_shape=jax.ShapeDtypeStruct((4 * aggs, wide), jnp.bfloat16),
        compiler_params=modest,
        cost_estimate=tiny,
        name="final",
    )(edge_second, adjoint, found)
    early_other = crossed(early, "xyz", 1)
    late_other = crossed(late, "xyz", 1)
    pairs = shards // 2
    packed = pl.pallas_call(
        pack_kernel,
        in_specs=[vmem] * 5,
        out_specs=[vmem] * pairs,
        out_shape=[jax.ShapeDtypeStruct((2 * MOST, 2 * wide), jnp.bfloat16)] * pairs,
        compiler_params=modest,
        cost_estimate=tiny,
        name="pack",
    )(picks, early, early_other, late, late_other)
    turns = list(range(2, pairs)) + [1]
    arrived = [crossed(packed[turn], "xyz", 2 * turn) for turn in turns]
    arrived = pl.pallas_call(
        functools.partial(unpack_kernel, turns=turns + [0]),
        in_specs=[smem] + [vmem] * pairs,
        out_specs=outside,
        out_shape=jax.ShapeDtypeStruct((shards * MOST, 2 * wide), jnp.float32),
        scratch_shapes=[
            pltpu.VMEM((pairs, 2 * MOST, 2 * wide), jnp.float32),
            pltpu.SemaphoreType.DMA((pairs,)),
        ],
        compiler_params=modest,
        cost_estimate=tiny,
        name="unpack",
    )(place, *arrived, packed[0])
    if shards * MOST == cap:
        result = arrived
    else:
        my_list = lax.dynamic_index_in_dim(owner_lists, lax.axis_index("xyz"), 0, keepdims=False)
        source = jnp.maximum(my_list, 0) // local_count
        order = jnp.arange(cap, dtype=jnp.int32)
        same = (source[:, None] == source[None, :]) & (order[None, :] < order[:, None])
        offset = jnp.sum(same.astype(jnp.int32), axis=1)
        picked = arrived[source * MOST + offset]
        result = jnp.where((my_list >= 0)[:, None], picked, 0.0)
    return result[None]


def solution(mesh):
    return jax.shard_map(
        on_device,
        mesh=mesh,
        in_specs=(
            P("ta", "xyz", None, None, None),
            P("ta", "xyz", None, None, None),
            P("ta", "xyz", None, None, None),
            P(),
        ),
        out_specs=P("ta", "xyz", None),
        check_vma=False,
    )
```

```python
import functools

import jax
import jax.numpy as jnp
from jax import lax
from jax.experimental import pallas as pl
from jax.experimental.pallas import tpu as pltpu
from jax.sharding import PartitionSpec as P

ROW_DIMS = (((1,), (1,)), ((), ()))
MAT_DIMS = (((1,), (0,)), ((), ()))
SIDE = 4
MOST = 8


def shifted(array, axis, by):
    count = lax.axis_size(axis)
    return lax.ppermute(array, axis, [(i, (i + by) % count) for i in range(count)])


def crossed(array, axis, bits):
    return lax.ppermute(array, axis, [(i, i ^ bits) for i in range(lax.axis_size(axis))])


def dot(left, right, dims):
    return lax.dot_general(left, right, dims, preferred_element_type=jnp.float32)


def swapped(array):
    return pltpu.roll(array, array.shape[-1] // 2, axis=array.ndim - 1)


def lower_half(shape):
    return lax.broadcasted_iota(jnp.int32, shape, len(shape) - 1) < shape[-1] // 2


def signs(shape, dtype):
    return jnp.where(lower_half(shape), 1.0, -1.0).astype(dtype)


def image_item(links, lower, upper, slot, left_ref, right_ref):
    sites, vectors, width = lower.shape
    half = width // 2
    aggs = sites // SIDE
    lanes = aggs * vectors
    sign = signs((vectors, width), jnp.bfloat16)
    zero = jnp.zeros((vectors, width), jnp.bfloat16)
    owner = lax.broadcasted_iota(jnp.int32, (half, 2 * lanes), 1) // (2 * vectors) % (aggs // 2)
    for part in range(SIDE):
        at = (slot * SIDE + part) * width
        mats = []
        plain, crossed = [], []
        for agg in range(aggs):
            site = agg * SIDE + part
            up = upper[site]
            pair = (up * sign, swapped(up))
            for rows, value in zip((plain, crossed), pair):
                rows.append(jnp.concatenate([value, zero] if agg % 2 == 0 else [zero, value], axis=1))
            if agg % 2 == 0:
                mats.append(jnp.concatenate([links[site], links[site + SIDE]], axis=1))
            left_ref[pl.ds(agg * vectors, vectors), pl.ds(at, width)] = lower[site]
        images = dot(jnp.concatenate(mats, axis=0), jnp.concatenate(plain + crossed, axis=0), ROW_DIMS)
        own = images[:half]
        for pair in range(1, aggs // 2):
            own = jnp.where(owner == pair, images[pair * half : (pair + 1) * half], own)
        own = own.astype(jnp.bfloat16)
        right_ref[pl.ds(at, half), :] = own
        right_ref[pl.ds(at + half, half), :] = jnp.concatenate([own[:, lanes:], -own[:, :lanes]], axis=1)


def adjoint_item(links, lower, slot, left_ref):
    sites, vectors, width = lower.shape
    half = width // 2
    low = lower_half((vectors, width))
    sign = signs((vectors, width), jnp.float32)
    zero = jnp.zeros((vectors, width), jnp.bfloat16)
    for agg in range(sites // SIDE):
        rows = []
        mats = []
        for pair in range(SIDE // 2):
            at = agg * SIDE + 2 * pair
            lo_a, lo_b = lower[at], lower[at + 1]
            rows += [
                jnp.where(low, lo_a, zero),
                jnp.where(low, swapped(lo_a), zero),
                jnp.where(low, zero, swapped(lo_b)),
                jnp.where(low, zero, lo_b),
            ]
            mats.append(jnp.concatenate([links[at], links[at + 1]], axis=0))
        prod = dot(jnp.concatenate(rows, axis=0), jnp.concatenate(mats, axis=1), MAT_DIMS)
        for part in range(SIDE):
            top = part * 2 * vectors
            mine = prod[top : top + 2 * vectors, part // 2 * width : (part // 2 + 1) * width]
            adj = sign * mine[:vectors] + swapped(mine[vectors:])
            left_ref[pl.ds(agg * vectors, vectors), pl.ds((slot * SIDE + part) * width, width)] = adj.astype(jnp.bfloat16)


def group_rows(left, right, dims, vectors):
    full = dot(left, right, dims)
    total = full.shape[1] // 2
    aggs = total // vectors
    lanes = lax.broadcasted_iota(jnp.int32, (vectors, 2 * total), 1) // vectors % aggs
    own = full[:vectors]
    for agg in range(1, aggs):
        own = jnp.where(lanes == agg, full[agg * vectors : (agg + 1) * vectors], own)
    pieces = []
    lane_group = lax.broadcasted_iota(jnp.int32, (aggs, total), 1) // vectors
    sub = lax.broadcasted_iota(jnp.int32, (aggs, total), 0)
    for piece in range(2 * vectors // aggs):
        part, row = divmod(piece * aggs, vectors)
        value = own[row : row + aggs, part * total : (part + 1) * total]
        step = 1
        while step < aggs:
            sub_bit = (sub // step) % 2
            lane_bit = (lane_group // step) % 2
            up = pltpu.roll(pltpu.roll(value, aggs - step, axis=0), step * vectors, axis=1)
            down = pltpu.roll(pltpu.roll(value, step, axis=0), total - step * vectors, axis=1)
            value = jnp.where(sub_bit == lane_bit, value, jnp.where(sub_bit == 0, up, down))
            step *= 2
        pieces.append(value)
    return jnp.concatenate(pieces, axis=1)


def slice_kernel(nulls, *refs, sources):
    edges, sems = refs[:-1], refs[-1]
    copies = []
    for edge, (start, count, at, space) in zip(edges, sources):
        for row in range(count):
            source = nulls.at[pl.ds(start + row, 1), pl.ds(at, space)]
            copies.append(pltpu.make_async_copy(source, edge.at[pl.ds(row, 1)], sems.at[len(copies)]))
    for copy in copies:
        copy.start()
    for copy in copies:
        copy.wait()


def choose_rows(place, lists, picks):
    me = place[0]
    shards, cap = lists.shape
    count = picks.shape[2] // 2
    lane = lax.broadcasted_iota(jnp.int32, (MOST, cap), 1)
    want = lax.broadcasted_iota(jnp.int32, (MOST, cap), 0)
    column = lax.broadcasted_iota(jnp.int32, (MOST, 2 * count), 1)
    quarter = count // 4
    inside = column % count
    turned = (inside // quarter % 2) * 2 * quarter + (inside // (2 * quarter)) * quarter + inside % quarter
    own_column = column < count
    side = lax.rem(me, 2)
    for turn in range(shards // 2):
        owner = 2 * jnp.bitwise_xor(me // 2, turn) + side
        mine = jnp.broadcast_to(lists[pl.ds(owner, 1), :], (MOST, cap))
        for parity in range(2):
            source = me - side + parity
            before = jnp.where((mine >= 0) & (mine < source * count), 1, 0)
            start = jnp.sum(before.astype(jnp.float32), axis=1, keepdims=True).astype(jnp.int32)
            match = (mine >= source * count) & (mine < (source + 1) * count) & (lane - start == want)
            chosen = jnp.sum(jnp.where(match, mine - source * count + 1, 0).astype(jnp.float32), axis=1, keepdims=True)
            chosen = chosen.astype(jnp.int32) - 1
            here = own_column == (side == parity)
            rows = pl.ds((2 * turn + parity) * MOST, MOST)
            picks[0, rows, :] = jnp.where(here & (inside == chosen), 1.0, 0.0)
            picks[1, rows, :] = jnp.where(here & (turned == chosen), 1.0, 0.0)


def inner_work(nulls, time_links, space_links, early, adjoint, links, vecs, left, right, sems):
    time_count, space_count, sites, vectors, width = nulls.shape
    copies = []
    bases = [pltpu.make_async_copy(nulls.at[t], vecs.at[t], sems.at[16 + t]) for t in range(4)]
    bases[1].start()
    bases[2].start()

    def fetch(source):
        slot = len(copies)
        copy = pltpu.make_async_copy(source, links.at[slot], sems.at[slot])
        copy.start()
        copies.append(copy)

    for x in range(4):
        fetch(time_links.at[0, x])
    bases[0].start()
    bases[3].start()
    for t in range(4):
        fetch(space_links.at[t, 0])
    for x in range(4):
        fetch(time_links.at[1, x])
    for t in range(4):
        fetch(space_links.at[t, 1])
    bases[1].wait()
    bases[2].wait()
    for a_x in range(2):
        copies[2 * a_x].wait()
        copies[2 * a_x + 1].wait()
        for c in range(2):
            x = 2 * a_x + c
            image_item(links.at[x], vecs.at[1, x], vecs.at[2, x], c, left.at[a_x], right.at[a_x])
    bases[0].wait()
    bases[3].wait()
    for a_t in range(2):
        copies[4 + 2 * a_t].wait()
        copies[5 + 2 * a_t].wait()
        for c in range(2):
            t = 2 * a_t + c
            image_item(links.at[4 + t], vecs.at[t, 1], vecs.at[t, 2], c, left.at[2 + a_t], right.at[2 + a_t])
    found = [group_rows(left[group], right[group], MAT_DIMS, vectors) for group in range(4)]
    early[...] = jnp.concatenate(found, axis=0)
    for x in range(4):
        copies[8 + x].wait()
    for x in range(4):
        adjoint_item(links.at[8 + x], vecs.at[3, x], x % 2, adjoint.at[x // 2])
    for t in range(4):
        copies[12 + t].wait()
    for t in range(4):
        adjoint_item(links.at[12 + t], vecs.at[t, 3], t % 2, adjoint.at[2 + t // 2])


def before_kernel(group, nulls, time_links, space_links, sliced, edge, *refs):
    edge[...] = sliced[...]

    @pl.when(lax.rem(group[0], 2) == 1)
    def _():
        inner_work(nulls, time_links, space_links, *refs)


def after_kernel(group, nulls, time_links, space_links, early_before, adjoint_before, early, adjoint, *refs):
    @pl.when(lax.rem(group[0], 2) == 0)
    def _():
        inner_work(nulls, time_links, space_links, early, adjoint, *refs)

    @pl.when(lax.rem(group[0], 2) == 1)
    def _():
        early[...] = early_before[...]
        adjoint[...] = adjoint_before[...]


def edge_rows(uppers, adjoint, vectors):
    width = uppers[0].shape[-1]
    sign = signs((vectors, width), jnp.bfloat16)
    parts = []
    for upper in uppers:
        sites = upper.shape[0]
        for site in range(SIDE):
            rows = [upper[agg * SIDE + site] for agg in range(sites // SIDE)]
            turned = [sign * swapped(row) for row in rows]
            parts.append(jnp.concatenate(rows + turned, axis=0))
    return group_rows(adjoint, jnp.concatenate(parts, axis=1), ROW_DIMS, vectors)


def middle_kernel(place, lists, space_edge, time_first, time_second, adjoint, found, picks):
    choose_rows(place, lists, picks)
    vectors = space_edge.shape[3]
    rows = []
    for a_x, time_edge in enumerate((time_first, time_second)):
        uppers = [time_edge.at[0, c] for c in range(2)]
        rows.append(edge_rows(uppers, adjoint[a_x], vectors))
    rows.append(edge_rows([space_edge.at[c, 0] for c in range(2)], adjoint[2], vectors))
    found[...] = jnp.concatenate(rows, axis=0)


def final_kernel(space_edge, adjoint, early, found, late):
    vectors = space_edge.shape[3]
    rows = edge_rows([space_edge.at[c, 0] for c in range(2)], adjoint[3], vectors)
    late[...] = jnp.concatenate([early[...], found[...], rows], axis=0).astype(jnp.bfloat16)


def pack_kernel(picks, late, late_other, *packed):
    quarter, width = late.shape[0] // 4, late.shape[1]
    for half in range(2):
        spans = [pl.ds((half + 2 * part) * quarter, quarter) for part in range(2)]
        rows = jnp.concatenate([piece[span, :] for piece in (late, late_other) for span in spans], axis=0)
        sent = dot(picks[half].astype(jnp.bfloat16), rows, MAT_DIMS)
        for turn, out in enumerate(packed):
            mine = sent[turn * 2 * MOST : (turn + 1) * 2 * MOST]
            out[:, pl.ds(half * width, width)] = mine.astype(jnp.bfloat16)


def unpack_kernel(place, *refs, turns):
    pair = place[0] // 2
    result, rows, sems = refs[-3:]
    copies = []
    for slot, turn in enumerate(turns):
        source = jnp.bitwise_xor(pair, turn)
        rows[slot] = refs[slot][...].astype(jnp.float32)
        target = result.at[pl.ds(pl.multiple_of(source * 2 * MOST, 2 * MOST), 2 * MOST)]
        copies.append(pltpu.make_async_copy(rows.at[slot], target, sems.at[slot]))
        copies[-1].start()
    for copy in copies:
        copy.wait()


def on_device(nulls, time_links, space_links, owner_lists):
    time_count, space_count, sites, vectors, width = nulls.shape
    shards, cap = owner_lists.shape
    aggs = sites // SIDE
    local_count = (time_count // 2) * (space_count // 2) * aggs
    wide = 2 * vectors * vectors
    place = lax.axis_index("xyz").astype(jnp.int32).reshape(1)
    group = lax.axis_index("ta").astype(jnp.int32).reshape(1)
    vmem = pl.BlockSpec(memory_space=pltpu.VMEM)
    smem = pl.BlockSpec(memory_space=pltpu.SMEM)
    anywhere = pl.BlockSpec(memory_space=pl.ANY)
    outside = pl.BlockSpec(memory_space=pltpu.HBM)
    half = width // 2
    roomy = pltpu.CompilerParams(vmem_limit_bytes=51 * 1024 * 1024)
    modest = pltpu.CompilerParams(vmem_limit_bytes=24 * 1024 * 1024)
    first = pltpu.CompilerParams(vmem_limit_bytes=52 * 1024 * 1024)
    tiny = pl.CostEstimate(flops=1000, bytes_accessed=1000, transcendentals=0)
    half_time = time_count // 2

    def sliced(name, *sources):
        shapes = [(count, space, sites, vectors, width) for _, count, _, space in sources]
        return pl.pallas_call(
            functools.partial(slice_kernel, sources=sources),
            in_specs=[outside],
            out_specs=[vmem] * len(sources),
            out_shape=[jax.ShapeDtypeStruct(shape, nulls.dtype) for shape in shapes],
            scratch_shapes=[pltpu.SemaphoreType.DMA((sum(source[1] for source in sources),))],
            compiler_params=first,
            cost_estimate=tiny,
            name=name,
        )(nulls)

    half_space = space_count // 2
    space_first, space_later, time_first, time_second = sliced(
        "slices",
        (0, half_time, 0, 1),
        (half_time, half_time, 0, 1),
        (0, 1, 0, half_space),
        (0, 1, half_space, half_space),
    )
    edge_first = shifted(space_first, "xyz", -1)
    edge_times = [shifted(time_first, "ta", -1), shifted(time_second, "ta", -1)]
    inner_out = [
        jax.ShapeDtypeStruct((4 * aggs, wide), jnp.float32),
        jax.ShapeDtypeStruct((4, vectors * aggs, 8 * width), jnp.bfloat16),
    ]
    inner_scratch = [
        pltpu.VMEM((16, sites, half, width), jnp.bfloat16),
        pltpu.VMEM(nulls.shape, nulls.dtype),
        pltpu.VMEM((4, vectors * aggs, 8 * width), jnp.bfloat16),
        pltpu.VMEM((4, 8 * width, 2 * vectors * aggs), jnp.bfloat16),
        pltpu.SemaphoreType.DMA((20,)),
    ]
    space_second, early_one, adjoint_one = pl.pallas_call(
        before_kernel,
        in_specs=[smem] + [outside] * 3 + [vmem],
        out_specs=[vmem] * 3,
        out_shape=[jax.ShapeDtypeStruct(space_first.shape, nulls.dtype)] + inner_out,
        scratch_shapes=inner_scratch,
        compiler_params=roomy,
        cost_estimate=tiny,
        name="before",
    )(group, nulls, time_links, space_links, space_later)
    edge_second = shifted(space_second, "xyz", -1)
    early, adjoint = pl.pallas_call(
        after_kernel,
        in_specs=[smem] + [outside] * 3 + [vmem] * 2,
        out_specs=[vmem] * 2,
        out_shape=inner_out,
        scratch_shapes=inner_scratch,
        compiler_params=roomy,
        cost_estimate=tiny,
        name="after",
    )(group, nulls, time_links, space_links, early_one, adjoint_one)
    found, picks = pl.pallas_call(
        middle_kernel,
        in_specs=[smem] + [vmem] * 5,
        out_specs=[vmem] * 2,
        out_shape=[
            jax.ShapeDtypeStruct((3 * aggs, wide), jnp.float32),
            jax.ShapeDtypeStruct((2, shards * MOST, 2 * local_count), jnp.float32),
        ],
        compiler_params=modest,
        cost_estimate=tiny,
        name="middle",
    )(place, owner_lists, edge_first, *edge_times, adjoint)
    late = pl.pallas_call(
        final_kernel,
        in_specs=[vmem] * 4,
        out_specs=vmem,
        out_shape=jax.ShapeDtypeStruct((8 * aggs, wide), jnp.bfloat16),
        compiler_params=modest,
        cost_estimate=tiny,
        name="final",
    )(edge_second, adjoint, early, found)
    late_other = crossed(late, "xyz", 1)
    pairs = shards // 2
    packed = pl.pallas_call(
        pack_kernel,
        in_specs=[vmem] * 3,
        out_specs=[vmem] * pairs,
        out_shape=[jax.ShapeDtypeStruct((2 * MOST, 2 * wide), jnp.bfloat16)] * pairs,
        compiler_params=modest,
        cost_estimate=tiny,
        name="pack",
    )(picks, late, late_other)
    turns = list(range(2, pairs)) + [1]
    arrived = [crossed(packed[turn], "xyz", 2 * turn) for turn in turns]
    arrived = pl.pallas_call(
        functools.partial(unpack_kernel, turns=turns + [0]),
        in_specs=[smem] + [vmem] * pairs,
        out_specs=outside,
        out_shape=jax.ShapeDtypeStruct((shards * MOST, 2 * wide), jnp.float32),
        scratch_shapes=[
            pltpu.VMEM((pairs, 2 * MOST, 2 * wide), jnp.float32),
            pltpu.SemaphoreType.DMA((pairs,)),
        ],
        compiler_params=modest,
        cost_estimate=tiny,
        name="unpack",
    )(place, *arrived, packed[0])
    if shards * MOST == cap:
        result = arrived
    else:
        my_list = lax.dynamic_index_in_dim(owner_lists, lax.axis_index("xyz"), 0, keepdims=False)
        source = jnp.maximum(my_list, 0) // local_count
        order = jnp.arange(cap, dtype=jnp.int32)
        same = (source[:, None] == source[None, :]) & (order[None, :] < order[:, None])
        offset = jnp.sum(same.astype(jnp.int32), axis=1)
        picked = arrived[source * MOST + offset]
        result = jnp.where((my_list >= 0)[:, None], picked, 0.0)
    return result[None]


def solution(mesh):
    return jax.shard_map(
        on_device,
        mesh=mesh,
        in_specs=(
            P("ta", "xyz", None, None, None),
            P("ta", "xyz", None, None, None),
            P("ta", "xyz", None, None, None),
            P(),
        ),
        out_specs=P("ta", "xyz", None),
        check_vma=False,
    )
```

```python
import functools

import jax
import jax.numpy as jnp
from jax import lax
from jax.experimental import pallas as pl
from jax.experimental.pallas import tpu as pltpu
from jax.sharding import PartitionSpec as P

ROW_DIMS = (((1,), (1,)), ((), ()))
MAT_DIMS = (((1,), (0,)), ((), ()))
SIDE = 4
MOST = 8


def shifted(array, axis, by):
    count = lax.axis_size(axis)
    return lax.ppermute(array, axis, [(i, (i + by) % count) for i in range(count)])


def crossed(array, axis, bits):
    return lax.ppermute(array, axis, [(i, i ^ bits) for i in range(lax.axis_size(axis))])


def dot(left, right, dims):
    return lax.dot_general(left, right, dims, preferred_element_type=jnp.float32)


def swapped(array):
    return pltpu.roll(array, array.shape[-1] // 2, axis=array.ndim - 1)


def lower_half(shape):
    return lax.broadcasted_iota(jnp.int32, shape, len(shape) - 1) < shape[-1] // 2


def signs(shape, dtype):
    return jnp.where(lower_half(shape), 1.0, -1.0).astype(dtype)


def image_item(links, lower, upper, slot, left_ref, right_ref):
    sites, vectors, width = lower.shape
    half = width // 2
    aggs = sites // SIDE
    lanes = aggs * vectors
    sign = signs((vectors, width), jnp.bfloat16)
    zero = jnp.zeros((vectors, width), jnp.bfloat16)
    owner = lax.broadcasted_iota(jnp.int32, (half, 2 * lanes), 1) // (2 * vectors) % (aggs // 2)
    for part in range(SIDE):
        at = (slot * SIDE + part) * width
        mats = []
        plain, crossed = [], []
        for agg in range(aggs):
            site = agg * SIDE + part
            up = upper[site]
            pair = (up * sign, swapped(up))
            for rows, value in zip((plain, crossed), pair):
                rows.append(jnp.concatenate([value, zero] if agg % 2 == 0 else [zero, value], axis=1))
            if agg % 2 == 0:
                mats.append(jnp.concatenate([links[site], links[site + SIDE]], axis=1))
            left_ref[pl.ds(agg * vectors, vectors), pl.ds(at, width)] = lower[site]
        images = dot(jnp.concatenate(mats, axis=0), jnp.concatenate(plain + crossed, axis=0), ROW_DIMS)
        own = images[:half]
        for pair in range(1, aggs // 2):
            own = jnp.where(owner == pair, images[pair * half : (pair + 1) * half], own)
        own = own.astype(jnp.bfloat16)
        right_ref[pl.ds(at, half), :] = own
        right_ref[pl.ds(at + half, half), :] = jnp.concatenate([own[:, lanes:], -own[:, :lanes]], axis=1)


def adjoint_item(links, lower, slot, left_ref):
    sites, vectors, width = lower.shape
    half = width // 2
    low = lower_half((vectors, width))
    sign = signs((vectors, width), jnp.float32)
    zero = jnp.zeros((vectors, width), jnp.bfloat16)
    for agg in range(sites // SIDE):
        rows = []
        mats = []
        for pair in range(SIDE // 2):
            at = agg * SIDE + 2 * pair
            lo_a, lo_b = lower[at], lower[at + 1]
            rows += [
                jnp.where(low, lo_a, zero),
                jnp.where(low, swapped(lo_a), zero),
                jnp.where(low, zero, swapped(lo_b)),
                jnp.where(low, zero, lo_b),
            ]
            mats.append(jnp.concatenate([links[at], links[at + 1]], axis=0))
        prod = dot(jnp.concatenate(rows, axis=0), jnp.concatenate(mats, axis=1), MAT_DIMS)
        for part in range(SIDE):
            top = part * 2 * vectors
            mine = prod[top : top + 2 * vectors, part // 2 * width : (part // 2 + 1) * width]
            adj = sign * mine[:vectors] + swapped(mine[vectors:])
            left_ref[pl.ds(agg * vectors, vectors), pl.ds((slot * SIDE + part) * width, width)] = adj.astype(jnp.bfloat16)


def group_rows(left, right, dims, vectors):
    full = dot(left, right, dims)
    total = full.shape[1] // 2
    aggs = total // vectors
    lanes = lax.broadcasted_iota(jnp.int32, (vectors, 2 * total), 1) // vectors % aggs
    own = full[:vectors]
    for agg in range(1, aggs):
        own = jnp.where(lanes == agg, full[agg * vectors : (agg + 1) * vectors], own)
    pieces = []
    lane_group = lax.broadcasted_iota(jnp.int32, (aggs, total), 1) // vectors
    sub = lax.broadcasted_iota(jnp.int32, (aggs, total), 0)
    for piece in range(2 * vectors // aggs):
        part, row = divmod(piece * aggs, vectors)
        value = own[row : row + aggs, part * total : (part + 1) * total]
        step = 1
        while step < aggs:
            sub_bit = (sub // step) % 2
            lane_bit = (lane_group // step) % 2
            up = pltpu.roll(pltpu.roll(value, aggs - step, axis=0), step * vectors, axis=1)
            down = pltpu.roll(pltpu.roll(value, step, axis=0), total - step * vectors, axis=1)
            value = jnp.where(sub_bit == lane_bit, value, jnp.where(sub_bit == 0, up, down))
            step *= 2
        pieces.append(value)
    return jnp.concatenate(pieces, axis=1)


def slice_kernel(nulls, *refs, sources, skip):
    edges, sems = refs[skip:-1], refs[-1]
    copies = []
    for edge, (start, count, at, space) in zip(edges, sources):
        for row in range(count):
            source = nulls.at[pl.ds(start + row, 1), pl.ds(at, space)]
            copies.append(pltpu.make_async_copy(source, edge.at[pl.ds(row, 1)], sems.at[len(copies)]))
    for copy in copies:
        copy.start()
    for copy in copies:
        copy.wait()


def choose_rows(place, lists, picks):
    me = place[0]
    shards, cap = lists.shape
    count = picks.shape[2] // 2
    lane = lax.broadcasted_iota(jnp.int32, (MOST, cap), 1)
    want = lax.broadcasted_iota(jnp.int32, (MOST, cap), 0)
    column = lax.broadcasted_iota(jnp.int32, (MOST, 2 * count), 1)
    quarter = count // 4
    inside = column % count
    turned = (inside // quarter % 2) * 2 * quarter + (inside // (2 * quarter)) * quarter + inside % quarter
    own_column = column < count
    side = lax.rem(me, 2)
    for turn in range(shards // 2):
        owner = 2 * jnp.bitwise_xor(me // 2, turn) + side
        mine = jnp.broadcast_to(lists[pl.ds(owner, 1), :], (MOST, cap))
        for parity in range(2):
            source = me - side + parity
            before = jnp.where((mine >= 0) & (mine < source * count), 1, 0)
            start = jnp.sum(before.astype(jnp.float32), axis=1, keepdims=True).astype(jnp.int32)
            match = (mine >= source * count) & (mine < (source + 1) * count) & (lane - start == want)
            chosen = jnp.sum(jnp.where(match, mine - source * count + 1, 0).astype(jnp.float32), axis=1, keepdims=True)
            chosen = chosen.astype(jnp.int32) - 1
            here = own_column == (side == parity)
            rows = pl.ds((2 * turn + parity) * MOST, MOST)
            picks[0, rows, :] = jnp.where(here & (inside == chosen), 1.0, 0.0)
            picks[1, rows, :] = jnp.where(here & (turned == chosen), 1.0, 0.0)


def inner_work(nulls, time_links, space_links, early, adjoint, links, vecs, left, right, sems):
    time_count, space_count, sites, vectors, width = nulls.shape
    copies = []
    bases = [pltpu.make_async_copy(nulls.at[t], vecs.at[t], sems.at[16 + t]) for t in range(4)]
    bases[1].start()
    bases[2].start()

    def fetch(source):
        slot = len(copies)
        copy = pltpu.make_async_copy(source, links.at[slot], sems.at[slot])
        copy.start()
        copies.append(copy)

    for x in range(4):
        fetch(time_links.at[0, x])
    bases[0].start()
    bases[3].start()
    for t in range(4):
        fetch(space_links.at[t, 0])
    for x in range(4):
        fetch(time_links.at[1, x])
    for t in range(4):
        fetch(space_links.at[t, 1])
    bases[1].wait()
    bases[2].wait()
    for a_x in range(2):
        copies[2 * a_x].wait()
        copies[2 * a_x + 1].wait()
        for c in range(2):
            x = 2 * a_x + c
            image_item(links.at[x], vecs.at[1, x], vecs.at[2, x], c, left.at[a_x], right.at[a_x])
    bases[0].wait()
    bases[3].wait()
    for a_t in range(2):
        copies[4 + 2 * a_t].wait()
        copies[5 + 2 * a_t].wait()
        for c in range(2):
            t = 2 * a_t + c
            image_item(links.at[4 + t], vecs.at[t, 1], vecs.at[t, 2], c, left.at[2 + a_t], right.at[2 + a_t])
    found = [group_rows(left[group], right[group], MAT_DIMS, vectors) for group in range(4)]
    early[...] = jnp.concatenate(found, axis=0)
    for x in range(4):
        copies[8 + x].wait()
    for x in range(4):
        adjoint_item(links.at[8 + x], vecs.at[3, x], x % 2, adjoint.at[x // 2])
    for t in range(4):
        copies[12 + t].wait()
    for t in range(4):
        adjoint_item(links.at[12 + t], vecs.at[t, 3], t % 2, adjoint.at[2 + t // 2])


def before_kernel(group, nulls, time_links, space_links, sliced, edge, *refs):
    edge[...] = sliced[...]

    @pl.when(lax.rem(group[0], 2) == 1)
    def _():
        inner_work(nulls, time_links, space_links, *refs)


def after_kernel(group, nulls, time_links, space_links, early_before, adjoint_before, early, adjoint, *refs):
    @pl.when(lax.rem(group[0], 2) == 0)
    def _():
        inner_work(nulls, time_links, space_links, early, adjoint, *refs)

    @pl.when(lax.rem(group[0], 2) == 1)
    def _():
        early[...] = early_before[...]
        adjoint[...] = adjoint_before[...]


def edge_rows(uppers, adjoint, vectors):
    width = uppers[0].shape[-1]
    sign = signs((vectors, width), jnp.bfloat16)
    parts = []
    for upper in uppers:
        sites = upper.shape[0]
        for site in range(SIDE):
            rows = [upper[agg * SIDE + site] for agg in range(sites // SIDE)]
            turned = [sign * swapped(row) for row in rows]
            parts.append(jnp.concatenate(rows + turned, axis=0))
    return group_rows(adjoint, jnp.concatenate(parts, axis=1), ROW_DIMS, vectors)


def middle_kernel(place, lists, space_edge, time_first, time_second, adjoint, found, picks):
    choose_rows(place, lists, picks)
    vectors = space_edge.shape[3]
    rows = []
    for a_x, time_edge in enumerate((time_first, time_second)):
        uppers = [time_edge.at[0, c] for c in range(2)]
        rows.append(edge_rows(uppers, adjoint[a_x], vectors))
    rows.append(edge_rows([space_edge.at[c, 0] for c in range(2)], adjoint[2], vectors))
    found[...] = jnp.concatenate(rows, axis=0)


def final_kernel(space_edge, adjoint, early, found, late):
    vectors = space_edge.shape[3]
    rows = edge_rows([space_edge.at[c, 0] for c in range(2)], adjoint[3], vectors)
    late[...] = jnp.concatenate([early[...], found[...], rows], axis=0).astype(jnp.bfloat16)


def pack_kernel(picks, late, late_other, *packed):
    quarter, width = late.shape[0] // 4, late.shape[1]
    for half in range(2):
        spans = [pl.ds((half + 2 * part) * quarter, quarter) for part in range(2)]
        rows = jnp.concatenate([piece[span, :] for piece in (late, late_other) for span in spans], axis=0)
        sent = dot(picks[half].astype(jnp.bfloat16), rows, MAT_DIMS)
        for turn, out in enumerate(packed):
            mine = sent[turn * 2 * MOST : (turn + 1) * 2 * MOST]
            out[:, pl.ds(half * width, width)] = mine.astype(jnp.bfloat16)


def unpack_kernel(place, *refs, turns):
    pair = place[0] // 2
    result, rows, sems = refs[-3:]
    copies = []
    for slot, turn in enumerate(turns):
        source = jnp.bitwise_xor(pair, turn)
        rows[slot] = refs[slot][...].astype(jnp.float32)
        target = result.at[pl.ds(pl.multiple_of(source * 2 * MOST, 2 * MOST), 2 * MOST)]
        copies.append(pltpu.make_async_copy(rows.at[slot], target, sems.at[slot]))
        copies[-1].start()
    for copy in copies:
        copy.wait()


def on_device(nulls, time_links, space_links, owner_lists):
    time_count, space_count, sites, vectors, width = nulls.shape
    shards, cap = owner_lists.shape
    aggs = sites // SIDE
    local_count = (time_count // 2) * (space_count // 2) * aggs
    wide = 2 * vectors * vectors
    place = lax.axis_index("xyz").astype(jnp.int32).reshape(1)
    group = lax.axis_index("ta").astype(jnp.int32).reshape(1)
    vmem = pl.BlockSpec(memory_space=pltpu.VMEM)
    smem = pl.BlockSpec(memory_space=pltpu.SMEM)
    anywhere = pl.BlockSpec(memory_space=pl.ANY)
    outside = pl.BlockSpec(memory_space=pltpu.HBM)
    half = width // 2
    roomy = pltpu.CompilerParams(vmem_limit_bytes=51 * 1024 * 1024)
    modest = pltpu.CompilerParams(vmem_limit_bytes=24 * 1024 * 1024)
    first = pltpu.CompilerParams(vmem_limit_bytes=52 * 1024 * 1024)
    tiny = pl.CostEstimate(flops=1000, bytes_accessed=1000, transcendentals=0)
    half_time = time_count // 2

    def sliced(name, *sources, after=()):
        shapes = [(count, space, sites, vectors, width) for _, count, _, space in sources]
        return pl.pallas_call(
            functools.partial(slice_kernel, sources=sources, skip=len(after)),
            in_specs=[outside] + [anywhere] * len(after),
            out_specs=[vmem] * len(sources),
            out_shape=[jax.ShapeDtypeStruct(shape, nulls.dtype) for shape in shapes],
            scratch_shapes=[pltpu.SemaphoreType.DMA((sum(source[1] for source in sources),))],
            compiler_params=first,
            cost_estimate=tiny,
            name=name,
        )(nulls, *after)

    half_space = space_count // 2
    (space_first,) = sliced("slice_first", (0, half_time, 0, 1))
    space_later, time_first, time_second = sliced(
        "slice_rest", (half_time, half_time, 0, 1), (0, 1, 0, half_space), (0, 1, half_space, half_space), after=(space_first,)
    )
    edge_first = shifted(space_first, "xyz", -1)
    edge_times = [shifted(time_first, "ta", -1), shifted(time_second, "ta", -1)]
    inner_out = [
        jax.ShapeDtypeStruct((4 * aggs, wide), jnp.float32),
        jax.ShapeDtypeStruct((4, vectors * aggs, 8 * width), jnp.bfloat16),
    ]
    inner_scratch = [
        pltpu.VMEM((16, sites, half, width), jnp.bfloat16),
        pltpu.VMEM(nulls.shape, nulls.dtype),
        pltpu.VMEM((4, vectors * aggs, 8 * width), jnp.bfloat16),
        pltpu.VMEM((4, 8 * width, 2 * vectors * aggs), jnp.bfloat16),
        pltpu.SemaphoreType.DMA((20,)),
    ]
    space_second, early_one, adjoint_one = pl.pallas_call(
        before_kernel,
        in_specs=[smem] + [outside] * 3 + [vmem],
        out_specs=[vmem] * 3,
        out_shape=[jax.ShapeDtypeStruct(space_first.shape, nulls.dtype)] + inner_out,
        scratch_shapes=inner_scratch,
        compiler_params=roomy,
        cost_estimate=tiny,
        name="before",
    )(group, nulls, time_links, space_links, space_later)
    edge_second = shifted(space_second, "xyz", -1)
    early, adjoint = pl.pallas_call(
        after_kernel,
        in_specs=[smem] + [outside] * 3 + [vmem] * 2,
        out_specs=[vmem] * 2,
        out_shape=inner_out,
        scratch_shapes=inner_scratch,
        compiler_params=roomy,
        cost_estimate=tiny,
        name="after",
    )(group, nulls, time_links, space_links, early_one, adjoint_one)
    found, picks = pl.pallas_call(
        middle_kernel,
        in_specs=[smem] + [vmem] * 5,
        out_specs=[vmem] * 2,
        out_shape=[
            jax.ShapeDtypeStruct((3 * aggs, wide), jnp.float32),
            jax.ShapeDtypeStruct((2, shards * MOST, 2 * local_count), jnp.float32),
        ],
        compiler_params=modest,
        cost_estimate=tiny,
        name="middle",
    )(place, owner_lists, edge_first, *edge_times, adjoint)
    late = pl.pallas_call(
        final_kernel,
        in_specs=[vmem] * 4,
        out_specs=vmem,
        out_shape=jax.ShapeDtypeStruct((8 * aggs, wide), jnp.bfloat16),
        compiler_params=modest,
        cost_estimate=tiny,
        name="final",
    )(edge_second, adjoint, early, found)
    late_other = crossed(late, "xyz", 1)
    pairs = shards // 2
    packed = pl.pallas_call(
        pack_kernel,
        in_specs=[vmem] * 3,
        out_specs=[vmem] * pairs,
        out_shape=[jax.ShapeDtypeStruct((2 * MOST, 2 * wide), jnp.bfloat16)] * pairs,
        compiler_params=modest,
        cost_estimate=tiny,
        name="pack",
    )(picks, late, late_other)
    turns = list(range(2, pairs)) + [1]
    arrived = [crossed(packed[turn], "xyz", 2 * turn) for turn in turns]
    arrived = pl.pallas_call(
        functools.partial(unpack_kernel, turns=turns + [0]),
        in_specs=[smem] + [vmem] * pairs,
        out_specs=outside,
        out_shape=jax.ShapeDtypeStruct((shards * MOST, 2 * wide), jnp.float32),
        scratch_shapes=[
            pltpu.VMEM((pairs, 2 * MOST, 2 * wide), jnp.float32),
            pltpu.SemaphoreType.DMA((pairs,)),
        ],
        compiler_params=modest,
        cost_estimate=tiny,
        name="unpack",
    )(place, *arrived, packed[0])
    if shards * MOST == cap:
        result = arrived
    else:
        my_list = lax.dynamic_index_in_dim(owner_lists, lax.axis_index("xyz"), 0, keepdims=False)
        source = jnp.maximum(my_list, 0) // local_count
        order = jnp.arange(cap, dtype=jnp.int32)
        same = (source[:, None] == source[None, :]) & (order[None, :] < order[:, None])
        offset = jnp.sum(same.astype(jnp.int32), axis=1)
        picked = arrived[source * MOST + offset]
        result = jnp.where((my_list >= 0)[:, None], picked, 0.0)
    return result[None]


def solution(mesh):
    return jax.shard_map(
        on_device,
        mesh=mesh,
        in_specs=(
            P("ta", "xyz", None, None, None),
            P("ta", "xyz", None, None, None),
            P("ta", "xyz", None, None, None),
            P(),
        ),
        out_specs=P("ta", "xyz", None),
        check_vma=False,
    )
```

```python
import functools

import jax
import jax.numpy as jnp
from jax import lax
from jax.experimental import pallas as pl
from jax.experimental.pallas import tpu as pltpu
from jax.sharding import PartitionSpec as P

ROW_DIMS = (((1,), (1,)), ((), ()))
MAT_DIMS = (((1,), (0,)), ((), ()))
SIDE = 4
MOST = 8


def shifted(array, axis, by):
    count = lax.axis_size(axis)
    return lax.ppermute(array, axis, [(i, (i + by) % count) for i in range(count)])


def crossed(array, axis, bits):
    return lax.ppermute(array, axis, [(i, i ^ bits) for i in range(lax.axis_size(axis))])


def dot(left, right, dims):
    return lax.dot_general(left, right, dims, preferred_element_type=jnp.float32)


def swapped(array):
    return pltpu.roll(array, array.shape[-1] // 2, axis=array.ndim - 1)


def lower_half(shape):
    return lax.broadcasted_iota(jnp.int32, shape, len(shape) - 1) < shape[-1] // 2


def signs(shape, dtype):
    return jnp.where(lower_half(shape), 1.0, -1.0).astype(dtype)


def image_item(links, lower, upper, slot, left_ref, right_ref):
    sites, vectors, width = lower.shape
    half = width // 2
    aggs = sites // SIDE
    lanes = aggs * vectors
    sign = signs((vectors, width), jnp.bfloat16)
    zero = jnp.zeros((vectors, width), jnp.bfloat16)
    owner = lax.broadcasted_iota(jnp.int32, (half, 2 * lanes), 1) // (2 * vectors) % (aggs // 2)
    for part in range(SIDE):
        at = (slot * SIDE + part) * width
        mats = []
        plain, crossed = [], []
        for agg in range(aggs):
            site = agg * SIDE + part
            up = upper[site]
            pair = (up * sign, swapped(up))
            for rows, value in zip((plain, crossed), pair):
                rows.append(jnp.concatenate([value, zero] if agg % 2 == 0 else [zero, value], axis=1))
            if agg % 2 == 0:
                mats.append(jnp.concatenate([links[site], links[site + SIDE]], axis=1))
            left_ref[pl.ds(agg * vectors, vectors), pl.ds(at, width)] = lower[site]
        images = dot(jnp.concatenate(mats, axis=0), jnp.concatenate(plain + crossed, axis=0), ROW_DIMS)
        own = images[:half]
        for pair in range(1, aggs // 2):
            own = jnp.where(owner == pair, images[pair * half : (pair + 1) * half], own)
        own = own.astype(jnp.bfloat16)
        right_ref[pl.ds(at, half), :] = own
        right_ref[pl.ds(at + half, half), :] = jnp.concatenate([own[:, lanes:], -own[:, :lanes]], axis=1)


def adjoint_item(links, lower, slot, left_ref):
    sites, vectors, width = lower.shape
    half = width // 2
    low = lower_half((vectors, width))
    sign = signs((vectors, width), jnp.float32)
    zero = jnp.zeros((vectors, width), jnp.bfloat16)
    for agg in range(sites // SIDE):
        rows = []
        mats = []
        for pair in range(SIDE // 2):
            at = agg * SIDE + 2 * pair
            lo_a, lo_b = lower[at], lower[at + 1]
            rows += [
                jnp.where(low, lo_a, zero),
                jnp.where(low, swapped(lo_a), zero),
                jnp.where(low, zero, swapped(lo_b)),
                jnp.where(low, zero, lo_b),
            ]
            mats.append(jnp.concatenate([links[at], links[at + 1]], axis=0))
        prod = dot(jnp.concatenate(rows, axis=0), jnp.concatenate(mats, axis=1), MAT_DIMS)
        for part in range(SIDE):
            top = part * 2 * vectors
            mine = prod[top : top + 2 * vectors, part // 2 * width : (part // 2 + 1) * width]
            adj = sign * mine[:vectors] + swapped(mine[vectors:])
            left_ref[pl.ds(agg * vectors, vectors), pl.ds((slot * SIDE + part) * width, width)] = adj.astype(jnp.bfloat16)


def group_rows(left, right, dims, vectors):
    full = dot(left, right, dims)
    total = full.shape[1] // 2
    aggs = total // vectors
    lanes = lax.broadcasted_iota(jnp.int32, (vectors, 2 * total), 1) // vectors % aggs
    own = full[:vectors]
    for agg in range(1, aggs):
        own = jnp.where(lanes == agg, full[agg * vectors : (agg + 1) * vectors], own)
    pieces = []
    lane_group = lax.broadcasted_iota(jnp.int32, (aggs, total), 1) // vectors
    sub = lax.broadcasted_iota(jnp.int32, (aggs, total), 0)
    for piece in range(2 * vectors // aggs):
        part, row = divmod(piece * aggs, vectors)
        value = own[row : row + aggs, part * total : (part + 1) * total]
        step = 1
        while step < aggs:
            sub_bit = (sub // step) % 2
            lane_bit = (lane_group // step) % 2
            up = pltpu.roll(pltpu.roll(value, aggs - step, axis=0), step * vectors, axis=1)
            down = pltpu.roll(pltpu.roll(value, step, axis=0), total - step * vectors, axis=1)
            value = jnp.where(sub_bit == lane_bit, value, jnp.where(sub_bit == 0, up, down))
            step *= 2
        pieces.append(value)
    return jnp.concatenate(pieces, axis=1)


def slice_kernel(nulls, *refs, sources, skip):
    edges, sems = refs[skip:-1], refs[-1]
    copies = []
    for edge, (start, count, at, space) in zip(edges, sources):
        for row in range(count):
            source = nulls.at[pl.ds(start + row, 1), pl.ds(at, space)]
            copies.append(pltpu.make_async_copy(source, edge.at[pl.ds(row, 1)], sems.at[len(copies)]))
    for copy in copies:
        copy.start()
    for copy in copies:
        copy.wait()


def choose_rows(place, lists, picks):
    me = place[0]
    shards, cap = lists.shape
    count = picks.shape[2] // 2
    lane = lax.broadcasted_iota(jnp.int32, (MOST, cap), 1)
    want = lax.broadcasted_iota(jnp.int32, (MOST, cap), 0)
    column = lax.broadcasted_iota(jnp.int32, (MOST, 2 * count), 1)
    quarter = count // 4
    inside = column % count
    turned = (inside // quarter % 2) * 2 * quarter + (inside // (2 * quarter)) * quarter + inside % quarter
    own_column = column < count
    side = lax.rem(me, 2)
    for turn in range(shards // 2):
        owner = 2 * jnp.bitwise_xor(me // 2, turn) + side
        mine = jnp.broadcast_to(lists[pl.ds(owner, 1), :], (MOST, cap))
        for parity in range(2):
            source = me - side + parity
            before = jnp.where((mine >= 0) & (mine < source * count), 1, 0)
            start = jnp.sum(before.astype(jnp.float32), axis=1, keepdims=True).astype(jnp.int32)
            match = (mine >= source * count) & (mine < (source + 1) * count) & (lane - start == want)
            chosen = jnp.sum(jnp.where(match, mine - source * count + 1, 0).astype(jnp.float32), axis=1, keepdims=True)
            chosen = chosen.astype(jnp.int32) - 1
            here = own_column == (side == parity)
            rows = pl.ds((2 * turn + parity) * MOST, MOST)
            picks[0, rows, :] = jnp.where(here & (inside == chosen), 1.0, 0.0)
            picks[1, rows, :] = jnp.where(here & (turned == chosen), 1.0, 0.0)


def inner_work(groups, images, nulls, time_links, space_links, early, adjoint, links, vecs, left, right, sems):
    vectors = nulls.shape[3]
    copies = {}
    bases = {}
    waited = set()

    def fetch(source, slot):
        copies[slot] = pltpu.make_async_copy(source, links.at[slot], sems.at[slot])
        copies[slot].start()

    def load(*rows):
        for row in rows:
            if row not in bases:
                bases[row] = pltpu.make_async_copy(nulls.at[row], vecs.at[row], sems.at[16 + row])
                bases[row].start()

    def need(*rows):
        for row in rows:
            if row not in waited:
                waited.add(row)
                bases[row].wait()

    if images:
        load(1, 2)
        for x in range(4):
            fetch(time_links.at[0, x], x)
        load(0, 3)
        for t in range(4):
            fetch(space_links.at[t, 0], 4 + t)
    for group in groups:
        for c in range(2):
            at = 2 * group + c
            source = time_links.at[1, at] if group < 2 else space_links.at[at - 4, 1]
            load(3 if group < 2 else at - 4)
            fetch(source, 8 + at)
    if images:
        for group in range(4):
            need(*((1, 2) if group < 2 else (0, 3)))
            copies[2 * group].wait()
            copies[2 * group + 1].wait()
            for c in range(2):
                at = 2 * group + c
                lower, upper = (vecs.at[1, at], vecs.at[2, at]) if group < 2 else (vecs.at[at - 4, 1], vecs.at[at - 4, 2])
                image_item(links.at[at], lower, upper, c, left.at[group], right.at[group])
        found = [group_rows(left[group], right[group], MAT_DIMS, vectors) for group in range(4)]
        early[...] = jnp.concatenate(found, axis=0)
    for group in groups:
        for c in range(2):
            at = 2 * group + c
            need(3 if group < 2 else at - 4)
            copies[8 + at].wait()
        for c in range(2):
            at = 2 * group + c
            lower = vecs.at[3, at] if group < 2 else vecs.at[at - 4, 3]
            adjoint_item(links.at[8 + at], lower, c, adjoint.at[group])


def before_kernel(group, nulls, time_links, space_links, sliced, edge, *refs):
    edge[...] = sliced[...]

    @pl.when(lax.rem(group[0], 2) == 1)
    def _():
        inner_work(range(3), True, nulls, time_links, space_links, *refs)


def after_kernel(group, nulls, time_links, space_links, early_before, adjoint_before, early, adjoint, *refs):
    @pl.when(lax.rem(group[0], 2) == 0)
    def _():
        inner_work(range(4), True, nulls, time_links, space_links, early, adjoint, *refs)

    @pl.when(lax.rem(group[0], 2) == 1)
    def _():
        early[...] = early_before[...]
        for group in range(3):
            adjoint[group] = adjoint_before[group]
        inner_work([3], False, nulls, time_links, space_links, early, adjoint, *refs)


def edge_rows(uppers, adjoint, vectors):
    width = uppers[0].shape[-1]
    sign = signs((vectors, width), jnp.bfloat16)
    parts = []
    for upper in uppers:
        sites = upper.shape[0]
        for site in range(SIDE):
            rows = [upper[agg * SIDE + site] for agg in range(sites // SIDE)]
            turned = [sign * swapped(row) for row in rows]
            parts.append(jnp.concatenate(rows + turned, axis=0))
    return group_rows(adjoint, jnp.concatenate(parts, axis=1), ROW_DIMS, vectors)


def middle_kernel(place, lists, space_edge, time_first, time_second, adjoint, found, picks):
    choose_rows(place, lists, picks)
    vectors = space_edge.shape[3]
    rows = []
    for a_x, time_edge in enumerate((time_first, time_second)):
        uppers = [time_edge.at[0, c] for c in range(2)]
        rows.append(edge_rows(uppers, adjoint[a_x], vectors))
    rows.append(edge_rows([space_edge.at[c, 0] for c in range(2)], adjoint[2], vectors))
    found[...] = jnp.concatenate(rows, axis=0)


def final_kernel(space_edge, adjoint, early, found, late):
    vectors = space_edge.shape[3]
    rows = edge_rows([space_edge.at[c, 0] for c in range(2)], adjoint[3], vectors)
    late[...] = jnp.concatenate([early[...], found[...], rows], axis=0).astype(jnp.bfloat16)


def pack_kernel(picks, late, late_other, *packed):
    quarter, width = late.shape[0] // 4, late.shape[1]
    for half in range(2):
        spans = [pl.ds((half + 2 * part) * quarter, quarter) for part in range(2)]
        rows = jnp.concatenate([piece[span, :] for piece in (late, late_other) for span in spans], axis=0)
        sent = dot(picks[half].astype(jnp.bfloat16), rows, MAT_DIMS)
        for turn, out in enumerate(packed):
            mine = sent[turn * 2 * MOST : (turn + 1) * 2 * MOST]
            out[:, pl.ds(half * width, width)] = mine.astype(jnp.bfloat16)


def unpack_kernel(place, *refs, turns):
    pair = place[0] // 2
    result, rows, sems = refs[-3:]
    copies = []
    for slot, turn in enumerate(turns):
        source = jnp.bitwise_xor(pair, turn)
        rows[slot] = refs[slot][...].astype(jnp.float32)
        target = result.at[pl.ds(pl.multiple_of(source * 2 * MOST, 2 * MOST), 2 * MOST)]
        copies.append(pltpu.make_async_copy(rows.at[slot], target, sems.at[slot]))
        copies[-1].start()
    for copy in copies:
        copy.wait()


def on_device(nulls, time_links, space_links, owner_lists):
    time_count, space_count, sites, vectors, width = nulls.shape
    shards, cap = owner_lists.shape
    aggs = sites // SIDE
    local_count = (time_count // 2) * (space_count // 2) * aggs
    wide = 2 * vectors * vectors
    place = lax.axis_index("xyz").astype(jnp.int32).reshape(1)
    group = lax.axis_index("ta").astype(jnp.int32).reshape(1)
    vmem = pl.BlockSpec(memory_space=pltpu.VMEM)
    smem = pl.BlockSpec(memory_space=pltpu.SMEM)
    anywhere = pl.BlockSpec(memory_space=pl.ANY)
    outside = pl.BlockSpec(memory_space=pltpu.HBM)
    half = width // 2
    roomy = pltpu.CompilerParams(vmem_limit_bytes=51 * 1024 * 1024)
    modest = pltpu.CompilerParams(vmem_limit_bytes=24 * 1024 * 1024)
    first = pltpu.CompilerParams(vmem_limit_bytes=52 * 1024 * 1024)
    tiny = pl.CostEstimate(flops=1000, bytes_accessed=1000, transcendentals=0)
    half_time = time_count // 2

    def sliced(name, *sources, after=()):
        shapes = [(count, space, sites, vectors, width) for _, count, _, space in sources]
        return pl.pallas_call(
            functools.partial(slice_kernel, sources=sources, skip=len(after)),
            in_specs=[outside] + [anywhere] * len(after),
            out_specs=[vmem] * len(sources),
            out_shape=[jax.ShapeDtypeStruct(shape, nulls.dtype) for shape in shapes],
            scratch_shapes=[pltpu.SemaphoreType.DMA((sum(source[1] for source in sources),))],
            compiler_params=first,
            cost_estimate=tiny,
            name=name,
        )(nulls, *after)

    half_space = space_count // 2
    (space_first,) = sliced("slice_first", (0, half_time, 0, 1))
    space_later, time_first, time_second = sliced(
        "slice_rest", (half_time, half_time, 0, 1), (0, 1, 0, half_space), (0, 1, half_space, half_space), after=(space_first,)
    )
    edge_first = shifted(space_first, "xyz", -1)
    edge_times = [shifted(time_first, "ta", -1), shifted(time_second, "ta", -1)]
    inner_out = [
        jax.ShapeDtypeStruct((4 * aggs, wide), jnp.float32),
        jax.ShapeDtypeStruct((4, vectors * aggs, 8 * width), jnp.bfloat16),
    ]
    inner_scratch = [
        pltpu.VMEM((16, sites, half, width), jnp.bfloat16),
        pltpu.VMEM(nulls.shape, nulls.dtype),
        pltpu.VMEM((4, vectors * aggs, 8 * width), jnp.bfloat16),
        pltpu.VMEM((4, 8 * width, 2 * vectors * aggs), jnp.bfloat16),
        pltpu.SemaphoreType.DMA((20,)),
    ]
    space_second, early_one, adjoint_one = pl.pallas_call(
        before_kernel,
        in_specs=[smem] + [outside] * 3 + [vmem],
        out_specs=[vmem] * 3,
        out_shape=[jax.ShapeDtypeStruct(space_first.shape, nulls.dtype)] + inner_out,
        scratch_shapes=inner_scratch,
        compiler_params=roomy,
        cost_estimate=tiny,
        name="before",
    )(group, nulls, time_links, space_links, space_later)
    edge_second = shifted(space_second, "xyz", -1)
    early, adjoint = pl.pallas_call(
        after_kernel,
        in_specs=[smem] + [outside] * 3 + [vmem] * 2,
        out_specs=[vmem] * 2,
        out_shape=inner_out,
        scratch_shapes=inner_scratch,
        compiler_params=roomy,
        cost_estimate=tiny,
        name="after",
    )(group, nulls, time_links, space_links, early_one, adjoint_one)
    found, picks = pl.pallas_call(
        middle_kernel,
        in_specs=[smem] + [vmem] * 5,
        out_specs=[vmem] * 2,
        out_shape=[
            jax.ShapeDtypeStruct((3 * aggs, wide), jnp.float32),
            jax.ShapeDtypeStruct((2, shards * MOST, 2 * local_count), jnp.float32),
        ],
        compiler_params=modest,
        cost_estimate=tiny,
        name="middle",
    )(place, owner_lists, edge_first, *edge_times, adjoint)
    late = pl.pallas_call(
        final_kernel,
        in_specs=[vmem] * 4,
        out_specs=vmem,
        out_shape=jax.ShapeDtypeStruct((8 * aggs, wide), jnp.bfloat16),
        compiler_params=modest,
        cost_estimate=tiny,
        name="final",
    )(edge_second, adjoint, early, found)
    late_other = crossed(late, "xyz", 1)
    pairs = shards // 2
    packed = pl.pallas_call(
        pack_kernel,
        in_specs=[vmem] * 3,
        out_specs=[vmem] * pairs,
        out_shape=[jax.ShapeDtypeStruct((2 * MOST, 2 * wide), jnp.bfloat16)] * pairs,
        compiler_params=modest,
        cost_estimate=tiny,
        name="pack",
    )(picks, late, late_other)
    turns = list(range(2, pairs)) + [1]
    arrived = [crossed(packed[turn], "xyz", 2 * turn) for turn in turns]
    arrived = pl.pallas_call(
        functools.partial(unpack_kernel, turns=turns + [0]),
        in_specs=[smem] + [vmem] * pairs,
        out_specs=outside,
        out_shape=jax.ShapeDtypeStruct((shards * MOST, 2 * wide), jnp.float32),
        scratch_shapes=[
            pltpu.VMEM((pairs, 2 * MOST, 2 * wide), jnp.float32),
            pltpu.SemaphoreType.DMA((pairs,)),
        ],
        compiler_params=modest,
        cost_estimate=tiny,
        name="unpack",
    )(place, *arrived, packed[0])
    if shards * MOST == cap:
        result = arrived
    else:
        my_list = lax.dynamic_index_in_dim(owner_lists, lax.axis_index("xyz"), 0, keepdims=False)
        source = jnp.maximum(my_list, 0) // local_count
        order = jnp.arange(cap, dtype=jnp.int32)
        same = (source[:, None] == source[None, :]) & (order[None, :] < order[:, None])
        offset = jnp.sum(same.astype(jnp.int32), axis=1)
        picked = arrived[source * MOST + offset]
        result = jnp.where((my_list >= 0)[:, None], picked, 0.0)
    return result[None]


def solution(mesh):
    return jax.shard_map(
        on_device,
        mesh=mesh,
        in_specs=(
            P("ta", "xyz", None, None, None),
            P("ta", "xyz", None, None, None),
            P("ta", "xyz", None, None, None),
            P(),
        ),
        out_specs=P("ta", "xyz", None),
        check_vma=False,
    )
```

```python
import functools

import jax
import jax.numpy as jnp
from jax import lax
from jax.experimental import pallas as pl
from jax.experimental.pallas import tpu as pltpu
from jax.sharding import PartitionSpec as P

ROW_DIMS = (((1,), (1,)), ((), ()))
MAT_DIMS = (((1,), (0,)), ((), ()))
SIDE = 4
MOST = 8


def shifted(array, axis, by):
    count = lax.axis_size(axis)
    return lax.ppermute(array, axis, [(i, (i + by) % count) for i in range(count)])


def crossed(array, axis, bits):
    return lax.ppermute(array, axis, [(i, i ^ bits) for i in range(lax.axis_size(axis))])


def dot(left, right, dims):
    return lax.dot_general(left, right, dims, preferred_element_type=jnp.float32)


def swapped(array):
    return pltpu.roll(array, array.shape[-1] // 2, axis=array.ndim - 1)


def lower_half(shape):
    return lax.broadcasted_iota(jnp.int32, shape, len(shape) - 1) < shape[-1] // 2


def signs(shape, dtype):
    return jnp.where(lower_half(shape), 1.0, -1.0).astype(dtype)


def image_item(links, lower, upper, slot, left_ref, right_ref):
    sites, vectors, width = lower.shape
    half = width // 2
    aggs = sites // SIDE
    lanes = aggs * vectors
    sign = signs((vectors, width), jnp.bfloat16)
    zero = jnp.zeros((vectors, width), jnp.bfloat16)
    owner = lax.broadcasted_iota(jnp.int32, (half, 2 * lanes), 1) // (2 * vectors) % (aggs // 2)
    for part in range(SIDE):
        at = (slot * SIDE + part) * width
        mats = []
        plain, crossed = [], []
        for agg in range(aggs):
            site = agg * SIDE + part
            up = upper[site]
            pair = (up * sign, swapped(up))
            for rows, value in zip((plain, crossed), pair):
                rows.append(jnp.concatenate([value, zero] if agg % 2 == 0 else [zero, value], axis=1))
            if agg % 2 == 0:
                mats.append(jnp.concatenate([links[site], links[site + SIDE]], axis=1))
            left_ref[pl.ds(agg * vectors, vectors), pl.ds(at, width)] = lower[site]
        images = dot(jnp.concatenate(mats, axis=0), jnp.concatenate(plain + crossed, axis=0), ROW_DIMS)
        own = images[:half]
        for pair in range(1, aggs // 2):
            own = jnp.where(owner == pair, images[pair * half : (pair + 1) * half], own)
        own = own.astype(jnp.bfloat16)
        right_ref[pl.ds(at, half), :] = own
        right_ref[pl.ds(at + half, half), :] = jnp.concatenate([own[:, lanes:], -own[:, :lanes]], axis=1)


def adjoint_item(links, lower, slot, left_ref):
    sites, vectors, width = lower.shape
    half = width // 2
    low = lower_half((vectors, width))
    sign = signs((vectors, width), jnp.float32)
    zero = jnp.zeros((vectors, width), jnp.bfloat16)
    for agg in range(sites // SIDE):
        rows = []
        mats = []
        for pair in range(SIDE // 2):
            at = agg * SIDE + 2 * pair
            lo_a, lo_b = lower[at], lower[at + 1]
            rows += [
                jnp.where(low, lo_a, zero),
                jnp.where(low, swapped(lo_a), zero),
                jnp.where(low, zero, swapped(lo_b)),
                jnp.where(low, zero, lo_b),
            ]
            mats.append(jnp.concatenate([links[at], links[at + 1]], axis=0))
        prod = dot(jnp.concatenate(rows, axis=0), jnp.concatenate(mats, axis=1), MAT_DIMS)
        for part in range(SIDE):
            top = part * 2 * vectors
            mine = prod[top : top + 2 * vectors, part // 2 * width : (part // 2 + 1) * width]
            adj = sign * mine[:vectors] + swapped(mine[vectors:])
            left_ref[pl.ds(agg * vectors, vectors), pl.ds((slot * SIDE + part) * width, width)] = adj.astype(jnp.bfloat16)


def group_rows(left, right, dims, vectors):
    full = dot(left, right, dims)
    total = full.shape[1] // 2
    aggs = total // vectors
    lanes = lax.broadcasted_iota(jnp.int32, (vectors, 2 * total), 1) // vectors % aggs
    own = full[:vectors]
    for agg in range(1, aggs):
        own = jnp.where(lanes == agg, full[agg * vectors : (agg + 1) * vectors], own)
    pieces = []
    lane_group = lax.broadcasted_iota(jnp.int32, (aggs, total), 1) // vectors
    sub = lax.broadcasted_iota(jnp.int32, (aggs, total), 0)
    for piece in range(2 * vectors // aggs):
        part, row = divmod(piece * aggs, vectors)
        value = own[row : row + aggs, part * total : (part + 1) * total]
        step = 1
        while step < aggs:
            sub_bit = (sub // step) % 2
            lane_bit = (lane_group // step) % 2
            up = pltpu.roll(pltpu.roll(value, aggs - step, axis=0), step * vectors, axis=1)
            down = pltpu.roll(pltpu.roll(value, step, axis=0), total - step * vectors, axis=1)
            value = jnp.where(sub_bit == lane_bit, value, jnp.where(sub_bit == 0, up, down))
            step *= 2
        pieces.append(value)
    return jnp.concatenate(pieces, axis=1)


def slice_kernel(nulls, *refs, sources, skip):
    edges, sems = refs[skip:-1], refs[-1]
    copies = []
    for edge, (start, count, at, space) in zip(edges, sources):
        for row in range(count):
            source = nulls.at[pl.ds(start + row, 1), pl.ds(at, space)]
            copies.append(pltpu.make_async_copy(source, edge.at[pl.ds(row, 1)], sems.at[len(copies)]))
    for copy in copies:
        copy.start()
    for copy in copies:
        copy.wait()


def choose_rows(place, lists, picks):
    me = place[0]
    shards, cap = lists.shape
    count = picks.shape[2] // 2
    lane = lax.broadcasted_iota(jnp.int32, (MOST, cap), 1)
    want = lax.broadcasted_iota(jnp.int32, (MOST, cap), 0)
    column = lax.broadcasted_iota(jnp.int32, (MOST, 2 * count), 1)
    quarter = count // 4
    inside = column % count
    turned = (inside // quarter % 2) * 2 * quarter + (inside // (2 * quarter)) * quarter + inside % quarter
    own_column = column < count
    side = lax.rem(me, 2)
    for turn in range(shards // 2):
        owner = 2 * jnp.bitwise_xor(me // 2, turn) + side
        mine = jnp.broadcast_to(lists[pl.ds(owner, 1), :], (MOST, cap))
        for parity in range(2):
            source = me - side + parity
            before = jnp.where((mine >= 0) & (mine < source * count), 1, 0)
            start = jnp.sum(before.astype(jnp.float32), axis=1, keepdims=True).astype(jnp.int32)
            match = (mine >= source * count) & (mine < (source + 1) * count) & (lane - start == want)
            chosen = jnp.sum(jnp.where(match, mine - source * count + 1, 0).astype(jnp.float32), axis=1, keepdims=True)
            chosen = chosen.astype(jnp.int32) - 1
            here = own_column == (side == parity)
            rows = pl.ds((2 * turn + parity) * MOST, MOST)
            picks[0, rows, :] = jnp.where(here & (inside == chosen), 1.0, 0.0)
            picks[1, rows, :] = jnp.where(here & (turned == chosen), 1.0, 0.0)


def inner_work(nulls, time_links, space_links, early, adjoint, links, vecs, left, right, sems):
    time_count, space_count, sites, vectors, width = nulls.shape
    copies = []
    bases = [pltpu.make_async_copy(nulls.at[t], vecs.at[t], sems.at[16 + t]) for t in range(4)]
    bases[1].start()
    bases[2].start()

    def fetch(source):
        slot = len(copies)
        copy = pltpu.make_async_copy(source, links.at[slot], sems.at[slot])
        copy.start()
        copies.append(copy)

    for x in range(4):
        fetch(time_links.at[0, x])
    bases[0].start()
    bases[3].start()
    for t in range(4):
        fetch(space_links.at[t, 0])
    for x in range(4):
        fetch(time_links.at[1, x])
    for t in range(4):
        fetch(space_links.at[t, 1])
    bases[1].wait()
    bases[2].wait()
    for a_x in range(2):
        copies[2 * a_x].wait()
        copies[2 * a_x + 1].wait()
        for c in range(2):
            x = 2 * a_x + c
            image_item(links.at[x], vecs.at[1, x], vecs.at[2, x], c, left.at[a_x], right.at[a_x])
    bases[0].wait()
    bases[3].wait()
    for a_t in range(2):
        copies[4 + 2 * a_t].wait()
        copies[5 + 2 * a_t].wait()
        for c in range(2):
            t = 2 * a_t + c
            image_item(links.at[4 + t], vecs.at[t, 1], vecs.at[t, 2], c, left.at[2 + a_t], right.at[2 + a_t])
    found = [group_rows(left[group], right[group], MAT_DIMS, vectors) for group in range(4)]
    early[...] = jnp.concatenate(found, axis=0)
    for x in range(4):
        copies[8 + x].wait()
    for x in range(4):
        adjoint_item(links.at[8 + x], vecs.at[3, x], x % 2, adjoint.at[x // 2])
    for t in range(4):
        copies[12 + t].wait()
    for t in range(4):
        adjoint_item(links.at[12 + t], vecs.at[t, 3], t % 2, adjoint.at[2 + t // 2])


def before_kernel(group, nulls, time_links, space_links, sliced, edge, *refs):
    edge[...] = sliced[...]

    @pl.when(lax.rem(group[0], 2) == 1)
    def _():
        inner_work(nulls, time_links, space_links, *refs)


def after_kernel(group, nulls, time_links, space_links, early_before, adjoint_before, early, adjoint, *refs):
    @pl.when(lax.rem(group[0], 2) == 0)
    def _():
        inner_work(nulls, time_links, space_links, early, adjoint, *refs)

    @pl.when(lax.rem(group[0], 2) == 1)
    def _():
        early[...] = early_before[...]
        adjoint[...] = adjoint_before[...]


def edge_rows(uppers, adjoint, vectors):
    width = uppers[0].shape[-1]
    sign = signs((vectors, width), jnp.bfloat16)
    parts = []
    for upper in uppers:
        sites = upper.shape[0]
        for site in range(SIDE):
            rows = [upper[agg * SIDE + site] for agg in range(sites // SIDE)]
            turned = [sign * swapped(row) for row in rows]
            parts.append(jnp.concatenate(rows + turned, axis=0))
    return group_rows(adjoint, jnp.concatenate(parts, axis=1), ROW_DIMS, vectors)


def middle_kernel(place, lists, space_edge, time_first, time_second, adjoint, found, picks):
    choose_rows(place, lists, picks)
    vectors = space_edge.shape[3]
    rows = []
    for a_x, time_edge in enumerate((time_first, time_second)):
        uppers = [time_edge.at[0, c] for c in range(2)]
        rows.append(edge_rows(uppers, adjoint[a_x], vectors))
    rows.append(edge_rows([space_edge.at[c, 0] for c in range(2)], adjoint[2], vectors))
    found[...] = jnp.concatenate(rows, axis=0)


def final_kernel(space_edge, adjoint, early, found, late):
    vectors = space_edge.shape[3]
    rows = edge_rows([space_edge.at[c, 0] for c in range(2)], adjoint[3], vectors)
    late[...] = jnp.concatenate([early[...], found[...], rows], axis=0).astype(jnp.bfloat16)


def pack_kernel(picks, late, late_other, *packed):
    quarter, width = late.shape[0] // 4, late.shape[1]
    for half in range(2):
        spans = [pl.ds((half + 2 * part) * quarter, quarter) for part in range(2)]
        rows = jnp.concatenate([piece[span, :] for piece in (late, late_other) for span in spans], axis=0)
        sent = dot(picks[half].astype(jnp.bfloat16), rows, MAT_DIMS)
        for turn, out in enumerate(packed):
            mine = sent[turn * 2 * MOST : (turn + 1) * 2 * MOST]
            out[:, pl.ds(half * width, width)] = mine.astype(jnp.bfloat16)


def unpack_kernel(place, *refs, turns):
    pair = place[0] // 2
    result, rows, sems = refs[-3:]
    copies = []
    for slot, turn in enumerate(turns):
        source = jnp.bitwise_xor(pair, turn)
        rows[slot] = refs[slot][...].astype(jnp.float32)
        target = result.at[pl.ds(pl.multiple_of(source * 2 * MOST, 2 * MOST), 2 * MOST)]
        copies.append(pltpu.make_async_copy(rows.at[slot], target, sems.at[slot]))
        copies[-1].start()
    for copy in copies:
        copy.wait()


def on_device(nulls, time_links, space_links, owner_lists):
    time_count, space_count, sites, vectors, width = nulls.shape
    shards, cap = owner_lists.shape
    aggs = sites // SIDE
    local_count = (time_count // 2) * (space_count // 2) * aggs
    wide = 2 * vectors * vectors
    place = lax.axis_index("xyz").astype(jnp.int32).reshape(1)
    group = lax.axis_index("ta").astype(jnp.int32).reshape(1)
    vmem = pl.BlockSpec(memory_space=pltpu.VMEM)
    smem = pl.BlockSpec(memory_space=pltpu.SMEM)
    anywhere = pl.BlockSpec(memory_space=pl.ANY)
    outside = pl.BlockSpec(memory_space=pltpu.HBM)
    half = width // 2
    roomy = pltpu.CompilerParams(vmem_limit_bytes=51 * 1024 * 1024)
    modest = pltpu.CompilerParams(vmem_limit_bytes=24 * 1024 * 1024)
    first = pltpu.CompilerParams(vmem_limit_bytes=52 * 1024 * 1024)
    tiny = pl.CostEstimate(flops=1000, bytes_accessed=1000, transcendentals=0)
    half_time = time_count // 2

    def sliced(name, *sources, after=()):
        shapes = [(count, space, sites, vectors, width) for _, count, _, space in sources]
        return pl.pallas_call(
            functools.partial(slice_kernel, sources=sources, skip=len(after)),
            in_specs=[outside] + [anywhere] * len(after),
            out_specs=[vmem] * len(sources),
            out_shape=[jax.ShapeDtypeStruct(shape, nulls.dtype) for shape in shapes],
            scratch_shapes=[pltpu.SemaphoreType.DMA((sum(source[1] for source in sources),))],
            compiler_params=first,
            cost_estimate=tiny,
            name=name,
        )(nulls, *after)

    half_space = space_count // 2
    (space_first,) = sliced("slice_first", (0, half_time, 0, 1))
    space_later, time_first, time_second = sliced(
        "slice_rest", (half_time, half_time, 0, 1), (0, 1, 0, half_space), (0, 1, half_space, half_space), after=(space_first,)
    )
    edge_first = shifted(space_first, "xyz", -1)
    edge_times = [shifted(time_first, "ta", -1), shifted(time_second, "ta", -1)]
    inner_out = [
        jax.ShapeDtypeStruct((4 * aggs, wide), jnp.float32),
        jax.ShapeDtypeStruct((4, vectors * aggs, 8 * width), jnp.bfloat16),
    ]
    inner_scratch = [
        pltpu.VMEM((16, sites, half, width), jnp.bfloat16),
        pltpu.VMEM(nulls.shape, nulls.dtype),
        pltpu.VMEM((4, vectors * aggs, 8 * width), jnp.bfloat16),
        pltpu.VMEM((4, 8 * width, 2 * vectors * aggs), jnp.bfloat16),
        pltpu.SemaphoreType.DMA((20,)),
    ]
    space_second, early_one, adjoint_one = pl.pallas_call(
        before_kernel,
        in_specs=[smem] + [outside] * 3 + [vmem],
        out_specs=[vmem] * 3,
        out_shape=[jax.ShapeDtypeStruct(space_first.shape, nulls.dtype)] + inner_out,
        scratch_shapes=inner_scratch,
        compiler_params=roomy,
        cost_estimate=tiny,
        name="before",
    )(group, nulls, time_links, space_links, space_later)
    edge_second = shifted(space_second, "xyz", -1)
    early, adjoint = pl.pallas_call(
        after_kernel,
        in_specs=[smem] + [outside] * 3 + [vmem] * 2,
        out_specs=[vmem] * 2,
        out_shape=inner_out,
        scratch_shapes=inner_scratch,
        compiler_params=roomy,
        cost_estimate=tiny,
        name="after",
    )(group, nulls, time_links, space_links, early_one, adjoint_one)
    found, picks = pl.pallas_call(
        middle_kernel,
        in_specs=[smem] + [vmem] * 5,
        out_specs=[vmem] * 2,
        out_shape=[
            jax.ShapeDtypeStruct((3 * aggs, wide), jnp.float32),
            jax.ShapeDtypeStruct((2, shards * MOST, 2 * local_count), jnp.float32),
        ],
        compiler_params=modest,
        cost_estimate=tiny,
        name="middle",
    )(place, owner_lists, edge_first, *edge_times, adjoint)
    late = pl.pallas_call(
        final_kernel,
        in_specs=[vmem] * 4,
        out_specs=vmem,
        out_shape=jax.ShapeDtypeStruct((8 * aggs, wide), jnp.bfloat16),
        compiler_params=modest,
        cost_estimate=tiny,
        name="final",
    )(edge_second, adjoint, early, found)
    late_other = crossed(late, "xyz", 1)
    pairs = shards // 2
    packed = pl.pallas_call(
        pack_kernel,
        in_specs=[vmem] * 3,
        out_specs=[vmem] * pairs,
        out_shape=[jax.ShapeDtypeStruct((2 * MOST, 2 * wide), jnp.bfloat16)] * pairs,
        compiler_params=modest,
        cost_estimate=tiny,
        name="pack",
    )(picks, late, late_other)
    turns = list(range(pairs - 1, 0, -1))
    arrived = [crossed(packed[turn], "xyz", 2 * turn) for turn in turns]
    arrived = pl.pallas_call(
        functools.partial(unpack_kernel, turns=turns + [0]),
        in_specs=[smem] + [vmem] * pairs,
        out_specs=outside,
        out_shape=jax.ShapeDtypeStruct((shards * MOST, 2 * wide), jnp.float32),
        scratch_shapes=[
            pltpu.VMEM((pairs, 2 * MOST, 2 * wide), jnp.float32),
            pltpu.SemaphoreType.DMA((pairs,)),
        ],
        compiler_params=modest,
        cost_estimate=tiny,
        name="unpack",
    )(place, *arrived, packed[0])
    if shards * MOST == cap:
        result = arrived
    else:
        my_list = lax.dynamic_index_in_dim(owner_lists, lax.axis_index("xyz"), 0, keepdims=False)
        source = jnp.maximum(my_list, 0) // local_count
        order = jnp.arange(cap, dtype=jnp.int32)
        same = (source[:, None] == source[None, :]) & (order[None, :] < order[:, None])
        offset = jnp.sum(same.astype(jnp.int32), axis=1)
        picked = arrived[source * MOST + offset]
        result = jnp.where((my_list >= 0)[:, None], picked, 0.0)
    return result[None]


def solution(mesh):
    return jax.shard_map(
        on_device,
        mesh=mesh,
        in_specs=(
            P("ta", "xyz", None, None, None),
            P("ta", "xyz", None, None, None),
            P("ta", "xyz", None, None, None),
            P(),
        ),
        out_specs=P("ta", "xyz", None),
        check_vma=False,
    )
```
